32 devices in a mesh: tm: 8 (over z, x), rows: 4 (over y, core).
Axes of the slice: x: 2, y: 2, z: 4, core: 2. Of those that a mesh axis runs over, the one named last changes fastest.
Arguments:
- gains: float32 [8, 1024, 1024], P('tm', 'rows'), may hold values from -0.1875 to 0.1875
- spreads: float32 [8, 1024, 1024], P('tm', 'rows'), may hold values from -1 to 6, as said below
- offsets: float32 [8, 1024, 4096], P('tm', None, 'rows'), may hold values from -6 to 6
Outputs:
- composed_gain: float32 [8, 1024, 1024], P('tm', 'rows')
- composed_spread: float32 [8, 1024, 1024], P('tm', 'rows')
- composed_offset: float32 [8, 1024, 4096], P('tm', None, 'rows')
The draws below stay inside these ranges and needn't reach their ends.
Inputs may be any that keep to these rules, and one draw needn't show every extreme that they name: `spreads`: each time step's matrix is symmetric.
All inputs are finite; a program needn't handle non-finite values.
Results may differ from the reference program's by a relative error of at most 0.0084.
Values may be sent and summed in bfloat16 or wider, within the bound.
No kernel may reach another device: no remote copies, remote signals or barrier semaphores. Data moves between devices by JAX's collectives and lax.ppermute only.
A program may use at most 64 MiB of HBM per device.

```python
import math
import jax
import jax.numpy as jnp
from jax import lax

D = 1024
LEVELS = 3
STEPS = 8
TRAJ = 4096


def draw_spreads(key, part):
    key = jax.random.fold_in(key, 7)
    first_key, second_key = jax.random.split(key)
    raw = jax.random.normal(first_key, (STEPS, D, D), jnp.float32)
    diagonal = jax.random.uniform(second_key, (STEPS, D), jnp.float32, 0.5, 2.0)
    symmetric = (raw + jnp.swapaxes(raw, 1, 2)) * (0.35 / math.sqrt(D))
    identity = jnp.eye(D, dtype=jnp.float32)
    return symmetric + diagonal[:, :, None] * identity[None, :, :]


def steps_of(rng, extent, cuts, smallest, top_value):
    def one(position, parts):
        heights = jax.random.uniform(jax.random.fold_in(jax.random.fold_in(rng, 6), position), (parts,), jnp.float32, smallest / len(cuts), top_value / len(cuts))
        return jnp.repeat(jnp.exp(heights), extent[position] // parts).reshape((-1,) + (1,) * (len(extent) - position - 1))

    level = one(*cuts[0])
    for cut in cuts[1:]:
        level = level * one(*cut)
    return level


def noise(key, shape, scale, most, pieces=(), held_as=jnp.bfloat16):
    drawn = jax.random.normal(key, shape, jnp.float32) * scale
    if len(pieces) > 0:
        drawn = steps_of(key, shape, pieces, -0.22, 0.18) * drawn
    return jnp.clip(drawn, min=-most, max=most).astype(held_as)


def setup_inputs(seed: int = 0) -> dict:
    streams_of = jax.random.split(jax.random.key(seed), 4)
    return {
        "gains": noise(streams_of[0], (STEPS, D, D), D ** -0.5, 0.1875, ((0, 8), (1, 4)), jnp.float32),
        "spreads": draw_spreads(jax.random.fold_in(streams_of[3], 71), 0),
        "offsets": noise(streams_of[2], (STEPS, D, TRAJ), 1.0, 6.0, ((0, 8), (2, 4)), jnp.float32),
    }


def later_steps(values, distance):
    return jnp.concatenate([values[distance:], jnp.zeros_like(values[:distance])], axis=0)


def reference(gains, spreads, offsets):
    steps_count = gains.shape[0]
    gain = gains
    spread = spreads
    offset = offsets
    highest = lax.Precision.HIGHEST
    size_d = gains.shape[1]
    identity = jnp.eye(size_d, dtype=gains.dtype)
    for section_number in range(LEVELS):
        distance = 2 ** section_number
        beyond = (jnp.arange(steps_count) + distance >= steps_count)
        own_low = gain.astype(jnp.bfloat16).astype(jnp.float32)
        far_gain = later_steps(gain, distance)
        far_gain = jnp.where(beyond[:, None, None], identity[None, :, :], far_gain)
        far_gain = far_gain.astype(jnp.bfloat16).astype(jnp.float32)
        far_spread = later_steps(spread, distance).astype(jnp.bfloat16).astype(jnp.float32)
        far_offset = later_steps(offset, distance).astype(jnp.bfloat16).astype(jnp.float32)
        middle = jnp.einsum("tij,tjk->tik", own_low, far_spread, precision=highest)
        middle = middle.astype(jnp.bfloat16).astype(jnp.float32)
        new_gain = jnp.einsum("tij,tjk->tik", own_low, far_gain, precision=highest)
        new_spread = jnp.einsum("tij,tkj->tik", middle, own_low, precision=highest) + spread
        new_offset = jnp.einsum("tij,tjk->tik", own_low, far_offset, precision=highest) + offset
        gain, spread, offset = new_gain, new_spread, new_offset
    return gain, spread, offset
```

```python
import jax
import jax.numpy as jnp
from jax import lax
from jax.sharding import Mesh, PartitionSpec as P

LEVELS = 3
LOW = jnp.bfloat16
WIDE = jnp.float32


def shifted(value, axis, steps):
    count = lax.axis_size(axis)
    first, last = (max(0, -steps), min(count, count - steps))
    return lax.ppermute(value, axis, [(source, source + steps) for source in range(first, last)])


def doubling(gains, spreads, offsets):
    gain = gains[0]
    spread = spreads[0]
    offset = offsets[0]
    size_d = gain.shape[1]
    identity = jnp.eye(size_d, dtype=LOW)
    for section_number in range(LEVELS):
        distance = 2**section_number
        beyond = lax.axis_index("tm") + distance >= lax.axis_size("tm")
        own_gain = gain.astype(LOW)
        own_spread = spread.astype(LOW)
        own_offset = offset.astype(LOW)
        own_full = lax.all_gather(own_gain, "rows", axis=0, tiled=True)
        spread_full = lax.all_gather(own_spread, "rows", axis=0, tiled=True)
        far_full, far_spread_full, far_offset = shifted((own_full, spread_full, own_offset), "tm", -distance)
        far_full = jnp.where(beyond, identity, far_full)
        row_start = lax.axis_index("rows") * gain.shape[0]
        own_rows = lax.dynamic_slice_in_dim(own_full, row_start, gain.shape[0], 0)
        middle = jnp.dot(own_rows, far_spread_full, preferred_element_type=WIDE).astype(LOW)
        new_gain = jnp.dot(own_rows, far_full, preferred_element_type=WIDE)
        new_spread = (
            lax.dot_general(middle, own_full, (((1,), (1,)), ((), ())), preferred_element_type=WIDE) + spread
        )
        new_offset = jnp.dot(own_full, far_offset, preferred_element_type=WIDE) + offset
        gain, spread, offset = (new_gain, new_spread, new_offset)
    return (gain[None], spread[None], offset[None])


def swap(value, axis):
    return lax.ppermute(value, axis, [(0, 1), (1, 0)])


def mm(a, b):
    return jnp.dot(a, b, preferred_element_type=WIDE)


def mm_bt(a, b):
    return lax.dot_general(a, b, (((1,), (1,)), ((), ())), preferred_element_type=WIDE)


def mm_atbt(a, b):
    return lax.dot_general(a, b, (((0,), (1,)), ((), ())), preferred_element_type=WIDE)


GROUP = ("y", "c", "x")


def exchange(blocks):
    return lax.all_to_all(blocks, GROUP, 0, 0)


def suffix(gains, spreads, offsets):
    pairs = lax.axis_size("z")
    x, y, c, z = (lax.axis_index(name) for name in ("x", "y", "c", "z"))
    even = x == 0
    gain, spread, offset = gains[0], spreads[0], offsets[0]
    rows, size_d = gain.shape
    part = rows // 2
    half = offset.shape[1] // 2
    groups = size_d // rows
    count = 2 * groups
    chunks = 2
    width = half // chunks

    e_low = gain.astype(LOW)
    e_x, e_y = swap(e_low, "x"), swap(e_low, "y")
    e_xy = jnp.concatenate([swap(e_x[:part], "y"), swap(e_y[part:], "x")], axis=0)
    pieces = [e_low, None, e_y, None, e_x, None, e_xy, None]
    for i in range(0, 8, 2):
        pieces[i + 1] = swap(pieces[i], "c")
    me = 4 * x + 2 * y + c
    both = jnp.zeros((8, rows, size_d), LOW)
    for i, piece in enumerate(pieces):
        both = lax.dynamic_update_index_in_dim(both, piece, me ^ i, 0)
    e0, e1 = both[:4].reshape(size_d, size_d), both[4:].reshape(size_d, size_d)

    l_low = spread.astype(LOW)
    l_got = swap(jnp.where(even, l_low[part:], l_low[:part]), "x")
    l_keep = jnp.where(even, spread[:part], spread[part:])
    l1_low = jnp.where(even, l_got, l_keep.astype(LOW))
    l0 = jnp.where(even, l_keep, l_got.astype(WIDE))

    g_keep = jnp.where(even, offset[:, :half], offset[:, half:])
    g_send = jnp.where(even, offset[:, half:], offset[:, :half]).astype(LOW)
    g_got = [swap(g_send[:, i * width : (i + 1) * width], "x") for i in range(chunks)]

    a_e = mm(e0, e1).astype(LOW)
    n = mm_bt(l1_low, e0).astype(LOW)
    n = jnp.broadcast_to(n.reshape(part, groups, 1, rows), (part, groups, 2, rows))
    n = exchange(jnp.transpose(n, (1, 2, 0, 3)).reshape(count, part, rows))
    a_l_rows = mm_atbt(n.reshape(size_d, rows), e0)
    a_l = lax.dynamic_slice_in_dim(a_l_rows, x * part, part, 0) + l0

    slab = (2 * y + c) * 2 + x
    now = lax.dynamic_slice_in_dim(a_e, slab * part, part, 1)
    column = lax.broadcasted_iota(jnp.int32, (size_d, part), 1) + slab * part
    row = lax.broadcasted_iota(jnp.int32, (size_d, part), 0)
    e_far = jnp.where((z == pairs - 1) & (row == column), 1, 0).astype(LOW)
    for hop in range(pairs - 1):
        source = pairs - 1 - hop
        got = lax.ppermute(now, "z", [(source, source - 1)])
        e_far = e_far + got
        if source > 1:
            now = mm(a_e, got).astype(LOW)
    out = jnp.stack([mm(a_e, e_far).astype(LOW), mm(e1, e_far).astype(LOW)])
    out = jnp.transpose(out.reshape(2, groups, rows, part), (1, 0, 2, 3)).reshape(count, rows, part)
    out_gain = jnp.transpose(exchange(out), (1, 0, 2)).reshape(rows, size_d).astype(WIDE)

    now = a_l.astype(LOW)
    l_far = jnp.zeros((part, size_d), LOW)
    for hop in range(pairs - 1):
        source = pairs - 1 - hop
        got = lax.ppermute(now, "z", [(source, source - 1)])
        l_far = l_far + got
        if source > 1:
            n = mm_bt(got, a_e).astype(LOW)
            n = exchange(jnp.transpose(n.reshape(part, count, part), (1, 0, 2)))
            now = (mm_atbt(n.reshape(size_d, part), a_e) + a_l).astype(LOW)
    own_e = jnp.where(even, a_e, e1)
    n = jnp.stack([mm_bt(l_far, a_e).astype(LOW), mm_bt(l_far, e1).astype(LOW)])
    n = jnp.transpose(n.reshape(2, part, groups, rows), (2, 0, 1, 3)).reshape(count, part, rows)
    n = exchange(n).reshape(size_d, rows)
    out_spread = mm_atbt(n, own_e) + jnp.where(even, a_l_rows, 0) + spread

    lefts, rights = [], []
    for i in range(chunks):
        cut = slice(i * width, (i + 1) * width)
        keep = g_keep[:, cut]
        g1_low = jnp.where(even, g_got[i], keep.astype(LOW))
        g0 = jnp.where(even, keep, g_got[i].astype(WIDE))
        p = mm(e0, g1_low)
        a_g = p + g0
        now = a_g.astype(LOW)
        g_far = jnp.zeros((size_d, width), LOW)
        for hop in range(pairs - 1):
            source = pairs - 1 - hop
            got = lax.ppermute(now, "z", [(source, source - 1)])
            g_far = g_far + got
            if source > 1:
                now = (mm(a_e, got) + a_g).astype(LOW)
        o0 = mm(a_e, g_far) + p
        o1 = mm(e1, g_far)
        mine = jnp.where(even, o0, o1) + keep
        other = swap(jnp.where(even, o1, o0).astype(LOW), "x")
        lefts.append(jnp.where(even, mine, other + offset[:, cut]))
        rights.append(jnp.where(even, other + offset[:, half + i * width : half + (i + 1) * width], mine))
    out_offset = jnp.concatenate(lefts + rights, axis=1)
    return (out_gain[None], out_spread[None], out_offset[None])


def solution(mesh):
    steps, rows = mesh.shape["tm"], mesh.shape["rows"]
    if steps <= 2**LEVELS and steps % 2 == 0 and rows == 4:
        devices = mesh.devices.reshape(steps // 2, 2, 2, 2)
        mesh = Mesh(devices, ("z", "x", "y", "c"))
        by_row, by_column = P(("z", "x"), ("y", "c"), None), P(("z", "x"), None, ("y", "c"))
        body = suffix
    else:
        by_row, by_column = P("tm", "rows", None), P("tm", None, "rows")
        body = doubling
    return jax.shard_map(
        body,
        mesh=mesh,
        in_specs=(by_row, by_row, by_column),
        out_specs=(by_row, by_row, by_column),
        check_vma=False,
    )
```

```python
import jax
import jax.numpy as jnp
from jax import lax
from jax.experimental import pallas as pl
from jax.experimental.pallas import tpu as pltpu
from jax.sharding import Mesh, PartitionSpec as P

LEVELS = 3
LOW = jnp.bfloat16
WIDE = jnp.float32
SCOPED = 40 * 2**20


def shifted(value, axis, steps):
    count = lax.axis_size(axis)
    first, last = (max(0, -steps), min(count, count - steps))
    return lax.ppermute(value, axis, [(source, source + steps) for source in range(first, last)])


def doubling(gains, spreads, offsets):
    gain = gains[0]
    spread = spreads[0]
    offset = offsets[0]
    size_d = gain.shape[1]
    identity = jnp.eye(size_d, dtype=LOW)
    for section_number in range(LEVELS):
        distance = 2**section_number
        beyond = lax.axis_index("tm") + distance >= lax.axis_size("tm")
        own_gain = gain.astype(LOW)
        own_spread = spread.astype(LOW)
        own_offset = offset.astype(LOW)
        own_full = lax.all_gather(own_gain, "rows", axis=0, tiled=True)
        spread_full = lax.all_gather(own_spread, "rows", axis=0, tiled=True)
        far_full, far_spread_full, far_offset = shifted((own_full, spread_full, own_offset), "tm", -distance)
        far_full = jnp.where(beyond, identity, far_full)
        row_start = lax.axis_index("rows") * gain.shape[0]
        own_rows = lax.dynamic_slice_in_dim(own_full, row_start, gain.shape[0], 0)
        middle = jnp.dot(own_rows, far_spread_full, preferred_element_type=WIDE).astype(LOW)
        new_gain = jnp.dot(own_rows, far_full, preferred_element_type=WIDE)
        new_spread = (
            lax.dot_general(middle, own_full, (((1,), (1,)), ((), ())), preferred_element_type=WIDE) + spread
        )
        new_offset = jnp.dot(own_full, far_offset, preferred_element_type=WIDE) + offset
        gain, spread, offset = (new_gain, new_spread, new_offset)
    return (gain[None], spread[None], offset[None])


def swap(value, axis):
    return lax.ppermute(value, axis, [(0, 1), (1, 0)])


def mm(a, b):
    return jnp.dot(a, b, preferred_element_type=WIDE)


def mm_bt(a, b):
    return lax.dot_general(a, b, (((1,), (1,)), ((), ())), preferred_element_type=WIDE)


def mm_atbt(a, b):
    return lax.dot_general(a, b, (((0,), (1,)), ((), ())), preferred_element_type=WIDE)


GROUP = ("y", "c", "x")


def exchange(blocks):
    return lax.all_to_all(blocks, GROUP, 0, 0)


def call(kernel, grid, ids, ins, outs, out_shapes, operands, scratch=(), aliases={}, flops=0, bytes_accessed=0):
    return pl.pallas_call(
        kernel,
        grid_spec=pltpu.PrefetchScalarGridSpec(
            num_scalar_prefetch=1, grid=grid, in_specs=ins, out_specs=outs, scratch_shapes=list(scratch)
        ),
        out_shape=out_shapes,
        input_output_aliases=aliases,
        cost_estimate=pl.CostEstimate(flops=flops, bytes_accessed=bytes_accessed, transcendentals=0),
        compiler_params=pltpu.CompilerParams(vmem_limit_bytes=SCOPED),
    )(ids, *operands)


def whole(shape):
    return pl.BlockSpec(shape, lambda *_: (0,) * len(shape))


def pair_kernel(ids, *refs):
    pieces, (l_ref, both, pair, n_ref) = refs[:8], refs[8:]
    me = 4 * ids[0] + 2 * ids[1] + ids[2]
    rows = pieces[0].shape[0]
    for i in range(8):
        place = me ^ i
        both[place >> 2, pl.ds(pl.multiple_of((place & 3) * rows, rows), rows), :] = pieces[i][...]
    for r in range(4):
        cut = slice(r * rows, (r + 1) * rows)
        n = mm_bt(l_ref[...], both[0, cut, :]).astype(LOW)
        n_ref[2 * r] = n
        n_ref[2 * r + 1] = n
        pair[cut, :] = mm(both[0, cut, :], both[1]).astype(LOW)


def compose_kernel(ids, pair, later, half_ref, other_ref, first, second, far):
    step = pl.program_id(0)
    size = half_ref.shape[0]
    c, z = ids[2], ids[3]

    @pl.when((step == 0) & (z % 2 == 0))
    def _():
        far[pl.ds(pl.multiple_of(c * size, size), size), :] = half_ref[...]
        far[pl.ds(pl.multiple_of((1 - c) * size, size), size), :] = other_ref[...]

    @pl.when(z % 2 == 0)
    def _():
        first[...] = mm(pair[...], far[...]).astype(LOW)
        second[...] = mm(later[0], far[...]).astype(LOW)

    @pl.when(z % 2 == 1)
    def _():
        first[...] = pair[...]
        second[...] = later[0]


def gain_kernel(ids, first, second, got_a, got_b, out, far):
    x, y, c, z = ids[0], ids[1], ids[2], ids[3]
    step = pl.program_id(0)
    size, part = far.shape

    @pl.when((step == 0) & (z < 2))
    def _():
        far[...] = got_a[...] + got_b[...]

    @pl.when((step == 0) & (z >= 2))
    def _():
        slab = (2 * y + c) * 2 + x
        column = lax.broadcasted_iota(jnp.int32, (size, part), 1) + slab * part
        row = lax.broadcasted_iota(jnp.int32, (size, part), 0)
        far[...] = jnp.where(row == column, 1.0, 0.0).astype(LOW)

    out[0] = mm(first[...], far[...]).astype(LOW)
    out[1] = mm(second[...], far[...]).astype(LOW)


def widen_kernel(ids, blocks, out):
    part = blocks.shape[2]
    for s in range(blocks.shape[0]):
        out[:, s * part : (s + 1) * part] = blocks[s].astype(WIDE)


def start_kernel(ids, e0, got, keep, p_ref, now, g1):
    step = pl.program_id(0)
    even = ids[0] == 0
    rows = e0.shape[1]
    cut = pl.ds(pl.multiple_of(step * rows, rows), rows)

    @pl.when((step == 0) & even)
    def _():
        g1[...] = got[...]

    @pl.when((step == 0) & jnp.logical_not(even))
    def _():
        g1[...] = keep[...].astype(LOW)

    p = mm(e0[0], g1[...])
    p_ref[...] = p

    @pl.when(even)
    def _():
        now[...] = (p + keep[cut, :]).astype(LOW)

    @pl.when(jnp.logical_not(even))
    def _():
        now[...] = (p + got[cut, :].astype(WIDE)).astype(LOW)


def hop_kernel(ids, pair, got, own, now):
    now[...] = (mm(pair[...], got[...]) + own[...].astype(WIDE)).astype(LOW)


def last_kernel(ids, pair, later, got_a, got_b, got_c, p_ref, keep, *refs):
    out, send, far = refs[-3:]
    even = ids[0] == 0

    @pl.when(pl.program_id(0) == 0)
    def _():
        far[...] = got_a[...] + got_b[...] + got_c[...]

    @pl.when(even)
    def _():
        out[...] = mm(pair[...], far[...]) + p_ref[...] + keep[...]
        send[...] = mm(later[0], far[...]).astype(LOW)

    @pl.when(jnp.logical_not(even))
    def _():
        out[...] = mm(later[0], far[...]) + keep[...]
        send[...] = (mm(pair[...], far[...]) + p_ref[...]).astype(LOW)


def add_kernel(ids, got, keep, into, out):
    out[...] = got[...].astype(WIDE) + keep[...]


def suffix(gains, spreads, offsets):
    x, y, c, z = (lax.axis_index(name) for name in ("x", "y", "c", "z"))
    even = x == 0
    gain, spread, offset = gains[0], spreads[0], offsets[0]
    rows, size_d = gain.shape
    part = rows // 2
    half = offset.shape[1] // 2
    chunks = 2
    width = half // chunks
    ids = jnp.stack([x, y, c, z]).astype(jnp.int32)
    slab = (2 * y + c) * 2 + x
    square = jax.ShapeDtypeStruct((size_d, size_d), LOW)

    e_low = gain.astype(LOW)
    e_x, e_y = swap(e_low, "x"), swap(e_low, "y")
    e_xy = jnp.concatenate([swap(e_x[:part], "y"), swap(e_y[part:], "x")], axis=0)
    pieces = [e_low, None, e_y, None, e_x, None, e_xy, None]
    for i in range(0, 8, 2):
        pieces[i + 1] = swap(pieces[i], "c")

    l_low = spread.astype(LOW)
    l_send = jnp.where(even, l_low[part:], l_low[:part])
    g_send = jnp.where(even, offset[:, half:], offset[:, :half]).astype(LOW)
    l_send, e_x = lax.optimization_barrier((l_send, e_x))
    g_send, e_xy = lax.optimization_barrier((g_send, e_xy))
    l_got = swap(l_send, "x")
    l_keep = jnp.where(even, spread[:part], spread[part:])
    l1_low = jnp.where(even, l_got, l_keep.astype(LOW))
    l0 = jnp.where(even, l_keep, l_got.astype(WIDE))
    g_got = [swap(g_send[:, i * width : (i + 1) * width], "x") for i in range(chunks)]

    both, a_e, n = call(
        pair_kernel, (1,), ids,
        [whole((rows, size_d))] * 8 + [whole((part, size_d))],
        [whole((2, size_d, size_d)), whole((size_d, size_d)), whole((8, part, rows))],
        [jax.ShapeDtypeStruct((2, size_d, size_d), LOW), square, jax.ShapeDtypeStruct((8, part, rows), LOW)],
        pieces + [l1_low],
        flops=2 * size_d**3, bytes_accessed=20 * size_d**2,
    )
    e0, e1 = both[0], both[1]
    n = exchange(n)
    a_l_rows = mm_atbt(n.reshape(size_d, rows), e0)
    a_l = lax.dynamic_slice_in_dim(a_l_rows, x * part, part, 0) + l0

    level = [(3, 2), (1, 0)]
    hold = size_d // 2
    e_half = lax.ppermute(lax.dynamic_slice_in_dim(a_e, c * hold, hold, 0), "z", level)
    tile = pl.BlockSpec((rows, size_d), lambda i, ids: (i, 0))
    tile0 = pl.BlockSpec((1, rows, size_d), lambda i, ids: (0, i, 0))
    tile1 = pl.BlockSpec((1, rows, size_d), lambda i, ids: (1, i, 0))
    c0_e, c1_e = call(
        compose_kernel, (4,), ids,
        [tile, tile1, whole((hold, size_d)), whole((hold, size_d))],
        [tile, tile], [square, square],
        [a_e, both, e_half, swap(e_half, "c")],
        scratch=[pltpu.VMEM((size_d, size_d), LOW)],
        flops=4 * size_d**3, bytes_accessed=12 * size_d**2,
    )
    e_slab = lax.dynamic_slice_in_dim(c0_e, slab * part, part, 1)
    got_a, got_b = lax.ppermute(e_slab, "z", [(2, 1)]), lax.ppermute(e_slab, "z", [(2, 0)])
    out = call(
        gain_kernel, (4,), ids,
        [tile, tile, whole((size_d, part)), whole((size_d, part))],
        pl.BlockSpec((2, rows, part), lambda i, ids: (i, 0, 0)),
        jax.ShapeDtypeStruct((8, rows, part), LOW),
        [c0_e, c1_e, got_a, got_b],
        scratch=[pltpu.VMEM((size_d, part), LOW)],
        flops=4 * size_d**2 * part, bytes_accessed=5 * size_d**2,
    )
    out_gain = call(
        widen_kernel, (1,), ids, [whole((8, rows, part))], whole((rows, size_d)),
        jax.ShapeDtypeStruct((rows, size_d), WIDE), [exchange(out)], bytes_accessed=6 * rows * size_d,
    )

    def for_rows(slab_rows, first, second):
        n = jnp.stack([mm_bt(slab_rows, first).astype(LOW), mm_bt(slab_rows, second).astype(LOW)])
        n = jnp.transpose(n.reshape(2, part, 4, rows), (2, 0, 1, 3)).reshape(8, part, rows)
        return exchange(n).reshape(size_d, rows)

    got = lax.ppermute(a_l.astype(LOW), "z", level)
    n = mm_bt(got, a_e).astype(LOW)
    n = exchange(jnp.transpose(n.reshape(part, 8, part), (1, 0, 2)))
    b_l = (mm_atbt(n.reshape(size_d, part), a_e) + a_l).astype(LOW)
    far = lax.ppermute(b_l, "z", [(2, 1)]) + lax.ppermute(b_l, "z", [(2, 0)])
    near = for_rows(got, a_e, e1)
    out_spread = mm_atbt(near, jnp.where(even, a_e, e1)) + jnp.where(even, a_l_rows, 0) + spread
    out_spread = mm_atbt(for_rows(far, c0_e, c1_e), jnp.where(even, c0_e, c1_e)) + out_spread

    column = jax.ShapeDtypeStruct((size_d, width), LOW)
    wide_column = jax.ShapeDtypeStruct((size_d, width), WIDE)
    block = pl.BlockSpec((rows, width), lambda i, ids: (i, 0))
    all_rows = whole((size_d, width))
    out_offset = None
    full = jax.ShapeDtypeStruct(offset.shape, WIDE)
    others = []
    for i in range(chunks):
        kept = pl.BlockSpec((rows, width), lambda s, ids, i=i: (s, ids[0] * chunks + i))
        kept_all = pl.BlockSpec((size_d, width), lambda s, ids, i=i: (0, ids[0] * chunks + i))
        p, own = call(
            start_kernel, (4,), ids, [tile0, all_rows, kept_all], [block, block], [wide_column, column],
            [both, g_got[i], offset], scratch=[pltpu.VMEM((size_d, width), LOW)],
            flops=2 * size_d**2 * width, bytes_accessed=2 * size_d**2 + 12 * size_d * width,
        )
        now, gots = own, []
        for source in (3, 2, 1):
            gots.append(lax.ppermute(now, "z", [(source, source - 1)]))
            if source > 1:
                now = call(
                    hop_kernel, (4,), ids, [tile, all_rows, block], block, column, [a_e, gots[-1], own],
                    flops=2 * size_d**2 * width, bytes_accessed=2 * size_d**2 + 6 * size_d * width,
                )
        extra = [] if out_offset is None else [out_offset]
        out_offset, other = call(
            last_kernel, (4,), ids,
            [tile, tile1, all_rows, all_rows, all_rows, block, kept] + [pl.BlockSpec(memory_space=pl.ANY)] * len(extra),
            [kept, block], [full, column],
            [a_e, both] + gots + [p, offset] + extra,
            scratch=[pltpu.VMEM((size_d, width), LOW)], aliases={8: 0} if extra else {},
            flops=4 * size_d**2 * width, bytes_accessed=4 * size_d**2 + 20 * size_d * width,
        )
        others.append(swap(other, "x"))
    for i in range(chunks):
        kept = pl.BlockSpec((rows, width), lambda s, ids, i=i: (s, (1 - ids[0]) * chunks + i))
        out_offset = call(
            add_kernel, (4,), ids, [block, kept, pl.BlockSpec(memory_space=pl.ANY)], kept, full,
            [others[i], offset, out_offset], aliases={3: 0}, bytes_accessed=10 * size_d * width,
        )
    return (out_gain[None], out_spread[None], out_offset[None])


def solution(mesh):
    steps, rows = mesh.shape["tm"], mesh.shape["rows"]
    if steps == 2**LEVELS and rows == 4:
        devices = mesh.devices.reshape(steps // 2, 2, 2, 2)
        mesh = Mesh(devices, ("z", "x", "y", "c"))
        by_row, by_column = P(("z", "x"), ("y", "c"), None), P(("z", "x"), None, ("y", "c"))
        body = suffix
    else:
        by_row, by_column = P("tm", "rows", None), P("tm", None, "rows")
        body = doubling
    return jax.shard_map(
        body,
        mesh=mesh,
        in_specs=(by_row, by_row, by_column),
        out_specs=(by_row, by_row, by_column),
        check_vma=False,
    )
```

```python
import jax
import jax.numpy as jnp
from jax import lax
from jax.experimental import pallas as pl
from jax.experimental.pallas import tpu as pltpu
from jax.sharding import Mesh, PartitionSpec as P

LEVELS = 3
LOW = jnp.bfloat16
WIDE = jnp.float32
MIB = 2**20


def shifted(value, axis, steps):
    count = lax.axis_size(axis)
    first, last = (max(0, -steps), min(count, count - steps))
    return lax.ppermute(value, axis, [(source, source + steps) for source in range(first, last)])


def doubling(gains, spreads, offsets):
    gain = gains[0]
    spread = spreads[0]
    offset = offsets[0]
    size_d = gain.shape[1]
    identity = jnp.eye(size_d, dtype=LOW)
    for section_number in range(LEVELS):
        distance = 2**section_number
        beyond = lax.axis_index("tm") + distance >= lax.axis_size("tm")
        own_gain = gain.astype(LOW)
        own_spread = spread.astype(LOW)
        own_offset = offset.astype(LOW)
        own_full = lax.all_gather(own_gain, "rows", axis=0, tiled=True)
        spread_full = lax.all_gather(own_spread, "rows", axis=0, tiled=True)
        far_full, far_spread_full, far_offset = shifted((own_full, spread_full, own_offset), "tm", -distance)
        far_full = jnp.where(beyond, identity, far_full)
        row_start = lax.axis_index("rows") * gain.shape[0]
        own_rows = lax.dynamic_slice_in_dim(own_full, row_start, gain.shape[0], 0)
        middle = jnp.dot(own_rows, far_spread_full, preferred_element_type=WIDE).astype(LOW)
        new_gain = jnp.dot(own_rows, far_full, preferred_element_type=WIDE)
        new_spread = (
            lax.dot_general(middle, own_full, (((1,), (1,)), ((), ())), preferred_element_type=WIDE) + spread
        )
        new_offset = jnp.dot(own_full, far_offset, preferred_element_type=WIDE) + offset
        gain, spread, offset = (new_gain, new_spread, new_offset)
    return (gain[None], spread[None], offset[None])


def swap(value, axis):
    return lax.ppermute(value, axis, [(0, 1), (1, 0)])


def mm(a, b):
    return jnp.dot(a, b, preferred_element_type=WIDE)


def mm_bt(a, b):
    return lax.dot_general(a, b, (((1,), (1,)), ((), ())), preferred_element_type=WIDE)


GROUP = ("y", "c", "x")


def exchange(blocks):
    return lax.all_to_all(blocks, GROUP, 0, 0)


def whole(shape):
    return pl.BlockSpec(shape, lambda *_: (0,) * len(shape))


def call(kernel, ids, ins, outs, operands, mib, flops=0, scratch=(), aliases={}):
    ins = [whole(operand.shape) if spec is None else spec for spec, operand in zip(ins, operands)]
    specs, shapes = [], []
    for out in outs:
        spec, shape = out if isinstance(out, tuple) else (None, out)
        specs.append(whole(shape.shape) if spec is None else spec)
        shapes.append(shape)
    moved = sum(a.size * a.dtype.itemsize for a in list(operands) + shapes)
    return pl.pallas_call(
        kernel,
        grid_spec=pltpu.PrefetchScalarGridSpec(
            num_scalar_prefetch=1, grid=(1,), in_specs=ins, out_specs=specs, scratch_shapes=list(scratch)
        ),
        out_shape=shapes,
        input_output_aliases=aliases,
        cost_estimate=pl.CostEstimate(flops=flops, bytes_accessed=moved, transcendentals=0),
        compiler_params=pltpu.CompilerParams(vmem_limit_bytes=mib * MIB),
    )(ids, *operands)


def low(*shape):
    return jax.ShapeDtypeStruct(shape, LOW)


def wide(*shape):
    return jax.ShapeDtypeStruct(shape, WIDE)


def gather_lanes(blocks, into, start, width):
    for s in range(blocks.shape[0]):
        into[:, s * width : (s + 1) * width] = blocks[s, :, start : start + width]


def pair_kernel(ids, *refs):
    pieces, (l_low, l_got, both, pair, m_ref) = refs[:8], refs[8:]
    x = ids[0]
    me = 4 * x + 2 * ids[1] + ids[2]
    rows = pieces[0].shape[0]
    part = rows // 2
    for i in range(8):
        place = me ^ i
        both[place >> 2, pl.ds(pl.multiple_of((place & 3) * rows, rows), rows), :] = pieces[i][...]

    def product(slab):
        for r in range(4):
            cut = slice(r * rows, (r + 1) * rows)
            m = mm_bt(both[0, cut, :], slab).astype(LOW)
            m_ref[2 * r] = m
            m_ref[2 * r + 1] = m

    @pl.when(x == 0)
    def _():
        product(l_got[...])

    @pl.when(x == 1)
    def _():
        product(l_low[part:, :])

    for r in range(4):
        cut = slice(r * rows, (r + 1) * rows)
        pair[cut, :] = mm(both[0, cut, :], both[1]).astype(LOW)


def spread_start_kernel(ids, blocks, e0, spread, l_got, prod, a_l, a_low, m):
    part = l_got.shape[0]
    gather_lanes(blocks, m, 0, part)
    prod[...] = mm_bt(m[...], e0[0])

    @pl.when(ids[0] == 0)
    def _():
        a_l[...] = (prod[:part, :] + spread[0, :part, :]).T

    @pl.when(ids[0] == 1)
    def _():
        a_l[...] = (prod[part:, :] + l_got[...].astype(WIDE)).T

    a_low[...] = a_l[...].astype(LOW)


def spread_hop_kernel(ids, pair, later, got, m_ref, near):
    part = got.shape[1]
    rows = 2 * part
    m = mm(pair[...], got[...]).astype(LOW)
    m_ref[...] = m
    other = mm(later[0], got[...]).astype(LOW)
    for r in range(4):
        near[2 * r] = m[r * rows : (r + 1) * rows, :]
        near[2 * r + 1] = other[r * rows : (r + 1) * rows, :]


def spread_next_kernel(ids, blocks, pair, a_l, b_l, m):
    gather_lanes(blocks, m, 0, m.shape[0])
    b_l[...] = (mm_bt(pair[...], m[...]) + a_l[...]).astype(LOW)


def near_kernel(ids, blocks, pair, later, prod, spread, out, m):
    gather_lanes(blocks, m, 0, blocks.shape[2])

    @pl.when(ids[0] == 0)
    def _():
        out[...] = mm_bt(m[...], pair[...]) + prod[...] + spread[0]

    @pl.when(ids[0] == 1)
    def _():
        out[...] = mm_bt(m[...], later[0]) + spread[0]


def compose_kernel(ids, pair, later, next_pair, first, second, slab_ref):
    part = slab_ref.shape[1]
    slab = (2 * ids[1] + ids[2]) * 2 + ids[0]

    @pl.when(ids[3] % 2 == 0)
    def _():
        first[...] = mm(pair[...], next_pair[...]).astype(LOW)
        second[...] = mm(later[0], next_pair[...]).astype(LOW)

    @pl.when(ids[3] % 2 == 1)
    def _():
        first[...] = pair[...]
        second[...] = later[0]

    slab_ref[...] = first[:, pl.ds(pl.multiple_of(slab * part, part), part)]


def far_kernel(ids, first, second, e_a, e_b, l_a, l_b, out, far):
    size, part = e_a.shape
    rows = 2 * part

    @pl.when(ids[3] < 2)
    def _():
        far[:, :part] = e_a[...] + e_b[...]

    @pl.when(ids[3] >= 2)
    def _():
        slab = (2 * ids[1] + ids[2]) * 2 + ids[0]
        column = lax.broadcasted_iota(jnp.int32, (size, part), 1) + slab * part
        row = lax.broadcasted_iota(jnp.int32, (size, part), 0)
        far[:, :part] = jnp.where(row == column, 1.0, 0.0).astype(LOW)

    far[:, part:] = l_a[...] + l_b[...]
    one = mm(first[...], far[...]).astype(LOW)
    two = mm(second[...], far[...]).astype(LOW)
    for r in range(4):
        out[2 * r] = one[r * rows : (r + 1) * rows, :]
        out[2 * r + 1] = two[r * rows : (r + 1) * rows, :]


def end_kernel(ids, blocks, first, second, near, out_gain, out_spread, m):
    part = blocks.shape[2] // 2
    gather_lanes(blocks, m, part, part)
    for s in range(blocks.shape[0]):
        out_gain[:, s * part : (s + 1) * part] = blocks[s, :, :part].astype(WIDE)

    @pl.when(ids[0] == 0)
    def _():
        out_spread[...] = mm_bt(m[...], first[...]) + near[...]

    @pl.when(ids[0] == 1)
    def _():
        out_spread[...] = mm_bt(m[...], second[...]) + near[...]


def start_kernel(ids, e0, got, keep, p_ref, now):
    @pl.when(ids[0] == 0)
    def _():
        p = mm(e0[0], got[...])
        p_ref[...] = p
        now[...] = (p + keep[...]).astype(LOW)

    @pl.when(ids[0] == 1)
    def _():
        p = mm(e0[0], keep[...].astype(LOW))
        p_ref[...] = p
        now[...] = (p + got[...].astype(WIDE)).astype(LOW)


def hop_kernel(ids, pair, got, own, now):
    now[...] = (mm(pair[...], got[...]) + own[...].astype(WIDE)).astype(LOW)


def last_kernel(ids, pair, later, got_a, got_b, got_c, p_ref, keep, *refs):
    out, send = refs[-2:]
    far = got_a[...] + got_b[...] + got_c[...]

    @pl.when(ids[0] == 0)
    def _():
        send[...] = mm(later[0], far).astype(LOW)
        out[...] = mm(pair[...], far) + p_ref[...] + keep[...]

    @pl.when(ids[0] == 1)
    def _():
        send[...] = (mm(pair[...], far) + p_ref[...]).astype(LOW)
        out[...] = mm(later[0], far) + keep[...]


def add_kernel(ids, got, keep, into, out):
    out[...] = got[...].astype(WIDE) + keep[...]


def suffix(gains, spreads, offsets):
    x, y, c, z = (lax.axis_index(name) for name in ("x", "y", "c", "z"))
    even = x == 0
    gain, offset = gains[0], offsets[0]
    rows, size_d = gain.shape
    part = rows // 2
    half = offset.shape[1] // 2
    chunks = 2
    width = half // chunks
    ids = jnp.stack([x, y, c, z]).astype(jnp.int32)
    level = [(3, 2), (1, 0)]

    e_low = gain.astype(LOW)
    e_x, e_y = swap(e_low, "x"), swap(e_low, "y")
    e_xy = jnp.concatenate([swap(e_x[:part], "y"), swap(e_y[part:], "x")], axis=0)
    pieces = [e_low, None, e_y, None, e_x, None, e_xy, None]
    for i in range(0, 8, 2):
        pieces[i + 1] = swap(pieces[i], "c")

    l_low = spreads[0].astype(LOW)
    l_send = jnp.where(even, l_low[part:], l_low[:part])
    g_send = jnp.where(even, offset[:, half:], offset[:, :half]).astype(LOW)
    l_send, e_x = lax.optimization_barrier((l_send, e_x))
    g_send, e_xy = lax.optimization_barrier((g_send, e_xy))
    l_got = swap(l_send, "x")
    g_got = [swap(g_send[:, i * width : (i + 1) * width], "x") for i in range(chunks)]

    both, a_e, m = call(
        pair_kernel, ids, [None] * 10,
        [low(2, size_d, size_d), low(size_d, size_d), low(8, rows, part)],
        pieces + [l_low, l_got], 24, flops=2 * size_d**3,
    )
    first = pl.BlockSpec((1, size_d, size_d), lambda i, ids: (0, 0, 0))
    later = pl.BlockSpec((1, size_d, size_d), lambda i, ids: (1, 0, 0))
    prod, a_l, a_low = call(
        spread_start_kernel, ids, [None, first, None, None],
        [wide(rows, size_d), wide(size_d, part), low(size_d, part)],
        [exchange(m), both, spreads, l_got], 14, flops=2 * rows * size_d**2,
        scratch=[pltpu.VMEM((rows, size_d), LOW)],
    )

    l_next = lax.ppermute(a_low, "z", level)
    quarter = lax.dynamic_slice_in_dim(a_e, (2 * y + c) * rows, rows, 0)
    e_next = lax.all_gather(lax.ppermute(quarter, "z", level), ("y", "c"), axis=0, tiled=True)
    m, near = call(
        spread_hop_kernel, ids, [None, later, None], [low(size_d, part), low(8, rows, part)],
        [a_e, both, l_next], 10, flops=4 * part * size_d**2,
    )
    (b_l,) = call(
        spread_next_kernel, ids, [None, None, None], [low(size_d, part)],
        [exchange(m.reshape(8, part, part)), a_e, a_l], 8, flops=2 * part * size_d**2,
        scratch=[pltpu.VMEM((part, size_d), LOW)],
    )
    l_far = lax.ppermute(b_l, "z", [(2, 1)]), lax.ppermute(b_l, "z", [(2, 0)])
    c0_e, c1_e, e_slab = call(
        compose_kernel, ids, [None, later, None],
        [low(size_d, size_d), low(size_d, size_d), low(size_d, part)],
        [a_e, both, e_next], 20, flops=4 * size_d**3,
    )
    e_far = lax.ppermute(e_slab, "z", [(2, 1)]), lax.ppermute(e_slab, "z", [(2, 0)])
    (near,) = call(
        near_kernel, ids, [None, None, later, None, None], [wide(rows, size_d)],
        [exchange(near), a_e, both, prod, spreads], 14, flops=2 * rows * size_d**2,
        scratch=[pltpu.VMEM((rows, size_d), LOW)],
    )

    (m,) = call(
        far_kernel, ids, [None] * 6, [low(8, rows, rows)], [c0_e, c1_e, *e_far, *l_far], 12,
        flops=4 * rows * size_d**2, scratch=[pltpu.VMEM((size_d, rows), LOW)],
    )
    out_gain, out_spread = call(
        end_kernel, ids, [None] * 4, [wide(rows, size_d), wide(rows, size_d)],
        [exchange(m), c0_e, c1_e, near], 14, flops=2 * rows * size_d**2,
        scratch=[pltpu.VMEM((rows, size_d), LOW)],
    )

    out_offset, others = None, []
    for i in range(chunks):
        kept = pl.BlockSpec((size_d, width), lambda s, ids, i=i: (0, ids[0] * chunks + i))
        p, own = call(
            start_kernel, ids, [first, None, kept], [wide(size_d, width), low(size_d, width)],
            [both, g_got[i], offset], 10, flops=2 * size_d**2 * width,
        )
        now, gots = own, []
        for source in (3, 2, 1):
            gots.append(lax.ppermute(now, "z", [(source, source - 1)]))
            if source > 1:
                (now,) = call(
                    hop_kernel, ids, [None] * 3, [low(size_d, width)], [a_e, gots[-1], own], 8,
                    flops=2 * size_d**2 * width,
                )
        extra = [] if out_offset is None else [out_offset]
        out_offset, other = call(
            last_kernel, ids, [None, later] + [None] * 4 + [kept] + [pl.BlockSpec(memory_space=pl.ANY)] * len(extra),
            [(kept, wide(*offset.shape)), low(size_d, width)],
            [a_e, both] + gots + [p, offset] + extra, 16, flops=4 * size_d**2 * width,
            aliases={8: 0} if extra else {},
        )
        others.append(swap(other, "x"))
    for i in range(chunks):
        kept = pl.BlockSpec((size_d, width), lambda s, ids, i=i: (0, (1 - ids[0]) * chunks + i))
        (out_offset,) = call(
            add_kernel, ids, [None, kept, pl.BlockSpec(memory_space=pl.ANY)], [(kept, wide(*offset.shape))],
            [others[i], offset, out_offset], 8, aliases={3: 0},
        )
    return (out_gain[None], out_spread[None], out_offset[None])


def solution(mesh):
    steps, rows = mesh.shape["tm"], mesh.shape["rows"]
    if steps == 2**LEVELS and rows == 4:
        devices = mesh.devices.reshape(steps // 2, 2, 2, 2)
        mesh = Mesh(devices, ("z", "x", "y", "c"))
        by_row, by_column = P(("z", "x"), ("y", "c"), None), P(("z", "x"), None, ("y", "c"))
        body = suffix
    else:
        by_row, by_column = P("tm", "rows", None), P("tm", None, "rows")
        body = doubling
    return jax.shard_map(
        body,
        mesh=mesh,
        in_specs=(by_row, by_row, by_column),
        out_specs=(by_row, by_row, by_column),
        check_vma=False,
    )
```

```python
import functools
import math

import jax
import jax.numpy as jnp
from jax import lax
from jax.experimental import pallas as pl
from jax.experimental.pallas import tpu as pltpu
from jax.sharding import Mesh, PartitionSpec as P

LEVELS = 3
LOW = jnp.bfloat16
WIDE = jnp.float32
MIB = 2**20


def shifted(value, axis, steps):
    count = lax.axis_size(axis)
    first, last = (max(0, -steps), min(count, count - steps))
    return lax.ppermute(value, axis, [(source, source + steps) for source in range(first, last)])


def doubling(gains, spreads, offsets):
    gain = gains[0]
    spread = spreads[0]
    offset = offsets[0]
    size_d = gain.shape[1]
    identity = jnp.eye(size_d, dtype=LOW)
    for section_number in range(LEVELS):
        distance = 2**section_number
        beyond = lax.axis_index("tm") + distance >= lax.axis_size("tm")
        own_gain = gain.astype(LOW)
        own_spread = spread.astype(LOW)
        own_offset = offset.astype(LOW)
        own_full = lax.all_gather(own_gain, "rows", axis=0, tiled=True)
        spread_full = lax.all_gather(own_spread, "rows", axis=0, tiled=True)
        far_full, far_spread_full, far_offset = shifted((own_full, spread_full, own_offset), "tm", -distance)
        far_full = jnp.where(beyond, identity, far_full)
        row_start = lax.axis_index("rows") * gain.shape[0]
        own_rows = lax.dynamic_slice_in_dim(own_full, row_start, gain.shape[0], 0)
        middle = jnp.dot(own_rows, far_spread_full, preferred_element_type=WIDE).astype(LOW)
        new_gain = jnp.dot(own_rows, far_full, preferred_element_type=WIDE)
        new_spread = (
            lax.dot_general(middle, own_full, (((1,), (1,)), ((), ())), preferred_element_type=WIDE) + spread
        )
        new_offset = jnp.dot(own_full, far_offset, preferred_element_type=WIDE) + offset
        gain, spread, offset = (new_gain, new_spread, new_offset)
    return (gain[None], spread[None], offset[None])


def swap(value, axis):
    return lax.ppermute(value, axis, [(0, 1), (1, 0)])


def mm(a, b):
    return jnp.dot(a, b, preferred_element_type=WIDE)


def mm_bt(a, b):
    return lax.dot_general(a, b, (((1,), (1,)), ((), ())), preferred_element_type=WIDE)


GROUP = ("y", "c", "x")


def exchange(blocks):
    return lax.all_to_all(blocks, GROUP, 0, 0)


def held(*shape, dtype=LOW):
    return pltpu.VMEM(shape, dtype)


def low(*shape):
    return jax.ShapeDtypeStruct(shape, LOW)


def wide(*shape):
    return jax.ShapeDtypeStruct(shape, WIDE)


ANY = pl.BlockSpec(memory_space=pl.ANY)
VMEM = pl.BlockSpec(memory_space=pltpu.VMEM)
SMEM = pl.BlockSpec(memory_space=pltpu.SMEM)


def call(kernel, ids, operands, outs, mib, flops=0, scratch=(), aliases={}, far_in=(), far_out=()):
    moved = sum(math.prod(a.shape) * jnp.dtype(a.dtype).itemsize for a in list(operands) + list(outs))
    return pl.pallas_call(
        kernel,
        in_specs=[SMEM] + [ANY if i in far_in else VMEM for i in range(len(operands))],
        out_specs=[ANY if i in far_out else VMEM for i in range(len(outs))],
        out_shape=list(outs),
        scratch_shapes=list(scratch),
        input_output_aliases=aliases,
        cost_estimate=pl.CostEstimate(flops=flops, bytes_accessed=moved, transcendentals=0),
        compiler_params=pltpu.CompilerParams(vmem_limit_bytes=mib * MIB),
    )(ids, *operands)


def gather_lanes(blocks, into, start, width):
    for s in range(blocks.shape[0]):
        into[:, s * width : (s + 1) * width] = blocks[s, :, start : start + width]


def pair_kernel(ids, *refs):
    pieces, (both, pair, quarter) = refs[:8], refs[8:]
    group = 2 * ids[1] + ids[2]
    me = 4 * ids[0] + group
    rows = pieces[0].shape[0]
    for i in range(8):
        place = me ^ i
        both[place >> 2, pl.ds(pl.multiple_of((place & 3) * rows, rows), rows), :] = pieces[i][...]
    for r in range(4):
        cut = slice(r * rows, (r + 1) * rows)
        pair[cut, :] = mm(both[0, cut, :], both[1]).astype(LOW)
    quarter[...] = pair[pl.ds(pl.multiple_of(group * rows, rows), rows), :]


def spread_kernel(ids, both, l_low, l_got, m_ref):
    part, rows = l_got.shape[0], l_low.shape[0]

    def product(slab):
        for r in range(4):
            m = mm_bt(both[0, r * rows : (r + 1) * rows, :], slab).astype(LOW)
            m_ref[2 * r] = m
            m_ref[2 * r + 1] = m

    @pl.when(ids[0] == 0)
    def _():
        product(l_got[...])

    @pl.when(ids[0] == 1)
    def _():
        product(l_low[part:, :])


def spread_start_kernel(ids, blocks, both, spread, l_got, prod, a_l, a_low, m):
    part = l_got.shape[0]
    gather_lanes(blocks, m, 0, part)
    prod[...] = mm_bt(m[...], both[0])

    @pl.when(ids[0] == 0)
    def _():
        a_l[...] = (prod[:part, :] + spread[0, :part, :]).T

    @pl.when(ids[0] == 1)
    def _():
        a_l[...] = (prod[part:, :] + l_got[...].astype(WIDE)).T

    a_low[...] = a_l[...].astype(LOW)


def spread_hop_kernel(ids, pair, both, got, m_ref, near):
    part = got.shape[1]
    rows = 2 * part
    m = mm(pair[...], got[...]).astype(LOW)
    m_ref[...] = m
    other = mm(both[1], got[...]).astype(LOW)
    for r in range(4):
        near[2 * r] = m[r * rows : (r + 1) * rows, :]
        near[2 * r + 1] = other[r * rows : (r + 1) * rows, :]


def spread_next_kernel(ids, blocks, pair, a_l, b_l, m):
    gather_lanes(blocks, m, 0, m.shape[0])
    b_l[...] = (mm_bt(pair[...], m[...]) + a_l[...]).astype(LOW)


def near_kernel(ids, blocks, pair, both, prod, spread, out, m):
    gather_lanes(blocks, m, 0, blocks.shape[2])

    @pl.when(ids[0] == 0)
    def _():
        out[...] = mm_bt(m[...], pair[...]) + prod[...] + spread[0]

    @pl.when(ids[0] == 1)
    def _():
        out[...] = mm_bt(m[...], both[1]) + spread[0]


def compose_kernel(ids, pair, both, *refs):
    quarters, (first, second, slab_ref, following) = refs[:4], refs[4:]
    part, rows = slab_ref.shape[1], quarters[0].shape[0]
    group = 2 * ids[1] + ids[2]

    @pl.when(ids[3] % 2 == 0)
    def _():
        for i in range(4):
            following[pl.ds(pl.multiple_of((group ^ i) * rows, rows), rows), :] = quarters[i][...]
        first[...] = mm(pair[...], following[...]).astype(LOW)
        second[...] = mm(both[1], following[...]).astype(LOW)

    @pl.when(ids[3] % 2 == 1)
    def _():
        first[...] = pair[...]
        second[...] = both[1]

    slab_ref[...] = first[:, pl.ds(pl.multiple_of((2 * group + ids[0]) * part, part), part)]


def far_kernel(ids, first, second, e_a, e_b, l_a, l_b, out, far):
    size, part = e_a.shape
    rows = 2 * part

    @pl.when(ids[3] < 2)
    def _():
        far[:, :part] = e_a[...] + e_b[...]

    @pl.when(ids[3] >= 2)
    def _():
        slab = (2 * ids[1] + ids[2]) * 2 + ids[0]
        column = lax.broadcasted_iota(jnp.int32, (size, part), 1) + slab * part
        row = lax.broadcasted_iota(jnp.int32, (size, part), 0)
        far[:, :part] = jnp.where(row == column, 1.0, 0.0).astype(LOW)

    far[:, part:] = l_a[...] + l_b[...]
    one = mm(first[...], far[...]).astype(LOW)
    two = mm(second[...], far[...]).astype(LOW)
    for r in range(4):
        out[2 * r] = one[r * rows : (r + 1) * rows, :]
        out[2 * r + 1] = two[r * rows : (r + 1) * rows, :]


def end_kernel(ids, blocks, first, second, near, out_gain, out_spread, m):
    part = blocks.shape[2] // 2
    gather_lanes(blocks, m, part, part)
    for s in range(blocks.shape[0]):
        out_gain[:, s * part : (s + 1) * part] = blocks[s, :, :part].astype(WIDE)

    @pl.when(ids[0] == 0)
    def _():
        out_spread[...] = mm_bt(m[...], first[...]) + near[...]

    @pl.when(ids[0] == 1)
    def _():
        out_spread[...] = mm_bt(m[...], second[...]) + near[...]


def columns(ref, side, chunk, width):
    start = side * (ref.shape[1] // 2) + chunk * width
    return ref.at[:, pl.ds(pl.multiple_of(start, width), width)]


def start_kernel(chunk, ids, both, got, offset, p_ref, now, keep, sem):
    copy = pltpu.make_async_copy(columns(offset, ids[0], chunk, keep.shape[1]), keep, sem)
    copy.start()

    @pl.when(ids[0] == 0)
    def _():
        p_ref[...] = mm(both[0], got[...])

    copy.wait()

    @pl.when(ids[0] == 0)
    def _():
        now[...] = (p_ref[...] + keep[...]).astype(LOW)

    @pl.when(ids[0] == 1)
    def _():
        p = mm(both[0], keep[...].astype(LOW))
        p_ref[...] = p
        now[...] = (p + got[...].astype(WIDE)).astype(LOW)


def hop_kernel(ids, pair, got, own, now):
    now[...] = (mm(pair[...], got[...]) + own[...].astype(WIDE)).astype(LOW)


def last_kernel(chunk, ids, pair, both, got_a, got_b, got_c, p_ref, offset, *refs):
    out, send, keep, far, sems = refs[-5:]
    width = keep.shape[1]
    copy = pltpu.make_async_copy(columns(offset, ids[0], chunk, width), keep, sems.at[0])
    copy.start()
    far[...] = got_a[...] + got_b[...] + got_c[...]

    @pl.when(ids[0] == 0)
    def _():
        send[...] = mm(both[1], far[...]).astype(LOW)

    @pl.when(ids[0] == 1)
    def _():
        send[...] = (mm(pair[...], far[...]) + p_ref[...]).astype(LOW)

    copy.wait()

    @pl.when(ids[0] == 0)
    def _():
        keep[...] = mm(pair[...], far[...]) + p_ref[...] + keep[...]

    @pl.when(ids[0] == 1)
    def _():
        keep[...] = mm(both[1], far[...]) + keep[...]

    copy = pltpu.make_async_copy(keep, columns(out, ids[0], chunk, width), sems.at[1])
    copy.start()
    copy.wait()


def add_kernel(chunk, ids, got, offset, into, out, keep, sems):
    width = keep.shape[1]
    copy = pltpu.make_async_copy(columns(offset, 1 - ids[0], chunk, width), keep, sems.at[0])
    copy.start()
    copy.wait()
    keep[...] = got[...].astype(WIDE) + keep[...]
    copy = pltpu.make_async_copy(keep, columns(out, 1 - ids[0], chunk, width), sems.at[1])
    copy.start()
    copy.wait()


def suffix(gains, spreads, offsets):
    x, y, c, z = (lax.axis_index(name) for name in ("x", "y", "c", "z"))
    even = x == 0
    gain, offset = gains[0], offsets[0]
    rows, size_d = gain.shape
    part = rows // 2
    half = offset.shape[1] // 2
    chunks = 2
    width = half // chunks
    ids = jnp.stack([x, y, c, z]).astype(jnp.int32)
    level = [(3, 2), (1, 0)]

    e_low = gain.astype(LOW)
    e_x, e_y = swap(e_low, "x"), swap(e_low, "y")
    e_xy = swap(e_x, "y")
    pieces = [e_low, None, e_y, None, e_x, None, e_xy, None]
    for i in range(0, 8, 2):
        pieces[i + 1] = swap(pieces[i], "c")

    l_low = spreads[0].astype(LOW)
    l_send = jnp.where(even, l_low[part:], l_low[:part])
    g_send = jnp.where(even, offset[:, half:], offset[:, :half]).astype(LOW)
    l_send, g_send, e_x = lax.optimization_barrier((l_send, g_send, e_x))
    l_got = swap(l_send, "x")
    g_got = [swap(g_send[:, i * width : (i + 1) * width], "x") for i in range(chunks)]

    both, a_e, quarter = call(
        pair_kernel, ids, pieces, [held(2, size_d, size_d), held(size_d, size_d), low(rows, size_d)], 16,
        flops=2 * size_d**3,
    )
    (m,) = call(spread_kernel, ids, [both, l_low, l_got], [low(8, rows, part)], 12, flops=2 * part * size_d**2)
    prod, a_l, a_low = call(
        spread_start_kernel, ids, [exchange(m), both, spreads, l_got],
        [held(rows, size_d, dtype=WIDE), held(size_d, part, dtype=WIDE), low(size_d, part)],
        14, flops=2 * rows * size_d**2, scratch=[pltpu.VMEM((rows, size_d), LOW)],
    )

    l_next = lax.ppermute(a_low, "z", level)
    quarter = lax.ppermute(quarter, "z", level)
    quarter_y = swap(quarter, "y")
    quarters = [quarter, swap(quarter, "c"), quarter_y, swap(quarter_y, "c")]
    m, near = call(
        spread_hop_kernel, ids, [a_e, both, l_next], [low(size_d, part), low(8, rows, part)], 12,
        flops=4 * part * size_d**2,
    )
    (b_l,) = call(
        spread_next_kernel, ids, [exchange(m.reshape(8, part, part)), a_e, a_l], [low(size_d, part)], 8,
        flops=2 * part * size_d**2, scratch=[pltpu.VMEM((part, size_d), LOW)],
    )
    l_far = lax.ppermute(b_l, "z", [(2, 1)]), lax.ppermute(b_l, "z", [(2, 0)])
    c0_e, c1_e, e_slab = call(
        compose_kernel, ids, [a_e, both, *quarters],
        [held(size_d, size_d), held(size_d, size_d), low(size_d, part)], 14,
        flops=4 * size_d**3, scratch=[pltpu.VMEM((size_d, size_d), LOW)],
    )
    e_far = lax.ppermute(e_slab, "z", [(2, 1)]), lax.ppermute(e_slab, "z", [(2, 0)])
    (near,) = call(
        near_kernel, ids, [exchange(near), a_e, both, prod, spreads], [held(rows, size_d, dtype=WIDE)], 12,
        flops=2 * rows * size_d**2, scratch=[pltpu.VMEM((rows, size_d), LOW)],
    )

    (m,) = call(
        far_kernel, ids, [c0_e, c1_e, *e_far, *l_far], [low(8, rows, rows)], 12,
        flops=4 * rows * size_d**2, scratch=[pltpu.VMEM((size_d, rows), LOW)],
    )
    out_gain, out_spread = call(
        end_kernel, ids, [exchange(m), c0_e, c1_e, near], [wide(rows, size_d), wide(rows, size_d)], 14,
        flops=2 * rows * size_d**2, scratch=[pltpu.VMEM((rows, size_d), LOW)],
    )

    out_offset, others = None, []
    keep = pltpu.VMEM((size_d, width), WIDE)
    column = pltpu.VMEM((size_d, width), LOW)
    for i in range(chunks):
        p, own = call(
            functools.partial(start_kernel, i), ids, [both, g_got[i], offset],
            [held(size_d, width, dtype=WIDE), low(size_d, width)], 8, flops=2 * size_d**2 * width,
            far_in=(2,), scratch=[keep, pltpu.SemaphoreType.DMA(())],
        )
        now, gots = own, []
        for source in (3, 2, 1):
            gots.append(lax.ppermute(now, "z", [(source, source - 1)]))
            if source > 1:
                (now,) = call(
                    hop_kernel, ids, [a_e, gots[-1], own], [low(size_d, width)], 8, flops=2 * size_d**2 * width
                )
        extra = [] if out_offset is None else [out_offset]
        out_offset, other = call(
            functools.partial(last_kernel, i), ids, [a_e, both] + gots + [p, offset] + extra,
            [wide(*offset.shape), low(size_d, width)], 12, flops=4 * size_d**2 * width,
            far_in=(6, 7), far_out=(0,), aliases={8: 0} if extra else {},
            scratch=[keep, column, pltpu.SemaphoreType.DMA((2,))],
        )
        others.append(swap(other, "x"))
    for i in range(chunks):
        (out_offset,) = call(
            functools.partial(add_kernel, i), ids, [others[i], offset, out_offset], [wide(*offset.shape)], 8,
            far_in=(1, 2), far_out=(0,), aliases={3: 0}, scratch=[keep, pltpu.SemaphoreType.DMA((2,))],
        )
    return (out_gain[None], out_spread[None], out_offset[None])


def solution(mesh):
    steps, rows = mesh.shape["tm"], mesh.shape["rows"]
    if steps == 2**LEVELS and rows == 4:
        devices = mesh.devices.reshape(steps // 2, 2, 2, 2)
        mesh = Mesh(devices, ("z", "x", "y", "c"))
        by_row, by_column = P(("z", "x"), ("y", "c"), None), P(("z", "x"), None, ("y", "c"))
        body = suffix
    else:
        by_row, by_column = P("tm", "rows", None), P("tm", None, "rows")
        body = doubling
    return jax.shard_map(
        body,
        mesh=mesh,
        in_specs=(by_row, by_row, by_column),
        out_specs=(by_row, by_row, by_column),
        check_vma=False,
    )
```

```python
import functools

import jax
import jax.numpy as jnp
from jax import lax
from jax.experimental import pallas as pl
from jax.experimental.pallas import tpu as pltpu
from jax.sharding import Mesh, PartitionSpec as P

LEVELS = 3
LOW = jnp.bfloat16
WIDE = jnp.float32
MIB = 2**20


def shifted(value, axis, steps):
    count = lax.axis_size(axis)
    first, last = (max(0, -steps), min(count, count - steps))
    return lax.ppermute(value, axis, [(source, source + steps) for source in range(first, last)])


def doubling(gains, spreads, offsets):
    gain = gains[0]
    spread = spreads[0]
    offset = offsets[0]
    size_d = gain.shape[1]
    identity = jnp.eye(size_d, dtype=LOW)
    for section_number in range(LEVELS):
        distance = 2**section_number
        beyond = lax.axis_index("tm") + distance >= lax.axis_size("tm")
        own_gain = gain.astype(LOW)
        own_spread = spread.astype(LOW)
        own_offset = offset.astype(LOW)
        own_full = lax.all_gather(own_gain, "rows", axis=0, tiled=True)
        spread_full = lax.all_gather(own_spread, "rows", axis=0, tiled=True)
        far_full, far_spread_full, far_offset = shifted((own_full, spread_full, own_offset), "tm", -distance)
        far_full = jnp.where(beyond, identity, far_full)
        row_start = lax.axis_index("rows") * gain.shape[0]
        own_rows = lax.dynamic_slice_in_dim(own_full, row_start, gain.shape[0], 0)
        middle = jnp.dot(own_rows, far_spread_full, preferred_element_type=WIDE).astype(LOW)
        new_gain = jnp.dot(own_rows, far_full, preferred_element_type=WIDE)
        new_spread = (
            lax.dot_general(middle, own_full, (((1,), (1,)), ((), ())), preferred_element_type=WIDE) + spread
        )
        new_offset = jnp.dot(own_full, far_offset, preferred_element_type=WIDE) + offset
        gain, spread, offset = (new_gain, new_spread, new_offset)
    return (gain[None], spread[None], offset[None])


def swap(value, axis):
    return lax.ppermute(value, axis, [(0, 1), (1, 0)])


def mm(a, b):
    return jnp.dot(a, b, preferred_element_type=WIDE)


def mm_bt(a, b):
    return lax.dot_general(a, b, (((1,), (1,)), ((), ())), preferred_element_type=WIDE)


GROUP = ("y", "c", "x")


def exchange(blocks):
    return lax.all_to_all(blocks, GROUP, 0, 0)


def held(*shape, dtype=LOW):
    return pltpu.VMEM(shape, dtype)


def low(*shape):
    return jax.ShapeDtypeStruct(shape, LOW)


def wide(*shape):
    return jax.ShapeDtypeStruct(shape, WIDE)


ANY = pl.BlockSpec(memory_space=pl.ANY)
VMEM = pl.BlockSpec(memory_space=pltpu.VMEM)
SMEM = pl.BlockSpec(memory_space=pltpu.SMEM)


class Order:
    def __init__(self, ids):
        self.ids = ids
        self.token = jnp.zeros((8, 128), jnp.int32)

    def call(self, kernel, operands, outs, mib, scratch=(), aliases={}, far_in=(), far_out=()):
        n, m = len(operands), len(outs)

        def body(ids, token, *refs):
            kernel(ids, *refs[: n + m], *refs[n + m + 1 :])

        results = pl.pallas_call(
            body,
            in_specs=[SMEM, ANY] + [ANY if i in far_in else VMEM for i in range(n)],
            out_specs=[ANY if i in far_out else VMEM for i in range(m)] + [ANY],
            out_shape=list(outs) + [jax.ShapeDtypeStruct(self.token.shape, jnp.int32)],
            scratch_shapes=list(scratch),
            input_output_aliases={1: m} | {2 + i: o for i, o in aliases.items()},
            cost_estimate=pl.CostEstimate(flops=1, bytes_accessed=1, transcendentals=0),
            compiler_params=pltpu.CompilerParams(vmem_limit_bytes=mib * MIB),
        )(self.ids, self.token, *operands)
        self.token = results[-1]
        return results[:-1]


def gather_lanes(blocks, into, start, width):
    for s in range(blocks.shape[0]):
        into[:, s * width : (s + 1) * width] = blocks[s, :, start : start + width]


def pair_kernel(ids, *refs):
    pieces, (both, pair, quarter, sems) = refs[:8], refs[8:]
    group = 2 * ids[1] + ids[2]
    me = 4 * ids[0] + group
    rows = pieces[0].shape[0]
    copies = []
    for i in range(8):
        place = me ^ i
        into = both.at[place >> 2, pl.ds(pl.multiple_of((place & 3) * rows, rows), rows), :]
        copies.append(pltpu.make_async_copy(pieces[i], into, sems.at[i]))
        copies[-1].start()
    for copy in copies:
        copy.wait()
    for r in range(4):
        cut = slice(r * rows, (r + 1) * rows)
        pair[cut, :] = mm(both[0, cut, :], both[1]).astype(LOW)
    quarter[...] = pair[pl.ds(pl.multiple_of(group * rows, rows), rows), :]


def spread_kernel(ids, both, l_low, l_got, m_ref):
    part, rows = l_got.shape[0], l_low.shape[0]

    def product(slab):
        for r in range(4):
            m = mm_bt(both[0, r * rows : (r + 1) * rows, :], slab).astype(LOW)
            m_ref[2 * r] = m
            m_ref[2 * r + 1] = m

    @pl.when(ids[0] == 0)
    def _():
        product(l_got[...])

    @pl.when(ids[0] == 1)
    def _():
        product(l_low[part:, :])


def spread_start_kernel(ids, blocks, both, spread, l_got, prod, a_l, a_low, m):
    part = l_got.shape[0]
    gather_lanes(blocks, m, 0, part)
    prod[...] = mm_bt(m[...], both[0])

    @pl.when(ids[0] == 0)
    def _():
        a_l[...] = (prod[:part, :] + spread[0, :part, :]).T

    @pl.when(ids[0] == 1)
    def _():
        a_l[...] = (prod[part:, :] + l_got[...].astype(WIDE)).T

    a_low[...] = a_l[...].astype(LOW)


def spread_hop_kernel(ids, pair, both, got, m_ref, near):
    part = got.shape[1]
    rows = 2 * part
    m = mm(pair[...], got[...]).astype(LOW)
    m_ref[...] = m
    other = mm(both[1], got[...]).astype(LOW)
    for r in range(4):
        near[2 * r] = m[r * rows : (r + 1) * rows, :]
        near[2 * r + 1] = other[r * rows : (r + 1) * rows, :]


def spread_next_kernel(ids, blocks, pair, a_l, b_l, m):
    gather_lanes(blocks, m, 0, m.shape[0])
    b_l[...] = (mm_bt(pair[...], m[...]) + a_l[...]).astype(LOW)


def near_kernel(ids, blocks, pair, both, prod, spread, out, m):
    gather_lanes(blocks, m, 0, blocks.shape[2])

    @pl.when(ids[0] == 0)
    def _():
        out[...] = mm_bt(m[...], pair[...]) + prod[...] + spread[0]

    @pl.when(ids[0] == 1)
    def _():
        out[...] = mm_bt(m[...], both[1]) + spread[0]


def compose_kernel(ids, pair, both, *refs):
    quarters, (first, second, slab_ref, following) = refs[:4], refs[4:]
    part, rows = slab_ref.shape[1], quarters[0].shape[0]
    group = 2 * ids[1] + ids[2]

    @pl.when(ids[3] % 2 == 0)
    def _():
        for i in range(4):
            following[pl.ds(pl.multiple_of((group ^ i) * rows, rows), rows), :] = quarters[i][...]
        first[...] = mm(pair[...], following[...]).astype(LOW)
        second[...] = mm(both[1], following[...]).astype(LOW)

    @pl.when(ids[3] % 2 == 1)
    def _():
        first[...] = pair[...]
        second[...] = both[1]

    slab_ref[...] = first[:, pl.ds(pl.multiple_of((2 * group + ids[0]) * part, part), part)]


def far_kernel(ids, first, second, e_a, e_b, l_a, l_b, out, far):
    size, part = e_a.shape
    rows = 2 * part

    @pl.when(ids[3] < 2)
    def _():
        far[:, :part] = e_a[...] + e_b[...]

    @pl.when(ids[3] >= 2)
    def _():
        slab = (2 * ids[1] + ids[2]) * 2 + ids[0]
        column = lax.broadcasted_iota(jnp.int32, (size, part), 1) + slab * part
        row = lax.broadcasted_iota(jnp.int32, (size, part), 0)
        far[:, :part] = jnp.where(row == column, 1.0, 0.0).astype(LOW)

    far[:, part:] = l_a[...] + l_b[...]
    one = mm(first[...], far[...]).astype(LOW)
    two = mm(second[...], far[...]).astype(LOW)
    for r in range(4):
        out[2 * r] = one[r * rows : (r + 1) * rows, :]
        out[2 * r + 1] = two[r * rows : (r + 1) * rows, :]


def end_kernel(ids, blocks, first, second, near, out_gain, out_spread, m):
    part = blocks.shape[2] // 2
    gather_lanes(blocks, m, part, part)
    for s in range(blocks.shape[0]):
        out_gain[:, s * part : (s + 1) * part] = blocks[s, :, :part].astype(WIDE)

    @pl.when(ids[0] == 0)
    def _():
        out_spread[...] = mm_bt(m[...], first[...]) + near[...]

    @pl.when(ids[0] == 1)
    def _():
        out_spread[...] = mm_bt(m[...], second[...]) + near[...]


def columns(ref, side, chunk, width):
    start = side * (ref.shape[1] // 2) + chunk * width
    return ref.at[:, pl.ds(pl.multiple_of(start, width), width)]


def start_kernel(chunk, ids, both, got, offset, p_ref, now, keep, sem):
    copy = pltpu.make_async_copy(columns(offset, ids[0], chunk, keep.shape[1]), keep, sem)
    copy.start()

    @pl.when(ids[0] == 0)
    def _():
        p_ref[...] = mm(both[0], got[...])

    copy.wait()

    @pl.when(ids[0] == 0)
    def _():
        now[...] = (p_ref[...] + keep[...]).astype(LOW)

    @pl.when(ids[0] == 1)
    def _():
        p = mm(both[0], keep[...].astype(LOW))
        p_ref[...] = p
        now[...] = (p + got[...].astype(WIDE)).astype(LOW)


def hop_kernel(ids, pair, got, own, now):
    now[...] = (mm(pair[...], got[...]) + own[...].astype(WIDE)).astype(LOW)


def last_kernel(chunk, ids, pair, both, got_a, got_b, got_c, p_ref, offset, *refs):
    out, send, keep, far, sems = refs[-5:]
    width = keep.shape[1]
    copy = pltpu.make_async_copy(columns(offset, ids[0], chunk, width), keep, sems.at[0])
    copy.start()
    far[...] = got_a[...] + got_b[...] + got_c[...]

    @pl.when(ids[0] == 0)
    def _():
        send[...] = mm(both[1], far[...]).astype(LOW)

    @pl.when(ids[0] == 1)
    def _():
        send[...] = (mm(pair[...], far[...]) + p_ref[...]).astype(LOW)

    copy.wait()

    @pl.when(ids[0] == 0)
    def _():
        keep[...] = mm(pair[...], far[...]) + p_ref[...] + keep[...]

    @pl.when(ids[0] == 1)
    def _():
        keep[...] = mm(both[1], far[...]) + keep[...]

    copy = pltpu.make_async_copy(keep, columns(out, ids[0], chunk, width), sems.at[1])
    copy.start()
    copy.wait()


def add_kernel(chunk, ids, got, offset, into, out, keep, sems):
    width = keep.shape[1]
    copy = pltpu.make_async_copy(columns(offset, 1 - ids[0], chunk, width), keep, sems.at[0])
    copy.start()
    copy.wait()
    keep[...] = got[...].astype(WIDE) + keep[...]
    copy = pltpu.make_async_copy(keep, columns(out, 1 - ids[0], chunk, width), sems.at[1])
    copy.start()
    copy.wait()


def suffix(gains, spreads, offsets):
    x, y, c, z = (lax.axis_index(name) for name in ("x", "y", "c", "z"))
    gain = gains[0]
    rows, size_d = gain.shape
    part = rows // 2
    chunks = 2
    half = offsets.shape[2] // 2
    width = half // chunks
    ids = jnp.stack([x, y, c, z]).astype(jnp.int32)
    level = [(3, 2), (1, 0)]
    order = Order(ids)
    in_hbm = lambda a: pltpu.with_memory_space_constraint(a, pltpu.HBM)

    e_low = gain.astype(LOW)
    e_x, e_y = swap(e_low, "x"), swap(e_low, "y")

    l_low = spreads[0].astype(LOW)
    l_send = lax.dynamic_slice_in_dim(l_low, (1 - x) * part, part, 0)
    g_send = [
        lax.dynamic_slice_in_dim(offsets[0], (1 - x) * half + i * width, width, 1).astype(LOW) for i in range(chunks)
    ]
    l_send, g_send[0], e_x = lax.optimization_barrier((l_send, g_send[0], e_x))
    e_xy = swap(e_x, "y")
    l_got = swap(l_send, "x")
    g_got = [swap(g_send[0], "x")]
    for i in range(1, chunks):
        g_send[i], g_got[-1] = lax.optimization_barrier((g_send[i], g_got[-1]))
        g_got.append(swap(g_send[i], "x"))
    pieces = [e_low, None, e_y, None, e_x, None, e_xy, None]
    for i in range(0, 8, 2):
        pieces[i + 1] = swap(pieces[i], "c")
    offset = in_hbm(offsets[0])

    keep = pltpu.VMEM((size_d, width), WIDE)
    column = pltpu.VMEM((size_d, width), LOW)
    slab_rows = pltpu.VMEM((rows, size_d), LOW)

    def start(i):
        return order.call(
            functools.partial(start_kernel, i), [both, g_got[i], offset],
            [held(size_d, width, dtype=WIDE), low(size_d, width)], 8,
            far_in=(2,), scratch=[keep, pltpu.SemaphoreType.DMA(())],
        )

    def down(value, source):
        return lax.ppermute(value, "z", [(source, source - 1)])

    def hop(i, got):
        return order.call(hop_kernel, [a_e, got, own[i]], [low(size_d, width)], 8)[0]

    def last(i, into):
        extra = [] if into is None else [into]
        return order.call(
            functools.partial(last_kernel, i), [a_e, both] + gots[i] + [p[i], offset] + extra,
            [wide(*offset.shape), low(size_d, width)], 12,
            far_in=(6, 7), far_out=(0,), aliases={7: 0} if extra else {},
            scratch=[keep, column, pltpu.SemaphoreType.DMA((2,))],
        )

    def add(i, got, into):
        return order.call(
            functools.partial(add_kernel, i), [got, offset, into], [wide(*offset.shape)], 8,
            far_in=(1, 2), far_out=(0,), aliases={2: 0}, scratch=[keep, pltpu.SemaphoreType.DMA((2,))],
        )[0]

    both, a_e, quarter = order.call(
        pair_kernel, [in_hbm(piece) for piece in pieces],
        [held(2, size_d, size_d), held(size_d, size_d), low(rows, size_d)], 16,
        far_in=range(8), scratch=[pltpu.SemaphoreType.DMA((8,))],
    )
    quarter = lax.ppermute(quarter, "z", level)
    quarter_y = swap(quarter, "y")
    quarters = [quarter, swap(quarter, "c"), quarter_y, swap(quarter_y, "c")]
    (m,) = order.call(spread_kernel, [both, l_low, l_got], [low(8, rows, part)], 12)
    m = exchange(m)
    p, own, gots = [None] * chunks, [None] * chunks, [[] for _ in range(chunks)]
    p[0], own[0] = start(0)
    gots[0].append(down(own[0], 3))
    prod, a_l, a_low = order.call(
        spread_start_kernel, [m, both, spreads, l_got],
        [held(rows, size_d, dtype=WIDE), held(size_d, part, dtype=WIDE), low(size_d, part)], 14, scratch=[slab_rows],
    )
    l_next = lax.ppermute(a_low, "z", level)
    p[1], own[1] = start(1)
    gots[1].append(down(own[1], 3))
    gots[0].append(down(hop(0, gots[0][0]), 2))

    m, near = order.call(spread_hop_kernel, [a_e, both, l_next], [low(size_d, part), low(8, rows, part)], 12)
    m = exchange(m.reshape(8, part, part))
    near = exchange(near)
    gots[1].append(down(hop(1, gots[1][0]), 2))
    (b_l,) = order.call(
        spread_next_kernel, [m, a_e, a_l], [low(size_d, part)], 8, scratch=[pltpu.VMEM((part, size_d), LOW)]
    )
    l_far = lax.ppermute(b_l, "z", [(2, 1)]), lax.ppermute(b_l, "z", [(2, 0)])
    gots[0].append(down(hop(0, gots[0][1]), 1))
    c0_e, c1_e, e_slab = order.call(
        compose_kernel, [a_e, both, *quarters], [held(size_d, size_d), held(size_d, size_d), low(size_d, part)], 14,
        scratch=[pltpu.VMEM((size_d, size_d), LOW)],
    )
    e_far = lax.ppermute(e_slab, "z", [(2, 1)]), lax.ppermute(e_slab, "z", [(2, 0)])
    gots[1].append(down(hop(1, gots[1][1]), 1))
    (near,) = order.call(
        near_kernel, [near, a_e, both, prod, spreads], [held(rows, size_d, dtype=WIDE)], 12, scratch=[slab_rows]
    )

    out_offset, other0 = last(0, None)
    other0 = swap(other0, "x")
    (m,) = order.call(
        far_kernel, [c0_e, c1_e, *e_far, *l_far], [low(8, rows, rows)], 12, scratch=[pltpu.VMEM((size_d, rows), LOW)]
    )
    m = exchange(m)
    out_offset, other1 = last(1, out_offset)
    other1 = swap(other1, "x")
    out_offset = add(0, other0, out_offset)
    out_gain, out_spread = order.call(
        end_kernel, [m, c0_e, c1_e, near], [wide(rows, size_d), wide(rows, size_d)], 14, scratch=[slab_rows]
    )
    out_offset = add(1, other1, out_offset)
    return (out_gain[None], out_spread[None], out_offset[None])


def solution(mesh):
    steps, rows = mesh.shape["tm"], mesh.shape["rows"]
    if steps == 2**LEVELS and rows == 4:
        devices = mesh.devices.reshape(steps // 2, 2, 2, 2)
        mesh = Mesh(devices, ("z", "x", "y", "c"))
        by_row, by_column = P(("z", "x"), ("y", "c"), None), P(("z", "x"), None, ("y", "c"))
        body = suffix
    else:
        by_row, by_column = P("tm", "rows", None), P("tm", None, "rows")
        body = doubling
    return jax.shard_map(
        body,
        mesh=mesh,
        in_specs=(by_row, by_row, by_column),
        out_specs=(by_row, by_row, by_column),
        check_vma=False,
    )
```

```python
import functools

import jax
import jax.numpy as jnp
from jax import lax
from jax.experimental import pallas as pl
from jax.experimental.pallas import tpu as pltpu
from jax.sharding import Mesh, PartitionSpec as P

LEVELS = 3
LOW = jnp.bfloat16
WIDE = jnp.float32
MIB = 2**20


def shifted(value, axis, steps):
    count = lax.axis_size(axis)
    first, last = (max(0, -steps), min(count, count - steps))
    return lax.ppermute(value, axis, [(source, source + steps) for source in range(first, last)])


def doubling(gains, spreads, offsets):
    gain = gains[0]
    spread = spreads[0]
    offset = offsets[0]
    size_d = gain.shape[1]
    identity = jnp.eye(size_d, dtype=LOW)
    for section_number in range(LEVELS):
        distance = 2**section_number
        beyond = lax.axis_index("tm") + distance >= lax.axis_size("tm")
        own_gain = gain.astype(LOW)
        own_spread = spread.astype(LOW)
        own_offset = offset.astype(LOW)
        own_full = lax.all_gather(own_gain, "rows", axis=0, tiled=True)
        spread_full = lax.all_gather(own_spread, "rows", axis=0, tiled=True)
        far_full, far_spread_full, far_offset = shifted((own_full, spread_full, own_offset), "tm", -distance)
        far_full = jnp.where(beyond, identity, far_full)
        row_start = lax.axis_index("rows") * gain.shape[0]
        own_rows = lax.dynamic_slice_in_dim(own_full, row_start, gain.shape[0], 0)
        middle = jnp.dot(own_rows, far_spread_full, preferred_element_type=WIDE).astype(LOW)
        new_gain = jnp.dot(own_rows, far_full, preferred_element_type=WIDE)
        new_spread = (
            lax.dot_general(middle, own_full, (((1,), (1,)), ((), ())), preferred_element_type=WIDE) + spread
        )
        new_offset = jnp.dot(own_full, far_offset, preferred_element_type=WIDE) + offset
        gain, spread, offset = (new_gain, new_spread, new_offset)
    return (gain[None], spread[None], offset[None])


def swap(value, axis):
    return lax.ppermute(value, axis, [(0, 1), (1, 0)])


def mm(a, b):
    return jnp.dot(a, b, preferred_element_type=WIDE)


def mm_bt(a, b):
    return lax.dot_general(a, b, (((1,), (1,)), ((), ())), preferred_element_type=WIDE)


GROUP = ("y", "c", "x")


def exchange(blocks):
    return lax.all_to_all(blocks, GROUP, 0, 0)


def low(*shape):
    return jax.ShapeDtypeStruct(shape, LOW)


def wide(*shape):
    return jax.ShapeDtypeStruct(shape, WIDE)


ANY = pl.BlockSpec(memory_space=pl.ANY)
VMEM = pl.BlockSpec(memory_space=pltpu.VMEM)
SMEM = pl.BlockSpec(memory_space=pltpu.SMEM)


class Refs:
    pass


class Order:
    def __init__(self, ids):
        self.ids = ids
        self.token = jnp.zeros((8, 128), jnp.int32)
        self.state = {}

    def call(self, kernel, operands, outs, mib, new={}, drop=(), scratch=(), aliases={}, far_in=(), far_out=()):
        n, m, old = len(operands), len(outs), list(self.state)
        going = [name for name in old if name not in drop]

        def body(ids, token, *refs):
            at = Refs()
            for name, ref in zip(old, refs):
                setattr(at, name, ref)
            ins, refs = refs[len(old) : len(old) + n], refs[len(old) + n :]
            results, refs = refs[:m], refs[m + 1 :]
            for name, ref in zip(going, refs):
                if name.startswith("far"):
                    setattr(at, name + "_next", ref)
            refs = refs[len(going) :]
            for name, ref in zip(new, refs):
                setattr(at, name, ref)
            kernel(ids, at, *ins, *results, *refs[len(new) :])

        first = 2 + len(old)
        links = {1: m} | {first + i: o for i, o in aliases.items()}
        links |= {2 + old.index(name): m + 1 + i for i, name in enumerate(going)}
        results = pl.pallas_call(
            body,
            in_specs=[SMEM, ANY] + [VMEM] * len(old) + [ANY if i in far_in else VMEM for i in range(n)],
            out_specs=[ANY if i in far_out else VMEM for i in range(m)] + [ANY] + [VMEM] * (len(going) + len(new)),
            out_shape=list(outs)
            + [jax.ShapeDtypeStruct(self.token.shape, jnp.int32)]
            + [pltpu.VMEM(self.state[name].shape, self.state[name].dtype) for name in going]
            + [pltpu.VMEM(shape, dtype) for shape, dtype in new.values()],
            scratch_shapes=list(scratch),
            input_output_aliases=links,
            cost_estimate=pl.CostEstimate(flops=1, bytes_accessed=1, transcendentals=0),
            compiler_params=pltpu.CompilerParams(vmem_limit_bytes=mib * MIB),
        )(self.ids, self.token, *self.state.values(), *operands)
        self.token = results[m]
        self.state = dict(zip(going + list(new), results[m + 1 :]))
        return results[:m]


def gather_lanes(blocks, into, start, width):
    for s in range(blocks.shape[0]):
        into[:, s * width : (s + 1) * width] = blocks[s, :, start : start + width]


def pair_kernel(ids, at, *refs):
    pieces, (quarter, sems) = refs[:8], refs[8:]
    group = 2 * ids[1] + ids[2]
    me = 4 * ids[0] + group
    rows = pieces[0].shape[0]
    copies = []
    for i in range(8):
        place = me ^ i
        into = at.both.at[place >> 2, pl.ds(pl.multiple_of((place & 3) * rows, rows), rows), :]
        copies.append(pltpu.make_async_copy(pieces[i], into, sems.at[i]))
        copies[-1].start()
    for copy in copies:
        copy.wait()
    for r in range(4):
        cut = slice(r * rows, (r + 1) * rows)
        at.pair[cut, :] = mm(at.both[0, cut, :], at.both[1]).astype(LOW)
    quarter[...] = at.pair[pl.ds(pl.multiple_of(group * rows, rows), rows), :]


def spread_kernel(ids, at, l_low, l_got, m_ref):
    part, rows = l_got.shape[0], l_low.shape[0]

    def product(slab):
        for r in range(4):
            m = mm_bt(at.both[0, r * rows : (r + 1) * rows, :], slab).astype(LOW)
            m_ref[2 * r] = m
            m_ref[2 * r + 1] = m

    @pl.when(ids[0] == 0)
    def _():
        product(l_got[...])

    @pl.when(ids[0] == 1)
    def _():
        product(l_low[part:, :])


def spread_start_kernel(ids, at, blocks, spread, l_got, a_low, m):
    part = l_got.shape[0]
    gather_lanes(blocks, m, 0, part)
    at.prod[...] = mm_bt(m[...], at.both[0])

    @pl.when(ids[0] == 0)
    def _():
        at.slab[...] = (at.prod[:part, :] + spread[0, :part, :]).T

    @pl.when(ids[0] == 1)
    def _():
        at.slab[...] = (at.prod[part:, :] + l_got[...].astype(WIDE)).T

    a_low[...] = at.slab[...].astype(LOW)


def spread_hop_kernel(ids, at, got, m_ref, near):
    part = got.shape[1]
    rows = 2 * part
    m = mm(at.pair[...], got[...]).astype(LOW)
    m_ref[...] = m
    other = mm(at.both[1], got[...]).astype(LOW)
    for r in range(4):
        near[2 * r] = m[r * rows : (r + 1) * rows, :]
        near[2 * r + 1] = other[r * rows : (r + 1) * rows, :]


def spread_next_kernel(ids, at, blocks, b_l, m):
    gather_lanes(blocks, m, 0, m.shape[0])
    b_l[...] = (mm_bt(at.pair[...], m[...]) + at.slab[...]).astype(LOW)


def near_kernel(ids, at, blocks, spread, m):
    gather_lanes(blocks, m, 0, blocks.shape[2])

    @pl.when(ids[0] == 0)
    def _():
        at.near[...] = mm_bt(m[...], at.pair[...]) + at.prod[...] + spread[0]

    @pl.when(ids[0] == 1)
    def _():
        at.near[...] = mm_bt(m[...], at.both[1]) + spread[0]


def next_gain_kernel(ids, at, *refs):
    quarters, (slab_ref, sems) = refs[:4], refs[4:]
    part, rows = slab_ref.shape[1], quarters[0].shape[0]
    group = 2 * ids[1] + ids[2]
    copies = []
    for i in range(4):
        into = at.following.at[pl.ds(pl.multiple_of((group ^ i) * rows, rows), rows), :]
        copies.append(pltpu.make_async_copy(quarters[i], into, sems.at[i]))
        copies[-1].start()
    for copy in copies:
        copy.wait()
    slab = pl.ds(pl.multiple_of((2 * group + ids[0]) * part, part), part)
    slab_ref[...] = mm(at.pair[...], at.following[:, slab]).astype(LOW)


def far_kernel(ids, at, e_a, e_b, l_a, l_b, out, far):
    size, part = e_a.shape
    rows = 2 * part

    @pl.when(ids[3] < 2)
    def _():
        far[:, :part] = e_a[...] + e_b[...]

    @pl.when(ids[3] >= 2)
    def _():
        slab = (2 * ids[1] + ids[2]) * 2 + ids[0]
        column = lax.broadcasted_iota(jnp.int32, (size, part), 1) + slab * part
        row = lax.broadcasted_iota(jnp.int32, (size, part), 0)
        far[:, :part] = jnp.where(row == column, 1.0, 0.0).astype(LOW)

    far[:, part:] = l_a[...] + l_b[...]

    @pl.when(ids[3] % 2 == 0)
    def _():
        far[...] = mm(at.following[...], far[...]).astype(LOW)

    one = mm(at.pair[...], far[...]).astype(LOW)
    two = mm(at.both[1], far[...]).astype(LOW)
    for r in range(4):
        out[2 * r] = one[r * rows : (r + 1) * rows, :]
        out[2 * r + 1] = two[r * rows : (r + 1) * rows, :]


def end_kernel(ids, at, blocks, out_gain, out_spread, m):
    part = blocks.shape[2] // 2
    gather_lanes(blocks, m, part, part)
    for s in range(blocks.shape[0]):
        out_gain[:, s * part : (s + 1) * part] = blocks[s, :, :part].astype(WIDE)

    @pl.when(ids[3] % 2 == 0)
    def _():
        m[...] = mm_bt(m[...], at.following[...]).astype(LOW)

    @pl.when(ids[0] == 0)
    def _():
        out_spread[...] = mm_bt(m[...], at.pair[...]) + at.near[...]

    @pl.when(ids[0] == 1)
    def _():
        out_spread[...] = mm_bt(m[...], at.both[1]) + at.near[...]


def columns(ref, side, chunk, width):
    start = side * (ref.shape[1] // 2) + chunk * width
    return ref.at[:, pl.ds(pl.multiple_of(start, width), width)]


def start_kernel(chunk, ids, at, got, offset, now, keep, sem):
    copy = pltpu.make_async_copy(columns(offset, ids[0], chunk, keep.shape[1]), keep, sem)
    copy.start()
    p, own = getattr(at, f"p{chunk}"), getattr(at, f"own{chunk}")

    @pl.when(ids[0] == 0)
    def _():
        p[...] = mm(at.both[0], got[...])

    copy.wait()

    @pl.when(ids[0] == 0)
    def _():
        own[...] = (p[...] + keep[...]).astype(LOW)

    @pl.when(ids[0] == 1)
    def _():
        p[...] = mm(at.both[0], keep[...].astype(LOW))
        own[...] = (p[...] + got[...].astype(WIDE)).astype(LOW)

    now[...] = own[...]


def hop_kernel(chunk, ids, at, got, now):
    own, far = getattr(at, f"own{chunk}"), getattr(at, f"far{chunk}")
    now[...] = (mm(at.pair[...], got[...]) + own[...].astype(WIDE)).astype(LOW)
    if hasattr(at, f"far{chunk}_next"):
        getattr(at, f"far{chunk}_next")[...] = far[...] + got[...]
    else:
        far[...] = got[...]


def last_kernel(chunk, ids, at, got, offset, *refs):
    out, send, keep, far, sems = refs[-5:]
    p = getattr(at, f"p{chunk}")
    width = keep.shape[1]
    copy = pltpu.make_async_copy(columns(offset, ids[0], chunk, width), keep, sems.at[0])
    copy.start()
    far[...] = getattr(at, f"far{chunk}")[...] + got[...]

    @pl.when(ids[0] == 0)
    def _():
        send[...] = mm(at.both[1], far[...]).astype(LOW)

    @pl.when(ids[0] == 1)
    def _():
        send[...] = (mm(at.pair[...], far[...]) + p[...]).astype(LOW)

    copy.wait()

    @pl.when(ids[0] == 0)
    def _():
        keep[...] = mm(at.pair[...], far[...]) + p[...] + keep[...]

    @pl.when(ids[0] == 1)
    def _():
        keep[...] = mm(at.both[1], far[...]) + keep[...]

    copy = pltpu.make_async_copy(keep, columns(out, ids[0], chunk, width), sems.at[1])
    copy.start()
    copy.wait()


def add_kernel(chunk, ids, at, got, offset, into, out, keep, sems):
    width = keep.shape[1]
    copy = pltpu.make_async_copy(columns(offset, 1 - ids[0], chunk, width), keep, sems.at[0])
    copy.start()
    copy.wait()
    keep[...] = got[...].astype(WIDE) + keep[...]
    copy = pltpu.make_async_copy(keep, columns(out, 1 - ids[0], chunk, width), sems.at[1])
    copy.start()
    copy.wait()


def suffix(gains, spreads, offsets):
    x, y, c, z = (lax.axis_index(name) for name in ("x", "y", "c", "z"))
    gain = gains[0]
    rows, size_d = gain.shape
    part = rows // 2
    chunks = 2
    half = offsets.shape[2] // 2
    width = half // chunks
    ids = jnp.stack([x, y, c, z]).astype(jnp.int32)
    level = [(3, 2), (1, 0)]
    order = Order(ids)
    in_hbm = lambda a: pltpu.with_memory_space_constraint(a, pltpu.HBM)

    e_low = gain.astype(LOW)
    e_x, e_y = swap(e_low, "x"), swap(e_low, "y")

    l_low = spreads[0].astype(LOW)
    l_send = lax.dynamic_slice_in_dim(l_low, (1 - x) * part, part, 0)
    g_send = [
        lax.dynamic_slice_in_dim(offsets[0], (1 - x) * half + i * width, width, 1).astype(LOW) for i in range(chunks)
    ]
    l_send, g_send[0], e_x = lax.optimization_barrier((l_send, g_send[0], e_x))
    e_xy = swap(e_x, "y")
    l_got = swap(l_send, "x")
    g_got = [swap(g_send[0], "x")]
    for i in range(1, chunks):
        g_send[i], g_got[-1] = lax.optimization_barrier((g_send[i], g_got[-1]))
        g_got.append(swap(g_send[i], "x"))
    pieces = [e_low, None, e_y, None, e_x, None, e_xy, None]
    for i in range(0, 8, 2):
        pieces[i + 1] = swap(pieces[i], "c")
    offset, spread = in_hbm(offsets[0]), in_hbm(spreads)

    keep = pltpu.VMEM((size_d, width), WIDE)
    column = pltpu.VMEM((size_d, width), LOW)
    slab_rows = pltpu.VMEM((rows, size_d), LOW)

    def start(i):
        new = {f"p{i}": ((size_d, width), WIDE), f"own{i}": ((size_d, width), LOW)}
        return order.call(
            functools.partial(start_kernel, i), [g_got[i], offset], [low(size_d, width)], 10,
            new=new, far_in=(1,), scratch=[keep, pltpu.SemaphoreType.DMA(())],
        )[0]

    def down(value, source):
        return lax.ppermute(value, "z", [(source, source - 1)])

    def hop(i, got):
        known = f"far{i}" in order.state
        return order.call(
            functools.partial(hop_kernel, i), [got], [low(size_d, width)], 10,
            new={} if known else {f"far{i}": ((size_d, width), LOW)}, drop=(f"own{i}",) if known else (),
        )[0]

    def last(i, got, into):
        extra = [] if into is None else [into]
        return order.call(
            functools.partial(last_kernel, i), [got, offset] + extra,
            [wide(*offset.shape), low(size_d, width)], 12, drop=(f"p{i}", f"far{i}"),
            far_in=(1, 2), far_out=(0,), aliases={2: 0} if extra else {},
            scratch=[keep, column, pltpu.SemaphoreType.DMA((2,))],
        )

    def add(i, got, into):
        return order.call(
            functools.partial(add_kernel, i), [got, offset, into], [wide(*offset.shape)], 10,
            far_in=(1, 2), far_out=(0,), aliases={2: 0}, scratch=[keep, pltpu.SemaphoreType.DMA((2,))],
        )[0]

    square = (size_d, size_d)
    (quarter,) = order.call(
        pair_kernel, pieces, [low(rows, size_d)], 16,
        new={"both": ((2,) + square, LOW), "pair": (square, LOW)},
        far_in=range(8), scratch=[pltpu.SemaphoreType.DMA((8,))],
    )
    quarter = lax.ppermute(quarter, "z", level)
    quarter_y = swap(quarter, "y")
    quarters = [quarter, swap(quarter, "c"), quarter_y, swap(quarter_y, "c")]
    (m,) = order.call(spread_kernel, [l_low, l_got], [low(8, rows, part)], 12)
    m = exchange(m)
    got0 = down(start(0), 3)
    (a_low,) = order.call(
        spread_start_kernel, [m, spread, l_got], [low(size_d, part)], 14,
        new={"prod": ((rows, size_d), WIDE), "slab": ((size_d, part), WIDE)}, scratch=[slab_rows],
    )
    l_next = lax.ppermute(a_low, "z", level)
    got1 = down(start(1), 3)
    got0 = down(hop(0, got0), 2)

    m, near = order.call(spread_hop_kernel, [l_next], [low(size_d, part), low(8, rows, part)], 12)
    m = exchange(m.reshape(8, part, part))
    near = exchange(near)
    got1 = down(hop(1, got1), 2)
    (b_l,) = order.call(
        spread_next_kernel, [m], [low(size_d, part)], 10, drop=("slab",), scratch=[pltpu.VMEM((part, size_d), LOW)]
    )
    l_far = lax.ppermute(b_l, "z", [(2, 1)]), lax.ppermute(b_l, "z", [(2, 0)])
    (e_slab,) = order.call(
        next_gain_kernel, quarters, [low(size_d, part)], 10,
        new={"following": (square, LOW)}, far_in=range(4), scratch=[pltpu.SemaphoreType.DMA((4,))],
    )
    e_far = lax.ppermute(e_slab, "z", [(2, 1)]), lax.ppermute(e_slab, "z", [(2, 0)])
    got0 = down(hop(0, got0), 1)
    order.call(
        near_kernel, [near, spread], [], 12, new={"near": ((rows, size_d), WIDE)}, drop=("prod",), scratch=[slab_rows]
    )
    got1 = down(hop(1, got1), 1)

    out_offset, other0 = last(0, got0, None)
    other0 = swap(other0, "x")
    (m,) = order.call(
        far_kernel, [*e_far, *l_far], [low(8, rows, rows)], 12, scratch=[pltpu.VMEM((size_d, rows), LOW)]
    )
    m = exchange(m)
    out_offset, other1 = last(1, got1, out_offset)
    other1 = swap(other1, "x")
    out_offset = add(0, other0, out_offset)
    out_gain, out_spread = order.call(
        end_kernel, [m], [wide(rows, size_d), wide(rows, size_d)], 14,
        drop=("both", "pair", "following", "near"), scratch=[slab_rows],
    )
    out_offset = add(1, other1, out_offset)
    return (out_gain[None], out_spread[None], out_offset[None])


def solution(mesh):
    steps, rows = mesh.shape["tm"], mesh.shape["rows"]
    if steps == 2**LEVELS and rows == 4:
        devices = mesh.devices.reshape(steps // 2, 2, 2, 2)
        mesh = Mesh(devices, ("z", "x", "y", "c"))
        by_row, by_column = P(("z", "x"), ("y", "c"), None), P(("z", "x"), None, ("y", "c"))
        body = suffix
    else:
        by_row, by_column = P("tm", "rows", None), P("tm", None, "rows")
        body = doubling
    return jax.shard_map(
        body,
        mesh=mesh,
        in_specs=(by_row, by_row, by_column),
        out_specs=(by_row, by_row, by_column),
        check_vma=False,
    )
```

```python
import functools

import jax
import jax.numpy as jnp
from jax import lax
from jax.experimental import pallas as pl
from jax.experimental.pallas import tpu as pltpu
from jax.sharding import Mesh, PartitionSpec as P

LEVELS = 3
LOW = jnp.bfloat16
WIDE = jnp.float32
MIB = 2**20


def shifted(value, axis, steps):
    count = lax.axis_size(axis)
    first, last = (max(0, -steps), min(count, count - steps))
    return lax.ppermute(value, axis, [(source, source + steps) for source in range(first, last)])


def doubling(gains, spreads, offsets):
    gain = gains[0]
    spread = spreads[0]
    offset = offsets[0]
    size_d = gain.shape[1]
    identity = jnp.eye(size_d, dtype=LOW)
    for section_number in range(LEVELS):
        distance = 2**section_number
        beyond = lax.axis_index("tm") + distance >= lax.axis_size("tm")
        own_gain = gain.astype(LOW)
        own_spread = spread.astype(LOW)
        own_offset = offset.astype(LOW)
        own_full = lax.all_gather(own_gain, "rows", axis=0, tiled=True)
        spread_full = lax.all_gather(own_spread, "rows", axis=0, tiled=True)
        far_full, far_spread_full, far_offset = shifted((own_full, spread_full, own_offset), "tm", -distance)
        far_full = jnp.where(beyond, identity, far_full)
        row_start = lax.axis_index("rows") * gain.shape[0]
        own_rows = lax.dynamic_slice_in_dim(own_full, row_start, gain.shape[0], 0)
        middle = jnp.dot(own_rows, far_spread_full, preferred_element_type=WIDE).astype(LOW)
        new_gain = jnp.dot(own_rows, far_full, preferred_element_type=WIDE)
        new_spread = (
            lax.dot_general(middle, own_full, (((1,), (1,)), ((), ())), preferred_element_type=WIDE) + spread
        )
        new_offset = jnp.dot(own_full, far_offset, preferred_element_type=WIDE) + offset
        gain, spread, offset = (new_gain, new_spread, new_offset)
    return (gain[None], spread[None], offset[None])


def swap(value, axis):
    return lax.ppermute(value, axis, [(0, 1), (1, 0)])


def mm(a, b):
    return jnp.dot(a, b, preferred_element_type=WIDE)


def mm_bt(a, b):
    return lax.dot_general(a, b, (((1,), (1,)), ((), ())), preferred_element_type=WIDE)


GROUP = ("y", "c", "x")


def exchange(blocks):
    return lax.all_to_all(blocks, GROUP, 0, 0)


def hbm(*shape, dtype=LOW):
    return pltpu.HBM(shape, dtype)


def wide(*shape):
    return jax.ShapeDtypeStruct(shape, WIDE)


ANY = pl.BlockSpec(memory_space=pl.ANY)
VMEM = pl.BlockSpec(memory_space=pltpu.VMEM)
SMEM = pl.BlockSpec(memory_space=pltpu.SMEM)


class Order:
    def __init__(self, ids):
        self.ids = ids
        self.token = jnp.zeros((8, 128), jnp.int32)

    def call(self, kernel, operands, outs, mib, scratch=(), aliases={}, far_in=(), far_out=()):
        n, m = len(operands), len(outs)

        def body(ids, token, *refs):
            kernel(ids, *refs[: n + m], *refs[n + m + 1 :])

        results = pl.pallas_call(
            body,
            in_specs=[SMEM, ANY] + [ANY if i in far_in else VMEM for i in range(n)],
            out_specs=[ANY if i in far_out else VMEM for i in range(m)] + [ANY],
            out_shape=list(outs) + [jax.ShapeDtypeStruct(self.token.shape, jnp.int32)],
            scratch_shapes=list(scratch),
            input_output_aliases={1: m} | {2 + i: o for i, o in aliases.items()},
            cost_estimate=pl.CostEstimate(flops=1, bytes_accessed=1, transcendentals=0),
            compiler_params=pltpu.CompilerParams(vmem_limit_bytes=mib * MIB),
        )(self.ids, self.token, *operands)
        self.token = results[-1]
        return results[:-1]


def gather_lanes(blocks, into, start, width):
    for s in range(blocks.shape[0]):
        into[:, s * width : (s + 1) * width] = blocks[s, :, start : start + width]


def pair_kernel(ids, *refs):
    pieces, (e0, e1, pair, quarter, both, sems) = refs[:8], refs[8:]
    group = 2 * ids[1] + ids[2]
    me = 4 * ids[0] + group
    rows = pieces[0].shape[0]
    copies = []
    for i in range(8):
        place = me ^ i
        into = both.at[place >> 2, pl.ds(pl.multiple_of((place & 3) * rows, rows), rows), :]
        copies.append(pltpu.make_async_copy(pieces[i], into, sems.at[i]))
        copies[-1].start()
    for copy in copies:
        copy.wait()
    copies = [pltpu.make_async_copy(both.at[i], e, sems.at[i]) for i, e in enumerate((e0, e1))]
    for copy in copies:
        copy.start()
    for r in range(4):
        cut = slice(r * rows, (r + 1) * rows)
        pair[cut, :] = mm(both[0, cut, :], both[1]).astype(LOW)
    quarter[...] = pair[pl.ds(pl.multiple_of(group * rows, rows), rows), :]
    for copy in copies:
        copy.wait()


def spread_kernel(ids, e0, l_low, l_got, m_ref):
    part, rows = l_got.shape[0], l_low.shape[0]

    def product(slab):
        for r in range(4):
            m = mm_bt(e0[r * rows : (r + 1) * rows, :], slab).astype(LOW)
            m_ref[2 * r] = m
            m_ref[2 * r + 1] = m

    @pl.when(ids[0] == 0)
    def _():
        product(l_got[...])

    @pl.when(ids[0] == 1)
    def _():
        product(l_low[part:, :])


def spread_start_kernel(ids, e0, blocks, spread, l_got, prod, slab, a_low, m):
    part = l_got.shape[0]
    gather_lanes(blocks, m, 0, part)
    prod[...] = mm_bt(m[...], e0[...])

    @pl.when(ids[0] == 0)
    def _():
        slab[...] = (prod[:part, :] + spread[0, :part, :]).T

    @pl.when(ids[0] == 1)
    def _():
        slab[...] = (prod[part:, :] + l_got[...].astype(WIDE)).T

    a_low[...] = slab[...].astype(LOW)


def spread_hop_kernel(ids, pair, e1, got, m_ref, near):
    part = got.shape[1]
    rows = 2 * part
    m = mm(pair[...], got[...]).astype(LOW)
    m_ref[...] = m
    other = mm(e1[...], got[...]).astype(LOW)
    for r in range(4):
        near[2 * r] = m[r * rows : (r + 1) * rows, :]
        near[2 * r + 1] = other[r * rows : (r + 1) * rows, :]


def spread_next_kernel(ids, pair, slab, blocks, b_l, m):
    gather_lanes(blocks, m, 0, m.shape[0])
    b_l[...] = (mm_bt(pair[...], m[...]) + slab[...]).astype(LOW)


def near_kernel(ids, pair, e1, prod, blocks, spread, near, m):
    gather_lanes(blocks, m, 0, blocks.shape[2])

    @pl.when(ids[0] == 0)
    def _():
        near[...] = mm_bt(m[...], pair[...]) + prod[...] + spread[0]

    @pl.when(ids[0] == 1)
    def _():
        near[...] = mm_bt(m[...], e1[...]) + spread[0]


def next_gain_kernel(ids, pair, *refs):
    quarters, (following, slab_ref, sems) = refs[:4], refs[4:]
    part, rows = slab_ref.shape[1], quarters[0].shape[0]
    group = 2 * ids[1] + ids[2]
    copies = []
    for i in range(4):
        into = following.at[pl.ds(pl.multiple_of((group ^ i) * rows, rows), rows), :]
        copies.append(pltpu.make_async_copy(quarters[i], into, sems.at[i]))
        copies[-1].start()
    for copy in copies:
        copy.wait()
    slab = pl.ds(pl.multiple_of((2 * group + ids[0]) * part, part), part)
    slab_ref[...] = mm(pair[...], following[:, slab]).astype(LOW)


def far_kernel(ids, pair, e1, following, e_a, e_b, l_a, l_b, out, far):
    size, part = e_a.shape
    rows = 2 * part

    @pl.when(ids[3] < 2)
    def _():
        far[:, :part] = e_a[...] + e_b[...]

    @pl.when(ids[3] >= 2)
    def _():
        slab = (2 * ids[1] + ids[2]) * 2 + ids[0]
        column = lax.broadcasted_iota(jnp.int32, (size, part), 1) + slab * part
        row = lax.broadcasted_iota(jnp.int32, (size, part), 0)
        far[:, :part] = jnp.where(row == column, 1.0, 0.0).astype(LOW)

    far[:, part:] = l_a[...] + l_b[...]

    @pl.when(ids[3] % 2 == 0)
    def _():
        far[...] = mm(following[...], far[...]).astype(LOW)

    one = mm(pair[...], far[...]).astype(LOW)
    two = mm(e1[...], far[...]).astype(LOW)
    for r in range(4):
        out[2 * r] = one[r * rows : (r + 1) * rows, :]
        out[2 * r + 1] = two[r * rows : (r + 1) * rows, :]


def end_kernel(ids, pair, e1, following, near, blocks, out_gain, out_spread, m):
    part = blocks.shape[2] // 2
    gather_lanes(blocks, m, part, part)
    for s in range(blocks.shape[0]):
        out_gain[:, s * part : (s + 1) * part] = blocks[s, :, :part].astype(WIDE)

    @pl.when(ids[3] % 2 == 0)
    def _():
        m[...] = mm_bt(m[...], following[...]).astype(LOW)

    @pl.when(ids[0] == 0)
    def _():
        out_spread[...] = mm_bt(m[...], pair[...]) + near[...]

    @pl.when(ids[0] == 1)
    def _():
        out_spread[...] = mm_bt(m[...], e1[...]) + near[...]


def columns(ref, side, chunk, width):
    start = side * (ref.shape[1] // 2) + chunk * width
    return ref.at[:, pl.ds(pl.multiple_of(start, width), width)]


def start_kernel(chunk, ids, e0, got, offset, p, own, keep, sem):
    copy = pltpu.make_async_copy(columns(offset, ids[0], chunk, keep.shape[1]), keep, sem)
    copy.start()

    @pl.when(ids[0] == 0)
    def _():
        p[...] = mm(e0[...], got[...])

    copy.wait()

    @pl.when(ids[0] == 0)
    def _():
        own[...] = (p[...] + keep[...]).astype(LOW)

    @pl.when(ids[0] == 1)
    def _():
        p[...] = mm(e0[...], keep[...].astype(LOW))
        own[...] = (p[...] + got[...].astype(WIDE)).astype(LOW)


def hop_kernel(ids, pair, got, own, now):
    now[...] = (mm(pair[...], got[...]) + own[...].astype(WIDE)).astype(LOW)


def last_kernel(chunk, ids, pair, e1, p, got_a, got_b, got_c, offset, *refs):
    out, send, keep, far, sems = refs[-5:]
    width = keep.shape[1]
    copy = pltpu.make_async_copy(columns(offset, ids[0], chunk, width), keep, sems.at[0])
    copy.start()
    for z, got in ((2, got_a), (1, got_b), (0, got_c)):

        @pl.when(ids[3] == z)
        def _():
            load = pltpu.make_async_copy(got, far, sems.at[1])
            load.start()
            load.wait()

    @pl.when(ids[3] == 3)
    def _():
        far[...] = jnp.zeros_like(far)

    @pl.when(ids[0] == 0)
    def _():
        send[...] = mm(e1[...], far[...]).astype(LOW)

    @pl.when(ids[0] == 1)
    def _():
        send[...] = (mm(pair[...], far[...]) + p[...]).astype(LOW)

    copy.wait()

    @pl.when(ids[0] == 0)
    def _():
        keep[...] = mm(pair[...], far[...]) + p[...] + keep[...]

    @pl.when(ids[0] == 1)
    def _():
        keep[...] = mm(e1[...], far[...]) + keep[...]

    copy = pltpu.make_async_copy(keep, columns(out, ids[0], chunk, width), sems.at[1])
    copy.start()
    copy.wait()


def add_kernel(chunk, ids, got, offset, into, out, keep, sems):
    width = keep.shape[1]
    copy = pltpu.make_async_copy(columns(offset, 1 - ids[0], chunk, width), keep, sems.at[0])
    copy.start()
    copy.wait()
    keep[...] = got[...].astype(WIDE) + keep[...]
    copy = pltpu.make_async_copy(keep, columns(out, 1 - ids[0], chunk, width), sems.at[1])
    copy.start()
    copy.wait()


def suffix(gains, spreads, offsets):
    x, y, c, z = (lax.axis_index(name) for name in ("x", "y", "c", "z"))
    gain = gains[0]
    rows, size_d = gain.shape
    part = rows // 2
    chunks = 2
    half = offsets.shape[2] // 2
    width = half // chunks
    ids = jnp.stack([x, y, c, z]).astype(jnp.int32)
    level = [(3, 2), (1, 0)]
    order = Order(ids)
    in_hbm = lambda a: pltpu.with_memory_space_constraint(a, pltpu.HBM)

    e_low = gain.astype(LOW)
    e_x, e_y = swap(e_low, "x"), swap(e_low, "y")

    l_low = spreads[0].astype(LOW)
    l_send = lax.dynamic_slice_in_dim(l_low, (1 - x) * part, part, 0)
    g_send = [
        lax.dynamic_slice_in_dim(offsets[0], (1 - x) * half + i * width, width, 1).astype(LOW) for i in range(chunks)
    ]
    l_send, g_send[0], e_x = lax.optimization_barrier((l_send, g_send[0], e_x))
    e_xy = swap(e_x, "y")
    l_got = swap(l_send, "x")
    g_got = [swap(g_send[0], "x")]
    for i in range(1, chunks):
        g_send[i], g_got[-1] = lax.optimization_barrier((g_send[i], g_got[-1]))
        g_got.append(swap(g_send[i], "x"))
    pieces = [e_low, None, e_y, None, e_x, None, e_xy, None]
    for i in range(0, 8, 2):
        pieces[i + 1] = swap(pieces[i], "c")
    offset, spread = in_hbm(offsets[0]), in_hbm(spreads)

    keep = pltpu.VMEM((size_d, width), WIDE)
    column = pltpu.VMEM((size_d, width), LOW)
    slab_rows = pltpu.VMEM((rows, size_d), LOW)

    def start(i):
        return order.call(
            functools.partial(start_kernel, i), [in_hbm(e0), g_got[i], offset], [hbm(size_d, width, dtype=WIDE), hbm(size_d, width)],
            12, far_in=(2,), scratch=[keep, pltpu.SemaphoreType.DMA(())],
        )

    def down(value, source):
        return lax.ppermute(value, "z", [(source, source - 1)])

    def hop(got, own):
        return order.call(hop_kernel, [pair, got, in_hbm(own)], [hbm(size_d, width)], 8)[0]

    def last(i, p, gots, into):
        extra = [] if into is None else [into]
        return order.call(
            functools.partial(last_kernel, i), [pair, in_hbm(e1), in_hbm(p), *gots, offset] + extra,
            [wide(*offset.shape), hbm(size_d, width)], 14,
            far_in=(3, 4, 5, 6, 7), far_out=(0,), aliases={7: 0} if extra else {},
            scratch=[keep, column, pltpu.SemaphoreType.DMA((2,))],
        )

    def add(i, got, into):
        return order.call(
            functools.partial(add_kernel, i), [got, offset, into], [wide(*offset.shape)], 8,
            far_in=(1, 2), far_out=(0,), aliases={2: 0}, scratch=[keep, pltpu.SemaphoreType.DMA((2,))],
        )[0]

    e0, e1, pair, quarter = order.call(
        pair_kernel, pieces,
        [hbm(size_d, size_d), hbm(size_d, size_d), pltpu.VMEM((size_d, size_d), LOW), hbm(rows, size_d)], 14,
        far_in=range(8), far_out=(0, 1),
        scratch=[pltpu.VMEM((2, size_d, size_d), LOW), pltpu.SemaphoreType.DMA((8,))],
    )
    quarter = lax.ppermute(quarter, "z", level)
    quarter_y = swap(quarter, "y")
    quarters = [quarter, swap(quarter, "c"), quarter_y, swap(quarter_y, "c")]
    (m,) = order.call(spread_kernel, [in_hbm(e0), l_low, l_got], [hbm(8, rows, part)], 8)
    m = exchange(m)
    p0, own0 = start(0)
    gots0 = [down(own0, 3)]
    prod, slab, a_low = order.call(
        spread_start_kernel, [in_hbm(e0), m, spread, l_got],
        [hbm(rows, size_d, dtype=WIDE), hbm(size_d, part, dtype=WIDE), hbm(size_d, part)], 12, scratch=[slab_rows],
    )
    l_next = lax.ppermute(a_low, "z", level)
    p1, own1 = start(1)
    gots1 = [down(own1, 3)]
    gots0.append(down(hop(gots0[0], own0), 2))

    m, near = order.call(spread_hop_kernel, [pair, in_hbm(e1), l_next], [hbm(size_d, part), hbm(8, rows, part)], 10)
    m = exchange(m.reshape(8, part, part))
    near = exchange(near)
    gots1.append(down(hop(gots1[0], own1), 2))
    (b_l,) = order.call(
        spread_next_kernel, [pair, in_hbm(slab), m], [hbm(size_d, part)], 8, scratch=[pltpu.VMEM((part, size_d), LOW)]
    )
    l_far = lax.ppermute(b_l, "z", [(2, 1)]), lax.ppermute(b_l, "z", [(2, 0)])
    following, e_slab = order.call(
        next_gain_kernel, [pair, *quarters], [hbm(size_d, size_d), hbm(size_d, part)], 10,
        far_in=(1, 2, 3, 4), scratch=[pltpu.SemaphoreType.DMA((4,))],
    )
    e_far = lax.ppermute(e_slab, "z", [(2, 1)]), lax.ppermute(e_slab, "z", [(2, 0)])
    gots0.append(down(hop(gots0[1], own0), 1))
    (near,) = order.call(
        near_kernel, [pair, in_hbm(e1), in_hbm(prod), near, spread], [hbm(rows, size_d, dtype=WIDE)], 12, scratch=[slab_rows]
    )
    gots1.append(down(hop(gots1[1], own1), 1))

    out_offset, other0 = last(0, p0, gots0, None)
    other0 = swap(other0, "x")
    (m,) = order.call(
        far_kernel, [pair, in_hbm(e1), in_hbm(following), *e_far, *l_far], [hbm(8, rows, rows)], 14,
        scratch=[pltpu.VMEM((size_d, rows), LOW)],
    )
    m = exchange(m)
    out_offset, other1 = last(1, p1, gots1, out_offset)
    other1 = swap(other1, "x")
    out_offset = add(0, other0, out_offset)
    out_gain, out_spread = order.call(
        end_kernel, [pair, in_hbm(e1), in_hbm(following), in_hbm(near), m], [wide(rows, size_d), wide(rows, size_d)], 14, scratch=[slab_rows]
    )
    out_offset = add(1, other1, out_offset)
    return (out_gain[None], out_spread[None], out_offset[None])


def solution(mesh):
    steps, rows = mesh.shape["tm"], mesh.shape["rows"]
    if steps == 2**LEVELS and rows == 4:
        devices = mesh.devices.reshape(steps // 2, 2, 2, 2)
        mesh = Mesh(devices, ("z", "x", "y", "c"))
        by_row, by_column = P(("z", "x"), ("y", "c"), None), P(("z", "x"), None, ("y", "c"))
        body = suffix
    else:
        by_row, by_column = P("tm", "rows", None), P("tm", None, "rows")
        body = doubling
    return jax.shard_map(
        body,
        mesh=mesh,
        in_specs=(by_row, by_row, by_column),
        out_specs=(by_row, by_row, by_column),
        check_vma=False,
    )
```

```python
import functools

import jax
import jax.numpy as jnp
from jax import lax
from jax.experimental import pallas as pl
from jax.experimental.pallas import tpu as pltpu
from jax.sharding import Mesh, PartitionSpec as P

LEVELS = 3
LOW = jnp.bfloat16
WIDE = jnp.float32
MIB = 2**20


def shifted(value, axis, steps):
    count = lax.axis_size(axis)
    first, last = (max(0, -steps), min(count, count - steps))
    return lax.ppermute(value, axis, [(source, source + steps) for source in range(first, last)])


def doubling(gains, spreads, offsets):
    gain = gains[0]
    spread = spreads[0]
    offset = offsets[0]
    size_d = gain.shape[1]
    identity = jnp.eye(size_d, dtype=LOW)
    for section_number in range(LEVELS):
        distance = 2**section_number
        beyond = lax.axis_index("tm") + distance >= lax.axis_size("tm")
        own_gain = gain.astype(LOW)
        own_spread = spread.astype(LOW)
        own_offset = offset.astype(LOW)
        own_full = lax.all_gather(own_gain, "rows", axis=0, tiled=True)
        spread_full = lax.all_gather(own_spread, "rows", axis=0, tiled=True)
        far_full, far_spread_full, far_offset = shifted((own_full, spread_full, own_offset), "tm", -distance)
        far_full = jnp.where(beyond, identity, far_full)
        row_start = lax.axis_index("rows") * gain.shape[0]
        own_rows = lax.dynamic_slice_in_dim(own_full, row_start, gain.shape[0], 0)
        middle = jnp.dot(own_rows, far_spread_full, preferred_element_type=WIDE).astype(LOW)
        new_gain = jnp.dot(own_rows, far_full, preferred_element_type=WIDE)
        new_spread = (
            lax.dot_general(middle, own_full, (((1,), (1,)), ((), ())), preferred_element_type=WIDE) + spread
        )
        new_offset = jnp.dot(own_full, far_offset, preferred_element_type=WIDE) + offset
        gain, spread, offset = (new_gain, new_spread, new_offset)
    return (gain[None], spread[None], offset[None])


def swap(value, axis):
    return lax.ppermute(value, axis, [(0, 1), (1, 0)])


def mm(a, b):
    return jnp.dot(a, b, preferred_element_type=WIDE)


def mm_bt(a, b):
    return lax.dot_general(a, b, (((1,), (1,)), ((), ())), preferred_element_type=WIDE)


GROUP = ("y", "c", "x")


def exchange(blocks):
    return lax.all_to_all(blocks, GROUP, 0, 0)


def hbm(*shape, dtype=LOW):
    return pltpu.HBM(shape, dtype)


def wide(*shape):
    return jax.ShapeDtypeStruct(shape, WIDE)


ANY = pl.BlockSpec(memory_space=pl.ANY)
VMEM = pl.BlockSpec(memory_space=pltpu.VMEM)
SMEM = pl.BlockSpec(memory_space=pltpu.SMEM)


class Order:
    def __init__(self, ids):
        self.ids = ids
        self.token = jnp.zeros((8, 128), jnp.int32)

    def call(self, kernel, operands, outs, mib, scratch=(), aliases={}, far_in=(), far_out=()):
        n, m = len(operands), len(outs)

        def body(ids, token, *refs):
            kernel(ids, *refs[: n + m], *refs[n + m + 1 :])

        results = pl.pallas_call(
            body,
            in_specs=[SMEM, ANY] + [ANY if i in far_in else VMEM for i in range(n)],
            out_specs=[ANY if i in far_out else VMEM for i in range(m)] + [ANY],
            out_shape=list(outs) + [jax.ShapeDtypeStruct(self.token.shape, jnp.int32)],
            scratch_shapes=list(scratch),
            input_output_aliases={1: m} | {2 + i: o for i, o in aliases.items()},
            cost_estimate=pl.CostEstimate(flops=1, bytes_accessed=1, transcendentals=0),
            compiler_params=pltpu.CompilerParams(vmem_limit_bytes=mib * MIB),
        )(self.ids, self.token, *operands)
        self.token = results[-1]
        return results[:-1]


def gather_lanes(blocks, into, start, width):
    for s in range(blocks.shape[0]):
        into[:, s * width : (s + 1) * width] = blocks[s, :, start : start + width]


def pair_kernel(ids, three, last, three_c, last_c, e0, e1, pair, quarter, both, sems):
    group = 2 * ids[1] + ids[2]
    me = 4 * ids[0] + group
    rows = last.shape[0]
    pieces = []
    for flip, (some, other) in enumerate(((three, last), (three_c, last_c))):
        pieces += [(some.at[i * rows : (i + 1) * rows, :], at + flip) for i, at in enumerate((0, 4, 2))]
        pieces.append((other, 6 + flip))
    copies = []
    for i, (piece, at) in enumerate(pieces):
        place = me ^ at
        into = both.at[place >> 2, pl.ds(pl.multiple_of((place & 3) * rows, rows), rows), :]
        copies.append(pltpu.make_async_copy(piece, into, sems.at[i]))
        copies[-1].start()
    for copy in copies:
        copy.wait()
    copies = [pltpu.make_async_copy(both.at[i], e, sems.at[i]) for i, e in enumerate((e0, e1))]
    for copy in copies:
        copy.start()
    for r in range(4):
        cut = slice(r * rows, (r + 1) * rows)
        pair[cut, :] = mm(both[0, cut, :], both[1]).astype(LOW)
    quarter[...] = pair[pl.ds(pl.multiple_of(group * rows, rows), rows), :]
    for copy in copies:
        copy.wait()


def spread_kernel(ids, e0, l_low, l_got, m_ref):
    part, rows = l_got.shape[0], l_low.shape[0]

    def product(slab):
        for r in range(4):
            m = mm_bt(e0[r * rows : (r + 1) * rows, :], slab).astype(LOW)
            m_ref[2 * r] = m
            m_ref[2 * r + 1] = m

    @pl.when(ids[0] == 0)
    def _():
        product(l_got[...])

    @pl.when(ids[0] == 1)
    def _():
        product(l_low[part:, :])


def spread_start_kernel(ids, e0, blocks, spread, l_got, prod, slab, a_low, m):
    part = l_got.shape[0]
    gather_lanes(blocks, m, 0, part)
    prod[...] = mm_bt(m[...], e0[...])

    @pl.when(ids[0] == 0)
    def _():
        slab[...] = (prod[:part, :] + spread[0, :part, :]).T

    @pl.when(ids[0] == 1)
    def _():
        slab[...] = (prod[part:, :] + l_got[...].astype(WIDE)).T

    a_low[...] = slab[...].astype(LOW)


def spread_hop_kernel(ids, pair, e1, got, m_ref, near):
    part = got.shape[1]
    rows = 2 * part
    m = mm(pair[...], got[...]).astype(LOW)
    m_ref[...] = m
    other = mm(e1[...], got[...]).astype(LOW)
    for r in range(4):
        near[2 * r] = m[r * rows : (r + 1) * rows, :]
        near[2 * r + 1] = other[r * rows : (r + 1) * rows, :]


def next_kernel(ids, pair, slab, blocks, quarters, quarters_c, following, out, m, sems):
    part = m.shape[0]
    rows = 2 * part
    group = 2 * ids[1] + ids[2]
    copies = []
    for i, (piece, at) in enumerate(((quarters, 0), (quarters, 2), (quarters_c, 1), (quarters_c, 3))):
        into = following.at[pl.ds(pl.multiple_of((group ^ at) * rows, rows), rows), :]
        cut = piece.at[(at >> 1) * rows : ((at >> 1) + 1) * rows, :]
        copies.append(pltpu.make_async_copy(cut, into, sems.at[i]))
        copies[-1].start()
    gather_lanes(blocks, m, 0, part)
    out[:, part:] = (mm_bt(pair[...], m[...]) + slab[...]).astype(LOW)
    for copy in copies:
        copy.wait()
    columns_here = pl.ds(pl.multiple_of((2 * group + ids[0]) * part, part), part)
    out[:, :part] = mm(pair[...], following[:, columns_here]).astype(LOW)


def near_kernel(ids, pair, e1, prod, blocks, spread, near, m):
    gather_lanes(blocks, m, 0, blocks.shape[2])

    @pl.when(ids[0] == 0)
    def _():
        near[...] = mm_bt(m[...], pair[...]) + prod[...] + spread[0]

    @pl.when(ids[0] == 1)
    def _():
        near[...] = mm_bt(m[...], e1[...]) + spread[0]


def far_kernel(ids, pair, e1, following, f_a, f_b, out, far):
    size, rows = far.shape
    part = rows // 2
    far[...] = f_a[...] + f_b[...]

    @pl.when(ids[3] >= 2)
    def _():
        slab = (2 * ids[1] + ids[2]) * 2 + ids[0]
        column = lax.broadcasted_iota(jnp.int32, (size, part), 1) + slab * part
        row = lax.broadcasted_iota(jnp.int32, (size, part), 0)
        far[:, :part] = jnp.where(row == column, 1.0, 0.0).astype(LOW)

    @pl.when(ids[3] % 2 == 0)
    def _():
        far[...] = mm(following[...], far[...]).astype(LOW)

    one = mm(pair[...], far[...]).astype(LOW)
    two = mm(e1[...], far[...]).astype(LOW)
    for r in range(4):
        out[2 * r] = one[r * rows : (r + 1) * rows, :]
        out[2 * r + 1] = two[r * rows : (r + 1) * rows, :]


def end_kernel(ids, pair, e1, following, near, blocks, out_gain, out_spread, m):
    part = blocks.shape[2] // 2
    gather_lanes(blocks, m, part, part)
    for s in range(blocks.shape[0]):
        out_gain[:, s * part : (s + 1) * part] = blocks[s, :, :part].astype(WIDE)

    @pl.when(ids[3] % 2 == 0)
    def _():
        m[...] = mm_bt(m[...], following[...]).astype(LOW)

    @pl.when(ids[0] == 0)
    def _():
        out_spread[...] = mm_bt(m[...], pair[...]) + near[...]

    @pl.when(ids[0] == 1)
    def _():
        out_spread[...] = mm_bt(m[...], e1[...]) + near[...]


def columns(ref, side, chunk, width):
    start = side * (ref.shape[1] // 2) + chunk * width
    return ref.at[:, pl.ds(pl.multiple_of(start, width), width)]


def start_kernel(chunk, ids, e0, got, offset, p, own, keep, sem):
    copy = pltpu.make_async_copy(columns(offset, ids[0], chunk, keep.shape[1]), keep, sem)
    copy.start()

    @pl.when(ids[0] == 0)
    def _():
        p[...] = mm(e0[...], got[...])

    copy.wait()

    @pl.when(ids[0] == 0)
    def _():
        own[...] = (p[...] + keep[...]).astype(LOW)

    @pl.when(ids[0] == 1)
    def _():
        p[...] = mm(e0[...], keep[...].astype(LOW))
        own[...] = (p[...] + got[...].astype(WIDE)).astype(LOW)


def hop_kernel(ids, pair, got, own, now):
    now[...] = (mm(pair[...], got[...]) + own[...].astype(WIDE)).astype(LOW)


def last_kernel(chunk, ids, pair, later, p_far, got_a, got_b, got_c, offset, *refs):
    out, send, keep, far, e1, p, sems = refs[-7:]
    width = keep.shape[1]
    for z, got in ((2, got_a), (1, got_b), (0, got_c)):

        @pl.when(ids[3] == z)
        def _():
            pltpu.make_async_copy(got, far, sems.at[0]).start()

    load_e1 = pltpu.make_async_copy(later, e1, sems.at[1])
    load_e1.start()
    load_p = pltpu.make_async_copy(p_far, p, sems.at[2])
    load_p.start()
    load_keep = pltpu.make_async_copy(columns(offset, ids[0], chunk, width), keep, sems.at[3])
    load_keep.start()

    @pl.when(ids[3] == 3)
    def _():
        far[...] = jnp.zeros_like(far)

    @pl.when(ids[3] != 3)
    def _():
        pltpu.make_async_copy(got_a, far, sems.at[0]).wait()

    first = mm(pair[...], far[...])
    load_p.wait()
    p[...] = first + p[...]
    load_keep.wait()
    load_e1.wait()

    @pl.when(ids[0] == 0)
    def _():
        keep[...] = p[...] + keep[...]

    @pl.when(ids[0] == 1)
    def _():
        keep[...] = mm(e1[...], far[...]) + keep[...]

    store = pltpu.make_async_copy(keep, columns(out, ids[0], chunk, width), sems.at[4])
    store.start()

    @pl.when(ids[0] == 0)
    def _():
        send[...] = mm(e1[...], far[...]).astype(LOW)

    @pl.when(ids[0] == 1)
    def _():
        send[...] = p[...].astype(LOW)

    store.wait()


def add_kernel(chunk, ids, got, offset, into, out, keep, sems):
    width = keep.shape[1]
    copy = pltpu.make_async_copy(columns(offset, 1 - ids[0], chunk, width), keep, sems.at[0])
    copy.start()
    copy.wait()
    keep[...] = got[...].astype(WIDE) + keep[...]
    copy = pltpu.make_async_copy(keep, columns(out, 1 - ids[0], chunk, width), sems.at[1])
    copy.start()
    copy.wait()


def suffix(gains, spreads, offsets):
    x, y, c, z = (lax.axis_index(name) for name in ("x", "y", "c", "z"))
    gain = gains[0]
    rows, size_d = gain.shape
    part = rows // 2
    chunks = 2
    half = offsets.shape[2] // 2
    width = half // chunks
    ids = jnp.stack([x, y, c, z]).astype(jnp.int32)
    level = [(3, 2), (1, 0)]
    order = Order(ids)
    in_hbm = lambda a: pltpu.with_memory_space_constraint(a, pltpu.HBM)

    e_low = gain.astype(LOW)
    e_x, e_y = swap(e_low, "x"), swap(e_low, "y")

    l_low = spreads[0].astype(LOW)
    l_send = lax.dynamic_slice_in_dim(l_low, (1 - x) * part, part, 0)
    g_send = [
        lax.dynamic_slice_in_dim(offsets[0], (1 - x) * half + i * width, width, 1).astype(LOW) for i in range(chunks)
    ]
    l_send, g_send[0], e_x = lax.optimization_barrier((l_send, g_send[0], e_x))
    e_xy = swap(e_x, "y")
    l_got = swap(l_send, "x")
    g_got = [swap(g_send[0], "x")]
    for i in range(1, chunks):
        g_send[i], g_got[-1] = lax.optimization_barrier((g_send[i], g_got[-1]))
        g_got.append(swap(g_send[i], "x"))
    three = jnp.concatenate([e_low, e_x, e_y], axis=0)
    pieces = [in_hbm(a) for a in (three, e_xy, swap(three, "c"), swap(e_xy, "c"))]
    offset, spread = in_hbm(offsets[0]), in_hbm(spreads)

    keep = pltpu.VMEM((size_d, width), WIDE)
    column = pltpu.VMEM((size_d, width), LOW)
    slab_rows = pltpu.VMEM((rows, size_d), LOW)

    def start(i):
        return order.call(
            functools.partial(start_kernel, i), [in_hbm(e0), g_got[i], offset], [hbm(size_d, width, dtype=WIDE), hbm(size_d, width)],
            12, far_in=(2,), scratch=[keep, pltpu.SemaphoreType.DMA(())],
        )

    def down(value, source):
        return lax.ppermute(value, "z", [(source, source - 1)])

    def hop(got, own):
        return order.call(hop_kernel, [pair, got, in_hbm(own)], [hbm(size_d, width)], 8)[0]

    def last(i, p, gots, into):
        extra = [] if into is None else [into]
        return order.call(
            functools.partial(last_kernel, i), [pair, in_hbm(e1), in_hbm(p), *gots, offset] + extra,
            [wide(*offset.shape), hbm(size_d, width)], 14,
            far_in=(1, 2, 3, 4, 5, 6, 7), far_out=(0,), aliases={7: 0} if extra else {},
            scratch=[keep, column, pltpu.VMEM((size_d, size_d), LOW), keep, pltpu.SemaphoreType.DMA((5,))],
        )

    def add(i, got, into):
        return order.call(
            functools.partial(add_kernel, i), [got, offset, into], [wide(*offset.shape)], 8,
            far_in=(1, 2), far_out=(0,), aliases={2: 0}, scratch=[keep, pltpu.SemaphoreType.DMA((2,))],
        )[0]

    e0, e1, pair, quarter = order.call(
        pair_kernel, pieces,
        [hbm(size_d, size_d), hbm(size_d, size_d), pltpu.VMEM((size_d, size_d), LOW), hbm(rows, size_d)], 14,
        far_in=range(4), far_out=(0, 1),
        scratch=[pltpu.VMEM((2, size_d, size_d), LOW), pltpu.SemaphoreType.DMA((8,))],
    )
    quarter = lax.ppermute(quarter, "z", level)
    quarter_y = swap(quarter, "y")
    quarters = jnp.concatenate([quarter, quarter_y], axis=0)
    quarters = [quarters, swap(quarters, "c")]
    (m,) = order.call(spread_kernel, [in_hbm(e0), l_low, l_got], [hbm(8, rows, part)], 8)
    m = exchange(m)
    p0, own0 = start(0)
    gots0 = [down(own0, 3)]
    p1, own1 = start(1)
    gots1 = [down(own1, 3)]
    prod, slab, a_low = order.call(
        spread_start_kernel, [in_hbm(e0), m, spread, l_got],
        [hbm(rows, size_d, dtype=WIDE), hbm(size_d, part, dtype=WIDE), hbm(size_d, part)], 12, scratch=[slab_rows],
    )
    l_next = lax.ppermute(a_low, "z", level)
    gots0.append(down(hop(gots0[0], own0), 2))

    m, near = order.call(spread_hop_kernel, [pair, in_hbm(e1), l_next], [hbm(size_d, part), hbm(8, rows, part)], 10)
    m = exchange(m.reshape(8, part, part))
    near = exchange(near)
    gots1.append(down(hop(gots1[0], own1), 2))
    gots0.append(down(hop(gots0[1], own0), 1))
    following, far_slab = order.call(
        next_kernel, [pair, in_hbm(slab), m, *quarters], [hbm(size_d, size_d), hbm(size_d, rows)], 12,
        far_in=(3, 4), scratch=[pltpu.VMEM((part, size_d), LOW), pltpu.SemaphoreType.DMA((4,))],
    )
    far = lax.ppermute(far_slab, "z", [(2, 1)]), lax.ppermute(far_slab, "z", [(2, 0)])
    (near,) = order.call(
        near_kernel, [pair, in_hbm(e1), in_hbm(prod), near, spread], [hbm(rows, size_d, dtype=WIDE)], 12,
        scratch=[slab_rows],
    )
    gots1.append(down(hop(gots1[1], own1), 1))

    out_offset, other0 = last(0, p0, gots0, None)
    other0 = swap(other0, "x")
    (m,) = order.call(
        far_kernel, [pair, in_hbm(e1), in_hbm(following), *far], [hbm(8, rows, rows)], 14,
        scratch=[pltpu.VMEM((size_d, rows), LOW)],
    )
    m = exchange(m)
    out_offset, other1 = last(1, p1, gots1, out_offset)
    other1 = swap(other1, "x")
    out_offset = add(0, other0, out_offset)
    out_gain, out_spread = order.call(
        end_kernel, [pair, in_hbm(e1), in_hbm(following), in_hbm(near), m], [wide(rows, size_d), wide(rows, size_d)], 14, scratch=[slab_rows]
    )
    out_offset = add(1, other1, out_offset)
    return (out_gain[None], out_spread[None], out_offset[None])


def solution(mesh):
    steps, rows = mesh.shape["tm"], mesh.shape["rows"]
    if steps == 2**LEVELS and rows == 4:
        devices = mesh.devices.reshape(steps // 2, 2, 2, 2)
        mesh = Mesh(devices, ("z", "x", "y", "c"))
        by_row, by_column = P(("z", "x"), ("y", "c"), None), P(("z", "x"), None, ("y", "c"))
        body = suffix
    else:
        by_row, by_column = P("tm", "rows", None), P("tm", None, "rows")
        body = doubling
    return jax.shard_map(
        body,
        mesh=mesh,
        in_specs=(by_row, by_row, by_column),
        out_specs=(by_row, by_row, by_column),
        check_vma=False,
    )
```

```python
import functools

import jax
import jax.numpy as jnp
from jax import lax
from jax.experimental import pallas as pl
from jax.experimental.pallas import tpu as pltpu
from jax.sharding import Mesh, PartitionSpec as P

LEVELS = 3
LOW = jnp.bfloat16
WIDE = jnp.float32
MIB = 2**20


def shifted(value, axis, steps):
    count = lax.axis_size(axis)
    first, last = (max(0, -steps), min(count, count - steps))
    return lax.ppermute(value, axis, [(source, source + steps) for source in range(first, last)])


def doubling(gains, spreads, offsets):
    gain = gains[0]
    spread = spreads[0]
    offset = offsets[0]
    size_d = gain.shape[1]
    identity = jnp.eye(size_d, dtype=LOW)
    for section_number in range(LEVELS):
        distance = 2**section_number
        beyond = lax.axis_index("tm") + distance >= lax.axis_size("tm")
        own_gain = gain.astype(LOW)
        own_spread = spread.astype(LOW)
        own_offset = offset.astype(LOW)
        own_full = lax.all_gather(own_gain, "rows", axis=0, tiled=True)
        spread_full = lax.all_gather(own_spread, "rows", axis=0, tiled=True)
        far_full, far_spread_full, far_offset = shifted((own_full, spread_full, own_offset), "tm", -distance)
        far_full = jnp.where(beyond, identity, far_full)
        row_start = lax.axis_index("rows") * gain.shape[0]
        own_rows = lax.dynamic_slice_in_dim(own_full, row_start, gain.shape[0], 0)
        middle = jnp.dot(own_rows, far_spread_full, preferred_element_type=WIDE).astype(LOW)
        new_gain = jnp.dot(own_rows, far_full, preferred_element_type=WIDE)
        new_spread = (
            lax.dot_general(middle, own_full, (((1,), (1,)), ((), ())), preferred_element_type=WIDE) + spread
        )
        new_offset = jnp.dot(own_full, far_offset, preferred_element_type=WIDE) + offset
        gain, spread, offset = (new_gain, new_spread, new_offset)
    return (gain[None], spread[None], offset[None])


def swap(value, axis):
    return lax.ppermute(value, axis, [(0, 1), (1, 0)])


def mm(a, b):
    return jnp.dot(a, b, preferred_element_type=WIDE)


def mm_bt(a, b):
    return lax.dot_general(a, b, (((1,), (1,)), ((), ())), preferred_element_type=WIDE)


GROUP = ("y", "c", "x")


def exchange(blocks):
    return lax.all_to_all(blocks, GROUP, 0, 0)


def hbm(*shape, dtype=LOW):
    return pltpu.HBM(shape, dtype)


def wide(*shape):
    return jax.ShapeDtypeStruct(shape, WIDE)


ANY = pl.BlockSpec(memory_space=pl.ANY)
VMEM = pl.BlockSpec(memory_space=pltpu.VMEM)
SMEM = pl.BlockSpec(memory_space=pltpu.SMEM)


class Order:
    def __init__(self, ids):
        self.ids = ids
        self.token = jnp.zeros((8, 128), jnp.int32)

    def call(self, kernel, operands, outs, mib, scratch=(), aliases={}, far_in=(), far_out=()):
        n, m = len(operands), len(outs)

        def body(ids, token, *refs):
            kernel(ids, *refs[: n + m], *refs[n + m + 1 :])

        results = pl.pallas_call(
            body,
            in_specs=[SMEM, ANY] + [ANY if i in far_in else VMEM for i in range(n)],
            out_specs=[ANY if i in far_out else VMEM for i in range(m)] + [ANY],
            out_shape=list(outs) + [jax.ShapeDtypeStruct(self.token.shape, jnp.int32)],
            scratch_shapes=list(scratch),
            input_output_aliases={1: m} | {2 + i: o for i, o in aliases.items()},
            cost_estimate=pl.CostEstimate(flops=1, bytes_accessed=1, transcendentals=0),
            compiler_params=pltpu.CompilerParams(vmem_limit_bytes=mib * MIB),
        )(self.ids, self.token, *operands)
        self.token = results[-1]
        return results[:-1]


def gather_lanes(blocks, into, start, width):
    for s in range(blocks.shape[0]):
        into[:, s * width : (s + 1) * width] = blocks[s, :, start : start + width]


def pair_kernel(ids, three, last, three_c, last_c, e0, e1, pair, quarter, both, sems):
    group = 2 * ids[1] + ids[2]
    me = 4 * ids[0] + group
    rows = last.shape[0]
    pieces = []
    for flip, (some, other) in enumerate(((three, last), (three_c, last_c))):
        pieces += [(some.at[i * rows : (i + 1) * rows, :], at + flip) for i, at in enumerate((0, 4, 2))]
        pieces.append((other, 6 + flip))
    copies = []
    for i, (piece, at) in enumerate(pieces):
        place = me ^ at
        into = both.at[place >> 2, pl.ds(pl.multiple_of((place & 3) * rows, rows), rows), :]
        copies.append(pltpu.make_async_copy(piece, into, sems.at[i]))
        copies[-1].start()
    for copy in copies:
        copy.wait()
    copies = [pltpu.make_async_copy(both.at[i], e, sems.at[i]) for i, e in enumerate((e0, e1))]
    for copy in copies:
        copy.start()
    for r in range(4):
        cut = slice(r * rows, (r + 1) * rows)
        pair[cut, :] = mm(both[0, cut, :], both[1]).astype(LOW)
    quarter[...] = pair[pl.ds(pl.multiple_of(group * rows, rows), rows), :]
    for copy in copies:
        copy.wait()


def spread_kernel(ids, e0, l_low, l_got, m_ref):
    part, rows = l_got.shape[0], l_low.shape[0]

    def product(slab):
        for r in range(4):
            m = mm_bt(e0[r * rows : (r + 1) * rows, :], slab).astype(LOW)
            m_ref[2 * r] = m
            m_ref[2 * r + 1] = m

    @pl.when(ids[0] == 0)
    def _():
        product(l_got[...])

    @pl.when(ids[0] == 1)
    def _():
        product(l_low[part:, :])


def spread_start_kernel(ids, e0, blocks, spread, l_got, unused, prod, slab, a_low, m):
    part = l_got.shape[0]
    gather_lanes(blocks, m, 0, part)
    prod[...] = mm_bt(m[...], e0[...])

    @pl.when(ids[0] == 0)
    def _():
        slab[...] = (prod[:part, :] + spread[0, :part, :]).T

    @pl.when(ids[0] == 1)
    def _():
        slab[...] = (prod[part:, :] + l_got[...].astype(WIDE)).T

    a_low[...] = slab[...].astype(LOW)


def spread_hop_kernel(ids, pair, e1, got, m_ref, near):
    part = got.shape[1]
    rows = 2 * part
    m = mm(pair[...], got[...]).astype(LOW)
    m_ref[...] = m
    other = mm(e1[...], got[...]).astype(LOW)
    for r in range(4):
        near[2 * r] = m[r * rows : (r + 1) * rows, :]
        near[2 * r + 1] = other[r * rows : (r + 1) * rows, :]


def next_kernel(ids, pair, slab, blocks, quarters, quarters_c, following, out, m, sems):
    part = m.shape[0]
    rows = 2 * part
    group = 2 * ids[1] + ids[2]
    copies = []
    for i, (piece, at) in enumerate(((quarters, 0), (quarters, 2), (quarters_c, 1), (quarters_c, 3))):
        into = following.at[pl.ds(pl.multiple_of((group ^ at) * rows, rows), rows), :]
        cut = piece.at[(at >> 1) * rows : ((at >> 1) + 1) * rows, :]
        copies.append(pltpu.make_async_copy(cut, into, sems.at[i]))
        copies[-1].start()
    gather_lanes(blocks, m, 0, part)
    out[:, part:] = (mm_bt(pair[...], m[...]) + slab[...]).astype(LOW)
    for copy in copies:
        copy.wait()
    columns_here = pl.ds(pl.multiple_of((2 * group + ids[0]) * part, part), part)
    out[:, :part] = mm(pair[...], following[:, columns_here]).astype(LOW)


def near_kernel(ids, pair, e1, prod, blocks, spread, near, m):
    gather_lanes(blocks, m, 0, blocks.shape[2])

    @pl.when(ids[0] == 0)
    def _():
        near[...] = mm_bt(m[...], pair[...]) + prod[...] + spread[0]

    @pl.when(ids[0] == 1)
    def _():
        near[...] = mm_bt(m[...], e1[...]) + spread[0]


def far_kernel(ids, pair, e1, following, f_a, f_b, out, far):
    size, rows = far.shape
    part = rows // 2
    far[...] = f_a[...] + f_b[...]

    @pl.when(ids[3] >= 2)
    def _():
        slab = (2 * ids[1] + ids[2]) * 2 + ids[0]
        column = lax.broadcasted_iota(jnp.int32, (size, part), 1) + slab * part
        row = lax.broadcasted_iota(jnp.int32, (size, part), 0)
        far[:, :part] = jnp.where(row == column, 1.0, 0.0).astype(LOW)

    @pl.when(ids[3] % 2 == 0)
    def _():
        far[...] = mm(following[...], far[...]).astype(LOW)

    one = mm(pair[...], far[...]).astype(LOW)
    two = mm(e1[...], far[...]).astype(LOW)
    for r in range(4):
        out[2 * r] = one[r * rows : (r + 1) * rows, :]
        out[2 * r + 1] = two[r * rows : (r + 1) * rows, :]


def end_kernel(ids, pair, e1, following, near, blocks, out_gain, out_spread, m):
    part = blocks.shape[2] // 2
    gather_lanes(blocks, m, part, part)
    for s in range(blocks.shape[0]):
        out_gain[:, s * part : (s + 1) * part] = blocks[s, :, :part].astype(WIDE)

    @pl.when(ids[3] % 2 == 0)
    def _():
        m[...] = mm_bt(m[...], following[...]).astype(LOW)

    @pl.when(ids[0] == 0)
    def _():
        out_spread[...] = mm_bt(m[...], pair[...]) + near[...]

    @pl.when(ids[0] == 1)
    def _():
        out_spread[...] = mm_bt(m[...], e1[...]) + near[...]


def columns(ref, side, chunk, width):
    start = side * (ref.shape[1] // 2) + chunk * width
    return ref.at[:, pl.ds(pl.multiple_of(start, width), width)]


def start_kernel(chunk, ids, e0, got, offset, p, own, keep, sem):
    copy = pltpu.make_async_copy(columns(offset, ids[0], chunk, keep.shape[1]), keep, sem)
    copy.start()

    @pl.when(ids[0] == 0)
    def _():
        p[...] = mm(e0[...], got[...])

    copy.wait()

    @pl.when(ids[0] == 0)
    def _():
        own[...] = (p[...] + keep[...]).astype(LOW)

    @pl.when(ids[0] == 1)
    def _():
        p[...] = mm(e0[...], keep[...].astype(LOW))
        own[...] = (p[...] + got[...].astype(WIDE)).astype(LOW)


def hop_kernel(ids, pair, got, own, now):
    now[...] = (mm(pair[...], got[...]) + own[...].astype(WIDE)).astype(LOW)


def last_kernel(chunk, ids, pair, later, p_far, got_a, got_b, got_c, offset, *refs):
    out, send, keep, far, e1, p, sems = refs[-7:]
    width = keep.shape[1]
    for z, got in ((2, got_a), (1, got_b), (0, got_c)):

        @pl.when(ids[3] == z)
        def _():
            pltpu.make_async_copy(got, far, sems.at[0]).start()

    load_e1 = pltpu.make_async_copy(later, e1, sems.at[1])
    load_e1.start()
    load_p = pltpu.make_async_copy(p_far, p, sems.at[2])
    load_p.start()
    load_keep = pltpu.make_async_copy(columns(offset, ids[0], chunk, width), keep, sems.at[3])
    load_keep.start()

    @pl.when(ids[3] == 3)
    def _():
        far[...] = jnp.zeros_like(far)

    @pl.when(ids[3] != 3)
    def _():
        pltpu.make_async_copy(got_a, far, sems.at[0]).wait()

    first = mm(pair[...], far[...])
    load_p.wait()
    p[...] = first + p[...]
    load_keep.wait()
    load_e1.wait()

    @pl.when(ids[0] == 0)
    def _():
        keep[...] = p[...] + keep[...]

    @pl.when(ids[0] == 1)
    def _():
        keep[...] = mm(e1[...], far[...]) + keep[...]

    store = pltpu.make_async_copy(keep, columns(out, ids[0], chunk, width), sems.at[4])
    store.start()

    @pl.when(ids[0] == 0)
    def _():
        send[...] = mm(e1[...], far[...]).astype(LOW)

    @pl.when(ids[0] == 1)
    def _():
        send[...] = p[...].astype(LOW)

    store.wait()


def add_kernel(chunk, ids, got, offset, into, out, keep, sems):
    width = keep.shape[1]
    copy = pltpu.make_async_copy(columns(offset, 1 - ids[0], chunk, width), keep, sems.at[0])
    copy.start()
    copy.wait()
    keep[...] = got[...].astype(WIDE) + keep[...]
    copy = pltpu.make_async_copy(keep, columns(out, 1 - ids[0], chunk, width), sems.at[1])
    copy.start()
    copy.wait()


def suffix(gains, spreads, offsets):
    x, y, c, z = (lax.axis_index(name) for name in ("x", "y", "c", "z"))
    gain = gains[0]
    rows, size_d = gain.shape
    part = rows // 2
    chunks = 2
    half = offsets.shape[2] // 2
    width = half // chunks
    ids = jnp.stack([x, y, c, z]).astype(jnp.int32)
    level = [(3, 2), (1, 0)]
    order = Order(ids)
    in_hbm = lambda a: pltpu.with_memory_space_constraint(a, pltpu.HBM)

    e_low = gain.astype(LOW)
    e_x, e_y = swap(e_low, "x"), swap(e_low, "y")

    l_low = spreads[0].astype(LOW)
    l_send = lax.dynamic_slice_in_dim(l_low, (1 - x) * part, part, 0)
    g_send = [
        lax.dynamic_slice_in_dim(offsets[0], (1 - x) * half + i * width, width, 1).astype(LOW) for i in range(chunks)
    ]
    tied = lax.optimization_barrier
    l_got = swap(l_send, "x")
    l_got, e_x = tied((l_got, e_x))
    g_send[0], e_x = tied((g_send[0], e_x))
    e_xy = swap(e_x, "y")
    g_got = [swap(g_send[0], "x")]
    g_got[0], e_xy = tied((g_got[0], e_xy))
    g_send[1], g_got[0] = tied((g_send[1], g_got[0]))
    g_got.append(swap(g_send[1], "x"))
    three = jnp.concatenate([e_low, e_x, e_y], axis=0)
    pieces = [in_hbm(a) for a in (three, e_xy, swap(three, "c"), swap(e_xy, "c"))]
    offset, spread = in_hbm(offsets[0]), in_hbm(spreads)

    keep = pltpu.VMEM((size_d, width), WIDE)
    column = pltpu.VMEM((size_d, width), LOW)
    slab_rows = pltpu.VMEM((rows, size_d), LOW)

    def start(i):
        return order.call(
            functools.partial(start_kernel, i), [in_hbm(e0), g_got[i], offset], [hbm(size_d, width, dtype=WIDE), hbm(size_d, width)],
            12, far_in=(2,), scratch=[keep, pltpu.SemaphoreType.DMA(())],
        )

    def down(value, source):
        return lax.ppermute(value, "z", [(source, source - 1)])

    def hop(got, own):
        return order.call(hop_kernel, [pair, got, in_hbm(own)], [hbm(size_d, width)], 8)[0]

    def last(i, p, gots, into):
        extra = [] if into is None else [into]
        return order.call(
            functools.partial(last_kernel, i), [pair, in_hbm(e1), in_hbm(p), *gots, offset] + extra,
            [wide(*offset.shape), hbm(size_d, width)], 14,
            far_in=(1, 2, 3, 4, 5, 6, 7), far_out=(0,), aliases={7: 0} if extra else {},
            scratch=[keep, column, pltpu.VMEM((size_d, size_d), LOW), keep, pltpu.SemaphoreType.DMA((5,))],
        )

    def add(i, got, into):
        return order.call(
            functools.partial(add_kernel, i), [got, offset, into], [wide(*offset.shape)], 8,
            far_in=(1, 2), far_out=(0,), aliases={2: 0}, scratch=[keep, pltpu.SemaphoreType.DMA((2,))],
        )[0]

    e0, e1, pair, quarter = order.call(
        pair_kernel, pieces,
        [hbm(size_d, size_d), hbm(size_d, size_d), pltpu.VMEM((size_d, size_d), LOW), hbm(rows, size_d)], 14,
        far_in=range(4), far_out=(0, 1),
        scratch=[pltpu.VMEM((2, size_d, size_d), LOW), pltpu.SemaphoreType.DMA((8,))],
    )
    quarter = lax.ppermute(quarter, "z", level)
    (m,) = order.call(spread_kernel, [in_hbm(e0), l_low, l_got], [hbm(8, rows, part)], 8)
    m = exchange(m)
    p0, own0 = start(0)
    gots0 = [down(own0, 3)]
    quarter, own0 = tied((quarter, own0))
    quarter_y = swap(quarter, "y")
    prod, slab, a_low = order.call(
        spread_start_kernel, [in_hbm(e0), m, spread, l_got, g_got[1]],
        [hbm(rows, size_d, dtype=WIDE), hbm(size_d, part, dtype=WIDE), hbm(size_d, part)], 12,
        far_in=(4,), scratch=[slab_rows],
    )
    l_next = lax.ppermute(a_low, "z", level)
    p1, own1 = start(1)
    gots1 = [down(own1, 3)]

    m, near = order.call(spread_hop_kernel, [pair, in_hbm(e1), l_next], [hbm(size_d, part), hbm(8, rows, part)], 10)
    m = exchange(m.reshape(8, part, part))
    now0 = hop(gots0[0], own0)
    gots0.append(down(now0, 2))
    quarter_y, now0 = tied((quarter_y, now0))
    quarters = jnp.concatenate([quarter, quarter_y], axis=0)
    quarters = [quarters, swap(quarters, "c")]
    following, far_slab = order.call(
        next_kernel, [pair, in_hbm(slab), m, *quarters], [hbm(size_d, size_d), hbm(size_d, rows)], 12,
        far_in=(3, 4), scratch=[pltpu.VMEM((part, size_d), LOW), pltpu.SemaphoreType.DMA((4,))],
    )
    far = lax.ppermute(far_slab, "z", [(2, 1)]), lax.ppermute(far_slab, "z", [(2, 0)])
    now1 = hop(gots1[0], own1)
    gots1.append(down(now1, 2))
    near, now1 = tied((near, now1))
    near = exchange(near)
    gots0.append(down(hop(gots0[1], own0), 1))
    (near,) = order.call(
        near_kernel, [pair, in_hbm(e1), in_hbm(prod), near, spread], [hbm(rows, size_d, dtype=WIDE)], 12,
        scratch=[slab_rows],
    )
    gots1.append(down(hop(gots1[1], own1), 1))

    out_offset, other0 = last(0, p0, gots0, None)
    other0 = swap(other0, "x")
    (m,) = order.call(
        far_kernel, [pair, in_hbm(e1), in_hbm(following), *far], [hbm(8, rows, rows)], 14,
        scratch=[pltpu.VMEM((size_d, rows), LOW)],
    )
    m = exchange(m)
    out_offset, other1 = last(1, p1, gots1, out_offset)
    other1 = swap(other1, "x")
    out_offset = add(0, other0, out_offset)
    out_gain, out_spread = order.call(
        end_kernel, [pair, in_hbm(e1), in_hbm(following), in_hbm(near), m], [wide(rows, size_d), wide(rows, size_d)], 14, scratch=[slab_rows]
    )
    out_offset = add(1, other1, out_offset)
    return (out_gain[None], out_spread[None], out_offset[None])


def solution(mesh):
    steps, rows = mesh.shape["tm"], mesh.shape["rows"]
    if steps == 2**LEVELS and rows == 4:
        devices = mesh.devices.reshape(steps // 2, 2, 2, 2)
        mesh = Mesh(devices, ("z", "x", "y", "c"))
        by_row, by_column = P(("z", "x"), ("y", "c"), None), P(("z", "x"), None, ("y", "c"))
        body = suffix
    else:
        by_row, by_column = P("tm", "rows", None), P("tm", None, "rows")
        body = doubling
    return jax.shard_map(
        body,
        mesh=mesh,
        in_specs=(by_row, by_row, by_column),
        out_specs=(by_row, by_row, by_column),
        check_vma=False,
    )
```

```python
import functools

import jax
import jax.numpy as jnp
from jax import lax
from jax.experimental import pallas as pl
from jax.experimental.pallas import tpu as pltpu
from jax.sharding import Mesh, PartitionSpec as P

LEVELS = 3
LOW = jnp.bfloat16
WIDE = jnp.float32
MIB = 2**20


def shifted(value, axis, steps):
    count = lax.axis_size(axis)
    first, last = (max(0, -steps), min(count, count - steps))
    return lax.ppermute(value, axis, [(source, source + steps) for source in range(first, last)])


def doubling(gains, spreads, offsets):
    gain = gains[0]
    spread = spreads[0]
    offset = offsets[0]
    size_d = gain.shape[1]
    identity = jnp.eye(size_d, dtype=LOW)
    for section_number in range(LEVELS):
        distance = 2**section_number
        beyond = lax.axis_index("tm") + distance >= lax.axis_size("tm")
        own_gain = gain.astype(LOW)
        own_spread = spread.astype(LOW)
        own_offset = offset.astype(LOW)
        own_full = lax.all_gather(own_gain, "rows", axis=0, tiled=True)
        spread_full = lax.all_gather(own_spread, "rows", axis=0, tiled=True)
        far_full, far_spread_full, far_offset = shifted((own_full, spread_full, own_offset), "tm", -distance)
        far_full = jnp.where(beyond, identity, far_full)
        row_start = lax.axis_index("rows") * gain.shape[0]
        own_rows = lax.dynamic_slice_in_dim(own_full, row_start, gain.shape[0], 0)
        middle = jnp.dot(own_rows, far_spread_full, preferred_element_type=WIDE).astype(LOW)
        new_gain = jnp.dot(own_rows, far_full, preferred_element_type=WIDE)
        new_spread = (
            lax.dot_general(middle, own_full, (((1,), (1,)), ((), ())), preferred_element_type=WIDE) + spread
        )
        new_offset = jnp.dot(own_full, far_offset, preferred_element_type=WIDE) + offset
        gain, spread, offset = (new_gain, new_spread, new_offset)
    return (gain[None], spread[None], offset[None])


def swap(value, axis):
    return lax.ppermute(value, axis, [(0, 1), (1, 0)])


def mm(a, b):
    return jnp.dot(a, b, preferred_element_type=WIDE)


def mm_bt(a, b):
    return lax.dot_general(a, b, (((1,), (1,)), ((), ())), preferred_element_type=WIDE)


GROUP = ("y", "c", "x")


def exchange(blocks):
    return lax.all_to_all(blocks, GROUP, 0, 0)


def hbm(*shape, dtype=LOW):
    return pltpu.HBM(shape, dtype)


def wide(*shape):
    return jax.ShapeDtypeStruct(shape, WIDE)


ANY = pl.BlockSpec(memory_space=pl.ANY)
VMEM = pl.BlockSpec(memory_space=pltpu.VMEM)
SMEM = pl.BlockSpec(memory_space=pltpu.SMEM)


class Order:
    def __init__(self, ids):
        self.ids = ids
        self.token = jnp.zeros((8, 128), jnp.int32)

    def call(self, kernel, operands, outs, mib, scratch=(), aliases={}, far_in=(), far_out=()):
        n, m = len(operands), len(outs)

        def body(ids, token, *refs):
            kernel(ids, *refs[: n + m], *refs[n + m + 1 :])

        results = pl.pallas_call(
            body,
            in_specs=[SMEM, ANY] + [ANY if i in far_in else VMEM for i in range(n)],
            out_specs=[ANY if i in far_out else VMEM for i in range(m)] + [ANY],
            out_shape=list(outs) + [jax.ShapeDtypeStruct(self.token.shape, jnp.int32)],
            scratch_shapes=list(scratch),
            input_output_aliases={1: m} | {2 + i: o for i, o in aliases.items()},
            cost_estimate=pl.CostEstimate(flops=1, bytes_accessed=1, transcendentals=0),
            compiler_params=pltpu.CompilerParams(vmem_limit_bytes=mib * MIB),
        )(self.ids, self.token, *operands)
        self.token = results[-1]
        return results[:-1]


def gather_lanes(blocks, into, start, width):
    for s in range(blocks.shape[0]):
        into[:, s * width : (s + 1) * width] = blocks[s, :, start : start + width]


def pair_kernel(ids, three, last, three_c, last_c, e0, e1, pair, quarter, both, sems):
    group = 2 * ids[1] + ids[2]
    me = 4 * ids[0] + group
    rows = last.shape[0]
    pieces = []
    for flip, (some, other) in enumerate(((three, last), (three_c, last_c))):
        pieces += [(some.at[i * rows : (i + 1) * rows, :], at + flip) for i, at in enumerate((0, 4, 2))]
        pieces.append((other, 6 + flip))
    copies = []
    for i, (piece, at) in enumerate(pieces):
        place = me ^ at
        into = both.at[place >> 2, pl.ds(pl.multiple_of((place & 3) * rows, rows), rows), :]
        copies.append(pltpu.make_async_copy(piece, into, sems.at[i]))
        copies[-1].start()
    for copy in copies:
        copy.wait()
    copies = [pltpu.make_async_copy(both.at[i], e, sems.at[i]) for i, e in enumerate((e0, e1))]
    for copy in copies:
        copy.start()
    for r in range(4):
        cut = slice(r * rows, (r + 1) * rows)
        pair[cut, :] = mm(both[0, cut, :], both[1]).astype(LOW)
    quarter[...] = pair[pl.ds(pl.multiple_of(group * rows, rows), rows), :]
    for copy in copies:
        copy.wait()


def spread_kernel(ids, e0, l_low, l_got, m_ref):
    part, rows = l_got.shape[0], l_low.shape[0]

    def product(slab):
        for r in range(4):
            m = mm_bt(e0[r * rows : (r + 1) * rows, :], slab).astype(LOW)
            m_ref[2 * r] = m
            m_ref[2 * r + 1] = m

    @pl.when(ids[0] == 0)
    def _():
        product(l_got[...])

    @pl.when(ids[0] == 1)
    def _():
        product(l_low[part:, :])


def spread_start_kernel(ids, e0, blocks, spread, l_got, unused, prod, slab, a_low, m):
    part = l_got.shape[0]
    gather_lanes(blocks, m, 0, part)
    prod[...] = mm_bt(m[...], e0[...])

    @pl.when(ids[0] == 0)
    def _():
        slab[...] = (prod[:part, :] + spread[0, :part, :]).T

    @pl.when(ids[0] == 1)
    def _():
        slab[...] = (prod[part:, :] + l_got[...].astype(WIDE)).T

    a_low[...] = slab[...].astype(LOW)


def spread_hop_kernel(ids, pair, e1, got, m_ref, near):
    part = got.shape[1]
    rows = 2 * part
    m = mm(pair[...], got[...]).astype(LOW)
    m_ref[...] = m
    other = mm(e1[...], got[...]).astype(LOW)
    for r in range(4):
        near[2 * r] = m[r * rows : (r + 1) * rows, :]
        near[2 * r + 1] = other[r * rows : (r + 1) * rows, :]


def next_kernel(ids, pair, slab, blocks, quarters, quarters_c, following, out, m, sems):
    part = m.shape[0]
    rows = 2 * part
    group = 2 * ids[1] + ids[2]
    copies = []
    for i, (piece, at) in enumerate(((quarters, 0), (quarters, 2), (quarters_c, 1), (quarters_c, 3))):
        into = following.at[pl.ds(pl.multiple_of((group ^ at) * rows, rows), rows), :]
        cut = piece.at[(at >> 1) * rows : ((at >> 1) + 1) * rows, :]
        copies.append(pltpu.make_async_copy(cut, into, sems.at[i]))
        copies[-1].start()
    gather_lanes(blocks, m, 0, part)
    out[:, part:] = (mm_bt(pair[...], m[...]) + slab[...]).astype(LOW)
    for copy in copies:
        copy.wait()
    columns_here = pl.ds(pl.multiple_of((2 * group + ids[0]) * part, part), part)
    out[:, :part] = mm(pair[...], following[:, columns_here]).astype(LOW)


def far_kernel(ids, pair, e1, following, f_a, f_b, unused, out, far):
    size, rows = far.shape
    part = rows // 2
    far[...] = f_a[...] + f_b[...]

    @pl.when(ids[3] >= 2)
    def _():
        slab = (2 * ids[1] + ids[2]) * 2 + ids[0]
        column = lax.broadcasted_iota(jnp.int32, (size, part), 1) + slab * part
        row = lax.broadcasted_iota(jnp.int32, (size, part), 0)
        far[:, :part] = jnp.where(row == column, 1.0, 0.0).astype(LOW)

    @pl.when(ids[3] % 2 == 0)
    def _():
        far[...] = mm(following[...], far[...]).astype(LOW)

    one = mm(pair[...], far[...]).astype(LOW)
    two = mm(e1[...], far[...]).astype(LOW)
    for r in range(4):
        out[2 * r] = one[r * rows : (r + 1) * rows, :]
        out[2 * r + 1] = two[r * rows : (r + 1) * rows, :]


def end_kernel(ids, pair, e1, following, near, prod, spread, blocks, out_gain, out_spread, m, m_near):
    part = blocks.shape[2] // 2
    gather_lanes(near, m_near, 0, part)
    gather_lanes(blocks, m, part, part)
    for s in range(blocks.shape[0]):
        out_gain[:, s * part : (s + 1) * part] = blocks[s, :, :part].astype(WIDE)

    @pl.when(ids[3] % 2 == 0)
    def _():
        m[...] = mm_bt(m[...], following[...]).astype(LOW)

    @pl.when(ids[0] == 0)
    def _():
        total = mm_bt(m_near[...], pair[...]) + prod[...] + spread[0]
        out_spread[...] = mm_bt(m[...], pair[...]) + total

    @pl.when(ids[0] == 1)
    def _():
        total = mm_bt(m_near[...], e1[...]) + spread[0]
        out_spread[...] = mm_bt(m[...], e1[...]) + total


def columns(ref, side, chunk, width):
    start = side * (ref.shape[1] // 2) + chunk * width
    return ref.at[:, pl.ds(pl.multiple_of(start, width), width)]


def start_kernel(chunk, ids, e0, got, offset, p, own, keep, sem):
    copy = pltpu.make_async_copy(columns(offset, ids[0], chunk, keep.shape[1]), keep, sem)
    copy.start()

    @pl.when(ids[0] == 0)
    def _():
        p[...] = mm(e0[...], got[...])

    copy.wait()

    @pl.when(ids[0] == 0)
    def _():
        own[...] = (p[...] + keep[...]).astype(LOW)

    @pl.when(ids[0] == 1)
    def _():
        p[...] = mm(e0[...], keep[...].astype(LOW))
        own[...] = (p[...] + got[...].astype(WIDE)).astype(LOW)


def hop_kernel(ids, pair, got, own, now):
    now[...] = (mm(pair[...], got[...]) + own[...].astype(WIDE)).astype(LOW)


def hop_start_kernel(chunk, ids, pair, got_hop, own_hop, e0, got, offset, unused, now, p, own, keep, sem):
    hop_kernel(ids, pair, got_hop, own_hop, now)
    start_kernel(chunk, ids, e0, got, offset, p, own, keep, sem)


def hops_kernel(ids, pair, got_a, own_a, got_b, own_b, now_a, now_b):
    hop_kernel(ids, pair, got_a, own_a, now_a)
    hop_kernel(ids, pair, got_b, own_b, now_b)


def last_kernel(chunk, ids, pair, later, p_far, got_a, got_b, got_c, offset, *refs):
    out, send, keep, far, e1, p, sems = refs[-7:]
    width = keep.shape[1]
    for z, got in ((2, got_a), (1, got_b), (0, got_c)):

        @pl.when(ids[3] == z)
        def _():
            pltpu.make_async_copy(got, far, sems.at[0]).start()

    load_e1 = pltpu.make_async_copy(later, e1, sems.at[1])
    load_e1.start()
    load_p = pltpu.make_async_copy(p_far, p, sems.at[2])
    load_p.start()
    load_keep = pltpu.make_async_copy(columns(offset, ids[0], chunk, width), keep, sems.at[3])
    load_keep.start()

    @pl.when(ids[3] == 3)
    def _():
        far[...] = jnp.zeros_like(far)

    @pl.when(ids[3] != 3)
    def _():
        pltpu.make_async_copy(got_a, far, sems.at[0]).wait()

    first = mm(pair[...], far[...])
    load_p.wait()
    p[...] = first + p[...]
    load_keep.wait()
    load_e1.wait()

    @pl.when(ids[0] == 0)
    def _():
        keep[...] = p[...] + keep[...]

    @pl.when(ids[0] == 1)
    def _():
        keep[...] = mm(e1[...], far[...]) + keep[...]

    store = pltpu.make_async_copy(keep, columns(out, ids[0], chunk, width), sems.at[4])
    store.start()

    @pl.when(ids[0] == 0)
    def _():
        send[...] = mm(e1[...], far[...]).astype(LOW)

    @pl.when(ids[0] == 1)
    def _():
        send[...] = p[...].astype(LOW)

    store.wait()


def add_kernel(chunk, ids, got, offset, into, out, keep, sems):
    width = keep.shape[1]
    copy = pltpu.make_async_copy(columns(offset, 1 - ids[0], chunk, width), keep, sems.at[0])
    copy.start()
    copy.wait()
    keep[...] = got[...].astype(WIDE) + keep[...]
    copy = pltpu.make_async_copy(keep, columns(out, 1 - ids[0], chunk, width), sems.at[1])
    copy.start()
    copy.wait()


def suffix(gains, spreads, offsets):
    x, y, c, z = (lax.axis_index(name) for name in ("x", "y", "c", "z"))
    gain = gains[0]
    rows, size_d = gain.shape
    part = rows // 2
    chunks = 2
    half = offsets.shape[2] // 2
    width = half // chunks
    ids = jnp.stack([x, y, c, z]).astype(jnp.int32)
    level = [(3, 2), (1, 0)]
    order = Order(ids)
    in_hbm = lambda a: pltpu.with_memory_space_constraint(a, pltpu.HBM)

    e_low = gain.astype(LOW)
    e_x, e_y = swap(e_low, "x"), swap(e_low, "y")

    l_low = spreads[0].astype(LOW)
    l_send = lax.dynamic_slice_in_dim(l_low, (1 - x) * part, part, 0)
    g_send = [
        lax.dynamic_slice_in_dim(offsets[0], (1 - x) * half + i * width, width, 1).astype(LOW) for i in range(chunks)
    ]
    tied = lax.optimization_barrier
    l_got = swap(l_send, "x")
    l_got, e_x = tied((l_got, e_x))
    g_send[0], e_x = tied((g_send[0], e_x))
    e_xy = swap(e_x, "y")
    g_got = [swap(g_send[0], "x")]
    g_got[0], e_xy = tied((g_got[0], e_xy))
    g_send[1], g_got[0] = tied((g_send[1], g_got[0]))
    g_got.append(swap(g_send[1], "x"))
    three = jnp.concatenate([e_low, e_x, e_y], axis=0)
    pieces = [in_hbm(a) for a in (three, e_xy, swap(three, "c"), swap(e_xy, "c"))]
    offset, spread = in_hbm(offsets[0]), in_hbm(spreads)

    keep = pltpu.VMEM((size_d, width), WIDE)
    column = pltpu.VMEM((size_d, width), LOW)
    slab_rows = pltpu.VMEM((rows, size_d), LOW)

    def start(i):
        return order.call(
            functools.partial(start_kernel, i), [in_hbm(e0), g_got[i], offset], [hbm(size_d, width, dtype=WIDE), hbm(size_d, width)],
            12, far_in=(2,), scratch=[keep, pltpu.SemaphoreType.DMA(())],
        )

    def down(value, source):
        return lax.ppermute(value, "z", [(source, source - 1)])

    def hop(got, own):
        return order.call(hop_kernel, [pair, got, in_hbm(own)], [hbm(size_d, width)], 8)[0]

    def last(i, p, gots, into):
        extra = [] if into is None else [into]
        return order.call(
            functools.partial(last_kernel, i), [pair, in_hbm(e1), in_hbm(p), *gots, offset] + extra,
            [wide(*offset.shape), hbm(size_d, width)], 14,
            far_in=(1, 2, 3, 4, 5, 6, 7), far_out=(0,), aliases={7: 0} if extra else {},
            scratch=[keep, column, pltpu.VMEM((size_d, size_d), LOW), keep, pltpu.SemaphoreType.DMA((5,))],
        )

    def add(i, got, into):
        return order.call(
            functools.partial(add_kernel, i), [got, offset, into], [wide(*offset.shape)], 8,
            far_in=(1, 2), far_out=(0,), aliases={2: 0}, scratch=[keep, pltpu.SemaphoreType.DMA((2,))],
        )[0]

    e0, e1, pair, quarter = order.call(
        pair_kernel, pieces,
        [hbm(size_d, size_d), hbm(size_d, size_d), pltpu.VMEM((size_d, size_d), LOW), hbm(rows, size_d)], 14,
        far_in=range(4), far_out=(0, 1),
        scratch=[pltpu.VMEM((2, size_d, size_d), LOW), pltpu.SemaphoreType.DMA((8,))],
    )
    quarter = lax.ppermute(quarter, "z", level)
    (m,) = order.call(spread_kernel, [in_hbm(e0), l_low, l_got], [hbm(8, rows, part)], 8)
    m = exchange(m)
    p0, own0 = start(0)
    gots0 = [down(own0, 3)]
    quarter, own0 = tied((quarter, own0))
    quarter_y = swap(quarter, "y")
    prod, slab, a_low = order.call(
        spread_start_kernel, [in_hbm(e0), m, spread, l_got, g_got[1]],
        [hbm(rows, size_d, dtype=WIDE), hbm(size_d, part, dtype=WIDE), hbm(size_d, part)], 12,
        far_in=(4,), scratch=[slab_rows],
    )
    l_next = lax.ppermute(a_low, "z", level)
    now0, p1, own1 = order.call(
        functools.partial(hop_start_kernel, 1), [pair, gots0[0], in_hbm(own0), in_hbm(e0), g_got[1], offset, quarter_y],
        [hbm(size_d, width), hbm(size_d, width, dtype=WIDE), hbm(size_d, width)], 16,
        far_in=(5, 6), scratch=[keep, pltpu.SemaphoreType.DMA(())],
    )
    gots0.append(down(now0, 2))
    gots1 = [down(own1, 3)]
    m, near = order.call(spread_hop_kernel, [pair, in_hbm(e1), l_next], [hbm(size_d, part), hbm(8, rows, part)], 10)
    near, quarter_y = tied((near, quarter_y))
    m = exchange(m.reshape(8, part, part))
    quarters = jnp.concatenate([quarter, quarter_y], axis=0)
    quarters = [quarters, swap(quarters, "c")]
    now0, now1 = order.call(
        hops_kernel, [pair, gots0[1], in_hbm(own0), gots1[0], in_hbm(own1)], [hbm(size_d, width)] * 2, 10
    )
    gots0.append(down(now0, 1))
    gots1.append(down(now1, 2))
    following, far_slab = order.call(
        next_kernel, [pair, in_hbm(slab), m, *quarters], [hbm(size_d, size_d), hbm(size_d, rows)], 12,
        far_in=(3, 4), scratch=[pltpu.VMEM((part, size_d), LOW), pltpu.SemaphoreType.DMA((4,))],
    )
    far = lax.ppermute(far_slab, "z", [(2, 1)]), lax.ppermute(far_slab, "z", [(2, 0)])
    near, far_slab = tied((near, far_slab))
    near = exchange(near)

    out_offset, other0 = last(0, p0, gots0, None)
    other0 = swap(other0, "x")
    gots1.append(down(hop(gots1[1], own1), 1))
    (m,) = order.call(
        far_kernel, [pair, in_hbm(e1), in_hbm(following), *far, near], [hbm(8, rows, rows)], 14,
        far_in=(5,), scratch=[pltpu.VMEM((size_d, rows), LOW)],
    )
    m = exchange(m)
    out_offset = add(0, other0, out_offset)
    out_offset, other1 = last(1, p1, gots1, out_offset)
    other1 = swap(other1, "x")
    out_gain, out_spread = order.call(
        end_kernel, [pair, in_hbm(e1), in_hbm(following), near, in_hbm(prod), spread, m],
        [wide(rows, size_d), wide(rows, size_d)], 18, scratch=[slab_rows, slab_rows],
    )
    out_offset = add(1, other1, out_offset)
    return (out_gain[None], out_spread[None], out_offset[None])


def solution(mesh):
    steps, rows = mesh.shape["tm"], mesh.shape["rows"]
    if steps == 2**LEVELS and rows == 4:
        devices = mesh.devices.reshape(steps // 2, 2, 2, 2)
        mesh = Mesh(devices, ("z", "x", "y", "c"))
        by_row, by_column = P(("z", "x"), ("y", "c"), None), P(("z", "x"), None, ("y", "c"))
        body = suffix
    else:
        by_row, by_column = P("tm", "rows", None), P("tm", None, "rows")
        body = doubling
    return jax.shard_map(
        body,
        mesh=mesh,
        in_specs=(by_row, by_row, by_column),
        out_specs=(by_row, by_row, by_column),
        check_vma=False,
    )
```

```python
import functools

import jax
import jax.numpy as jnp
from jax import lax
from jax.experimental import pallas as pl
from jax.experimental.pallas import tpu as pltpu
from jax.sharding import Mesh, PartitionSpec as P

LEVELS = 3
LOW = jnp.bfloat16
WIDE = jnp.float32
MIB = 2**20


def shifted(value, axis, steps):
    count = lax.axis_size(axis)
    first, last = (max(0, -steps), min(count, count - steps))
    return lax.ppermute(value, axis, [(source, source + steps) for source in range(first, last)])


def doubling(gains, spreads, offsets):
    gain = gains[0]
    spread = spreads[0]
    offset = offsets[0]
    size_d = gain.shape[1]
    identity = jnp.eye(size_d, dtype=LOW)
    for section_number in range(LEVELS):
        distance = 2**section_number
        beyond = lax.axis_index("tm") + distance >= lax.axis_size("tm")
        own_gain = gain.astype(LOW)
        own_spread = spread.astype(LOW)
        own_offset = offset.astype(LOW)
        own_full = lax.all_gather(own_gain, "rows", axis=0, tiled=True)
        spread_full = lax.all_gather(own_spread, "rows", axis=0, tiled=True)
        far_full, far_spread_full, far_offset = shifted((own_full, spread_full, own_offset), "tm", -distance)
        far_full = jnp.where(beyond, identity, far_full)
        row_start = lax.axis_index("rows") * gain.shape[0]
        own_rows = lax.dynamic_slice_in_dim(own_full, row_start, gain.shape[0], 0)
        middle = jnp.dot(own_rows, far_spread_full, preferred_element_type=WIDE).astype(LOW)
        new_gain = jnp.dot(own_rows, far_full, preferred_element_type=WIDE)
        new_spread = (
            lax.dot_general(middle, own_full, (((1,), (1,)), ((), ())), preferred_element_type=WIDE) + spread
        )
        new_offset = jnp.dot(own_full, far_offset, preferred_element_type=WIDE) + offset
        gain, spread, offset = (new_gain, new_spread, new_offset)
    return (gain[None], spread[None], offset[None])


def swap(value, axis):
    return lax.ppermute(value, axis, [(0, 1), (1, 0)])


def mm(a, b):
    return jnp.dot(a, b, preferred_element_type=WIDE)


def mm_bt(a, b):
    return lax.dot_general(a, b, (((1,), (1,)), ((), ())), preferred_element_type=WIDE)


GROUP = ("y", "c", "x")


def exchange(blocks):
    return lax.all_to_all(blocks, GROUP, 0, 0)


def hbm(*shape, dtype=LOW):
    return pltpu.HBM(shape, dtype)


def wide(*shape):
    return jax.ShapeDtypeStruct(shape, WIDE)


ANY = pl.BlockSpec(memory_space=pl.ANY)
VMEM = pl.BlockSpec(memory_space=pltpu.VMEM)
SMEM = pl.BlockSpec(memory_space=pltpu.SMEM)


class Order:
    def __init__(self, ids):
        self.ids = ids
        self.token = jnp.zeros((8, 128), jnp.int32)

    def call(self, kernel, operands, outs, mib, scratch=(), aliases={}, far_in=(), far_out=()):
        n, m = len(operands), len(outs)

        def body(ids, token, *refs):
            kernel(ids, *refs[: n + m], *refs[n + m + 1 :])

        results = pl.pallas_call(
            body,
            in_specs=[SMEM, ANY] + [ANY if i in far_in else VMEM for i in range(n)],
            out_specs=[ANY if i in far_out else VMEM for i in range(m)] + [ANY],
            out_shape=list(outs) + [jax.ShapeDtypeStruct(self.token.shape, jnp.int32)],
            scratch_shapes=list(scratch),
            input_output_aliases={1: m} | {2 + i: o for i, o in aliases.items()},
            cost_estimate=pl.CostEstimate(flops=1, bytes_accessed=1, transcendentals=0),
            compiler_params=pltpu.CompilerParams(vmem_limit_bytes=mib * MIB),
        )(self.ids, self.token, *operands)
        self.token = results[-1]
        return results[:-1]


def gather_lanes(blocks, into, start, width):
    for s in range(blocks.shape[0]):
        into[:, s * width : (s + 1) * width] = blocks[s, :, start : start + width]


def pair_kernel(ids, three, last, three_c, last_c, e0, e1, pair, quarter, both, sems):
    group = 2 * ids[1] + ids[2]
    me = 4 * ids[0] + group
    rows = last.shape[0]
    pieces = []
    for flip, (some, other) in enumerate(((three, last), (three_c, last_c))):
        pieces += [(some.at[i * rows : (i + 1) * rows, :], at + flip) for i, at in enumerate((0, 4, 2))]
        pieces.append((other, 6 + flip))
    copies = []
    for i, (piece, at) in enumerate(pieces):
        place = me ^ at
        into = both.at[place >> 2, pl.ds(pl.multiple_of((place & 3) * rows, rows), rows), :]
        copies.append(pltpu.make_async_copy(piece, into, sems.at[i]))
        copies[-1].start()
    for copy in copies:
        copy.wait()
    copies = [pltpu.make_async_copy(both.at[i], e, sems.at[i]) for i, e in enumerate((e0, e1))]
    for copy in copies:
        copy.start()
    for r in range(4):
        cut = slice(r * rows, (r + 1) * rows)
        pair[cut, :] = mm(both[0, cut, :], both[1]).astype(LOW)
    quarter[...] = pair[pl.ds(pl.multiple_of(group * rows, rows), rows), :]
    for copy in copies:
        copy.wait()


def spread_kernel(ids, e0, l_low, l_got, unused, m_ref):
    part, rows = l_got.shape[0], l_low.shape[0]

    def product(slab):
        for r in range(4):
            m = mm_bt(e0[r * rows : (r + 1) * rows, :], slab).astype(LOW)
            m_ref[2 * r] = m
            m_ref[2 * r + 1] = m

    @pl.when(ids[0] == 0)
    def _():
        product(l_got[...])

    @pl.when(ids[0] == 1)
    def _():
        product(l_low[part:, :])


def spread_start_kernel(ids, e0, blocks, spread, l_got, unused, prod, slab, a_low, m):
    part = l_got.shape[0]
    gather_lanes(blocks, m, 0, part)
    prod[...] = mm_bt(m[...], e0[...])

    @pl.when(ids[0] == 0)
    def _():
        slab[...] = (prod[:part, :] + spread[0, :part, :]).T

    @pl.when(ids[0] == 1)
    def _():
        slab[...] = (prod[part:, :] + l_got[...].astype(WIDE)).T

    a_low[...] = slab[...].astype(LOW)


def spread_hop_kernel(ids, pair, e1, got, unused, m_ref, near):
    part = got.shape[1]
    rows = 2 * part
    m = mm(pair[...], got[...]).astype(LOW)
    m_ref[...] = m
    other = mm(e1[...], got[...]).astype(LOW)
    for r in range(4):
        near[2 * r] = m[r * rows : (r + 1) * rows, :]
        near[2 * r + 1] = other[r * rows : (r + 1) * rows, :]


def next_kernel(ids, pair, slab, blocks, quarters, quarters_c, following, out, m, sems):
    part = m.shape[0]
    rows = 2 * part
    group = 2 * ids[1] + ids[2]
    copies = []
    for i, (piece, at) in enumerate(((quarters, 0), (quarters, 2), (quarters_c, 1), (quarters_c, 3))):
        into = following.at[pl.ds(pl.multiple_of((group ^ at) * rows, rows), rows), :]
        cut = piece.at[(at >> 1) * rows : ((at >> 1) + 1) * rows, :]
        copies.append(pltpu.make_async_copy(cut, into, sems.at[i]))
        copies[-1].start()
    gather_lanes(blocks, m, 0, part)
    out[:, part:] = (mm_bt(pair[...], m[...]) + slab[...]).astype(LOW)
    for copy in copies:
        copy.wait()
    columns_here = pl.ds(pl.multiple_of((2 * group + ids[0]) * part, part), part)
    out[:, :part] = mm(pair[...], following[:, columns_here]).astype(LOW)


def far_kernel(ids, pair, e1, following, f_a, f_b, unused, out, far):
    size, rows = far.shape
    part = rows // 2
    far[...] = f_a[...] + f_b[...]

    @pl.when(ids[3] >= 2)
    def _():
        slab = (2 * ids[1] + ids[2]) * 2 + ids[0]
        column = lax.broadcasted_iota(jnp.int32, (size, part), 1) + slab * part
        row = lax.broadcasted_iota(jnp.int32, (size, part), 0)
        far[:, :part] = jnp.where(row == column, 1.0, 0.0).astype(LOW)

    @pl.when(ids[3] % 2 == 0)
    def _():
        far[...] = mm(following[...], far[...]).astype(LOW)

    one = mm(pair[...], far[...]).astype(LOW)
    two = mm(e1[...], far[...]).astype(LOW)
    for r in range(4):
        out[2 * r] = one[r * rows : (r + 1) * rows, :]
        out[2 * r + 1] = two[r * rows : (r + 1) * rows, :]


def end_kernel(ids, pair, e1, following, near, prod, spread, blocks, out_gain, out_spread, m, m_near):
    part = blocks.shape[2] // 2
    gather_lanes(near, m_near, 0, part)
    gather_lanes(blocks, m, part, part)
    for s in range(blocks.shape[0]):
        out_gain[:, s * part : (s + 1) * part] = blocks[s, :, :part].astype(WIDE)

    @pl.when(ids[3] % 2 == 0)
    def _():
        m[...] = mm_bt(m[...], following[...]).astype(LOW)

    @pl.when(ids[0] == 0)
    def _():
        total = mm_bt(m_near[...], pair[...]) + prod[...] + spread[0]
        out_spread[...] = mm_bt(m[...], pair[...]) + total

    @pl.when(ids[0] == 1)
    def _():
        total = mm_bt(m_near[...], e1[...]) + spread[0]
        out_spread[...] = mm_bt(m[...], e1[...]) + total


def columns(ref, side, chunk, width):
    start = side * (ref.shape[1] // 2) + chunk * width
    return ref.at[:, pl.ds(pl.multiple_of(start, width), width)]


def start_kernel(chunk, ids, e0, got, offset, p, own, keep, sem):
    copy = pltpu.make_async_copy(columns(offset, ids[0], chunk, keep.shape[1]), keep, sem)
    copy.start()

    @pl.when(ids[0] == 0)
    def _():
        p[...] = mm(e0[...], got[...])

    copy.wait()

    @pl.when(ids[0] == 0)
    def _():
        own[...] = (p[...] + keep[...]).astype(LOW)

    @pl.when(ids[0] == 1)
    def _():
        p[...] = mm(e0[...], keep[...].astype(LOW))
        own[...] = (p[...] + got[...].astype(WIDE)).astype(LOW)


def hop_kernel(ids, pair, got, own, now):
    now[...] = (mm(pair[...], got[...]) + own[...].astype(WIDE)).astype(LOW)


def hop_start_kernel(chunk, ids, pair, got_hop, own_hop, e0, got, offset, now, p, own, keep, sem):
    hop_kernel(ids, pair, got_hop, own_hop, now)
    start_kernel(chunk, ids, e0, got, offset, p, own, keep, sem)


def hops_kernel(ids, pair, got_a, own_a, got_b, own_b, now_a, now_b):
    hop_kernel(ids, pair, got_a, own_a, now_a)
    hop_kernel(ids, pair, got_b, own_b, now_b)


def last_kernel(chunk, ids, pair, later, p_far, got_a, got_b, got_c, offset, *refs):
    out, send, keep, far, e1, p, sems = refs[-7:]
    width = keep.shape[1]
    for z, got in ((2, got_a), (1, got_b), (0, got_c)):

        @pl.when(ids[3] == z)
        def _():
            pltpu.make_async_copy(got, far, sems.at[0]).start()

    load_e1 = pltpu.make_async_copy(later, e1, sems.at[1])
    load_e1.start()
    load_p = pltpu.make_async_copy(p_far, p, sems.at[2])
    load_p.start()
    load_keep = pltpu.make_async_copy(columns(offset, ids[0], chunk, width), keep, sems.at[3])
    load_keep.start()

    @pl.when(ids[3] == 3)
    def _():
        far[...] = jnp.zeros_like(far)

    @pl.when(ids[3] != 3)
    def _():
        pltpu.make_async_copy(got_a, far, sems.at[0]).wait()

    first = mm(pair[...], far[...])
    load_p.wait()
    p[...] = first + p[...]
    load_keep.wait()
    load_e1.wait()

    @pl.when(ids[0] == 0)
    def _():
        keep[...] = p[...] + keep[...]

    @pl.when(ids[0] == 1)
    def _():
        keep[...] = mm(e1[...], far[...]) + keep[...]

    store = pltpu.make_async_copy(keep, columns(out, ids[0], chunk, width), sems.at[4])
    store.start()

    @pl.when(ids[0] == 0)
    def _():
        send[...] = mm(e1[...], far[...]).astype(LOW)

    @pl.when(ids[0] == 1)
    def _():
        send[...] = p[...].astype(LOW)

    store.wait()


def add_kernel(chunk, ids, got, offset, into, out, keep, sems):
    width = keep.shape[1]
    copy = pltpu.make_async_copy(columns(offset, 1 - ids[0], chunk, width), keep, sems.at[0])
    copy.start()
    copy.wait()
    keep[...] = got[...].astype(WIDE) + keep[...]
    copy = pltpu.make_async_copy(keep, columns(out, 1 - ids[0], chunk, width), sems.at[1])
    copy.start()
    copy.wait()


def suffix(gains, spreads, offsets):
    x, y, c, z = (lax.axis_index(name) for name in ("x", "y", "c", "z"))
    gain = gains[0]
    rows, size_d = gain.shape
    part = rows // 2
    chunks = 2
    half = offsets.shape[2] // 2
    width = half // chunks
    ids = jnp.stack([x, y, c, z]).astype(jnp.int32)
    level = [(3, 2), (1, 0)]
    order = Order(ids)
    in_hbm = lambda a: pltpu.with_memory_space_constraint(a, pltpu.HBM)

    e_low = gain.astype(LOW)
    e_x, e_y = swap(e_low, "x"), swap(e_low, "y")

    l_low = spreads[0].astype(LOW)
    l_send = lax.dynamic_slice_in_dim(l_low, (1 - x) * part, part, 0)
    g_send = [
        lax.dynamic_slice_in_dim(offsets[0], (1 - x) * half + i * width, width, 1).astype(LOW) for i in range(chunks)
    ]
    tied = lax.optimization_barrier
    l_send, g_send[0], e_x = tied((l_send, g_send[0], e_x))
    e_xy = swap(e_x, "y")
    l_got = swap(l_send, "x")
    g_got = [swap(g_send[0], "x")]
    l_got, e_xy = tied((l_got, e_xy))
    g_send[1], g_got[0] = tied((g_send[1], g_got[0]))
    g_got.append(swap(g_send[1], "x"))
    three = jnp.concatenate([e_low, e_x, e_y], axis=0)
    pieces = [in_hbm(a) for a in (three, e_xy, swap(three, "c"), swap(e_xy, "c"))]
    offset, spread = in_hbm(offsets[0]), in_hbm(spreads)

    keep = pltpu.VMEM((size_d, width), WIDE)
    column = pltpu.VMEM((size_d, width), LOW)
    slab_rows = pltpu.VMEM((rows, size_d), LOW)

    def start(i):
        return order.call(
            functools.partial(start_kernel, i), [in_hbm(e0), g_got[i], offset], [hbm(size_d, width, dtype=WIDE), hbm(size_d, width)],
            12, far_in=(2,), scratch=[keep, pltpu.SemaphoreType.DMA(())],
        )

    def down(value, source):
        return lax.ppermute(value, "z", [(source, source - 1)])

    def hop(got, own):
        return order.call(hop_kernel, [pair, got, in_hbm(own)], [hbm(size_d, width)], 8)[0]

    def last(i, p, gots, into):
        extra = [] if into is None else [into]
        return order.call(
            functools.partial(last_kernel, i), [pair, in_hbm(e1), in_hbm(p), *gots, offset] + extra,
            [wide(*offset.shape), hbm(size_d, width)], 14,
            far_in=(1, 2, 3, 4, 5, 6, 7), far_out=(0,), aliases={7: 0} if extra else {},
            scratch=[keep, column, pltpu.VMEM((size_d, size_d), LOW), keep, pltpu.SemaphoreType.DMA((5,))],
        )

    def add(i, got, into):
        return order.call(
            functools.partial(add_kernel, i), [got, offset, into], [wide(*offset.shape)], 8,
            far_in=(1, 2), far_out=(0,), aliases={2: 0}, scratch=[keep, pltpu.SemaphoreType.DMA((2,))],
        )[0]

    e0, e1, pair, quarter = order.call(
        pair_kernel, pieces,
        [hbm(size_d, size_d), hbm(size_d, size_d), pltpu.VMEM((size_d, size_d), LOW), hbm(rows, size_d)], 14,
        far_in=range(4), far_out=(0, 1),
        scratch=[pltpu.VMEM((2, size_d, size_d), LOW), pltpu.SemaphoreType.DMA((8,))],
    )
    quarter = lax.ppermute(quarter, "z", level)
    (m,) = order.call(spread_kernel, [in_hbm(e0), l_low, l_got, g_got[0]], [hbm(8, rows, part)], 8, far_in=(3,))
    m = exchange(m)
    p0, own0 = start(0)
    gots0 = [down(own0, 3)]
    quarter, own0 = tied((quarter, own0))
    quarter_y = swap(quarter, "y")
    prod, slab, a_low = order.call(
        spread_start_kernel, [in_hbm(e0), m, spread, l_got, g_got[1]],
        [hbm(rows, size_d, dtype=WIDE), hbm(size_d, part, dtype=WIDE), hbm(size_d, part)], 12,
        far_in=(4,), scratch=[slab_rows],
    )
    l_next = lax.ppermute(a_low, "z", level)
    now0, p1, own1 = order.call(
        functools.partial(hop_start_kernel, 1), [pair, gots0[0], in_hbm(own0), in_hbm(e0), g_got[1], offset],
        [hbm(size_d, width), hbm(size_d, width, dtype=WIDE), hbm(size_d, width)], 16,
        far_in=(5,), scratch=[keep, pltpu.SemaphoreType.DMA(())],
    )
    gots0.append(down(now0, 2))
    gots1 = [down(own1, 3)]
    quarters = jnp.concatenate([quarter, quarter_y], axis=0)
    m, near = order.call(
        spread_hop_kernel, [pair, in_hbm(e1), l_next, quarters], [hbm(size_d, part), hbm(8, rows, part)], 10, far_in=(3,)
    )
    m = exchange(m.reshape(8, part, part))
    quarters, near = tied((quarters, near))
    quarters = [quarters, swap(quarters, "c")]
    now0, now1 = order.call(
        hops_kernel, [pair, gots0[1], in_hbm(own0), gots1[0], in_hbm(own1)], [hbm(size_d, width)] * 2, 10
    )
    gots0.append(down(now0, 1))
    gots1.append(down(now1, 2))
    following, far_slab = order.call(
        next_kernel, [pair, in_hbm(slab), m, *quarters], [hbm(size_d, size_d), hbm(size_d, rows)], 12,
        far_in=(3, 4), scratch=[pltpu.VMEM((part, size_d), LOW), pltpu.SemaphoreType.DMA((4,))],
    )
    far = lax.ppermute(far_slab, "z", [(2, 1)]), lax.ppermute(far_slab, "z", [(2, 0)])
    near, far_slab = tied((near, far_slab))
    near = exchange(near)

    out_offset, other0 = last(0, p0, gots0, None)
    other0 = swap(other0, "x")
    gots1.append(down(hop(gots1[1], own1), 1))
    (m,) = order.call(
        far_kernel, [pair, in_hbm(e1), in_hbm(following), *far, near], [hbm(8, rows, rows)], 14,
        far_in=(5,), scratch=[pltpu.VMEM((size_d, rows), LOW)],
    )
    m = exchange(m)
    out_offset = add(0, other0, out_offset)
    out_offset, other1 = last(1, p1, gots1, out_offset)
    other1 = swap(other1, "x")
    out_gain, out_spread = order.call(
        end_kernel, [pair, in_hbm(e1), in_hbm(following), near, in_hbm(prod), spread, m],
        [wide(rows, size_d), wide(rows, size_d)], 18, scratch=[slab_rows, slab_rows],
    )
    out_offset = add(1, other1, out_offset)
    return (out_gain[None], out_spread[None], out_offset[None])


def solution(mesh):
    steps, rows = mesh.shape["tm"], mesh.shape["rows"]
    if steps == 2**LEVELS and rows == 4:
        devices = mesh.devices.reshape(steps // 2, 2, 2, 2)
        mesh = Mesh(devices, ("z", "x", "y", "c"))
        by_row, by_column = P(("z", "x"), ("y", "c"), None), P(("z", "x"), None, ("y", "c"))
        body = suffix
    else:
        by_row, by_column = P("tm", "rows", None), P("tm", None, "rows")
        body = doubling
    return jax.shard_map(
        body,
        mesh=mesh,
        in_specs=(by_row, by_row, by_column),
        out_specs=(by_row, by_row, by_column),
        check_vma=False,
    )
```

```python
import functools

import jax
import jax.numpy as jnp
from jax import lax
from jax.experimental import pallas as pl
from jax.experimental.pallas import tpu as pltpu
from jax.sharding import Mesh, PartitionSpec as P

LEVELS = 3
LOW = jnp.bfloat16
WIDE = jnp.float32
MIB = 2**20


def shifted(value, axis, steps):
    count = lax.axis_size(axis)
    first, last = (max(0, -steps), min(count, count - steps))
    return lax.ppermute(value, axis, [(source, source + steps) for source in range(first, last)])


def doubling(gains, spreads, offsets):
    gain = gains[0]
    spread = spreads[0]
    offset = offsets[0]
    size_d = gain.shape[1]
    identity = jnp.eye(size_d, dtype=LOW)
    for section_number in range(LEVELS):
        distance = 2**section_number
        beyond = lax.axis_index("tm") + distance >= lax.axis_size("tm")
        own_gain = gain.astype(LOW)
        own_spread = spread.astype(LOW)
        own_offset = offset.astype(LOW)
        own_full = lax.all_gather(own_gain, "rows", axis=0, tiled=True)
        spread_full = lax.all_gather(own_spread, "rows", axis=0, tiled=True)
        far_full, far_spread_full, far_offset = shifted((own_full, spread_full, own_offset), "tm", -distance)
        far_full = jnp.where(beyond, identity, far_full)
        row_start = lax.axis_index("rows") * gain.shape[0]
        own_rows = lax.dynamic_slice_in_dim(own_full, row_start, gain.shape[0], 0)
        middle = jnp.dot(own_rows, far_spread_full, preferred_element_type=WIDE).astype(LOW)
        new_gain = jnp.dot(own_rows, far_full, preferred_element_type=WIDE)
        new_spread = (
            lax.dot_general(middle, own_full, (((1,), (1,)), ((), ())), preferred_element_type=WIDE) + spread
        )
        new_offset = jnp.dot(own_full, far_offset, preferred_element_type=WIDE) + offset
        gain, spread, offset = (new_gain, new_spread, new_offset)
    return (gain[None], spread[None], offset[None])


def swap(value, axis):
    return lax.ppermute(value, axis, [(0, 1), (1, 0)])


def mm(a, b):
    return jnp.dot(a, b, preferred_element_type=WIDE)


def mm_bt(a, b):
    return lax.dot_general(a, b, (((1,), (1,)), ((), ())), preferred_element_type=WIDE)


GROUP = ("y", "c", "x")


def exchange(blocks):
    return lax.all_to_all(blocks, GROUP, 0, 0)


def hbm(*shape, dtype=LOW):
    return pltpu.HBM(shape, dtype)


def wide(*shape):
    return jax.ShapeDtypeStruct(shape, WIDE)


ANY = pl.BlockSpec(memory_space=pl.ANY)
VMEM = pl.BlockSpec(memory_space=pltpu.VMEM)
SMEM = pl.BlockSpec(memory_space=pltpu.SMEM)


class Order:
    def __init__(self, ids):
        self.ids = ids
        self.token = jnp.zeros((8, 128), jnp.int32)

    def call(self, kernel, operands, outs, mib, scratch=(), aliases={}, far_in=(), far_out=()):
        n, m = len(operands), len(outs)

        def body(ids, token, *refs):
            kernel(ids, *refs[: n + m], *refs[n + m + 1 :])

        results = pl.pallas_call(
            body,
            in_specs=[SMEM, ANY] + [ANY if i in far_in else VMEM for i in range(n)],
            out_specs=[ANY if i in far_out else VMEM for i in range(m)] + [ANY],
            out_shape=list(outs) + [jax.ShapeDtypeStruct(self.token.shape, jnp.int32)],
            scratch_shapes=list(scratch),
            input_output_aliases={1: m} | {2 + i: o for i, o in aliases.items()},
            cost_estimate=pl.CostEstimate(flops=1, bytes_accessed=1, transcendentals=0),
            compiler_params=pltpu.CompilerParams(vmem_limit_bytes=mib * MIB),
        )(self.ids, self.token, *operands)
        self.token = results[-1]
        return results[:-1]


def gather_lanes(blocks, into, start, width):
    for s in range(blocks.shape[0]):
        into[:, s * width : (s + 1) * width] = blocks[s, :, start : start + width]


def pair_kernel(ids, three, last, three_c, last_c, e0, e1, pair, quarter, both, sems):
    group = 2 * ids[1] + ids[2]
    me = 4 * ids[0] + group
    rows = last.shape[0]
    pieces = []
    for flip, (some, other) in enumerate(((three, last), (three_c, last_c))):
        pieces += [(some.at[i * rows : (i + 1) * rows, :], at + flip) for i, at in enumerate((0, 4, 2))]
        pieces.append((other, 6 + flip))
    copies = []
    for i, (piece, at) in enumerate(pieces):
        place = me ^ at
        into = both.at[place >> 2, pl.ds(pl.multiple_of((place & 3) * rows, rows), rows), :]
        copies.append(pltpu.make_async_copy(piece, into, sems.at[i]))
        copies[-1].start()
    for copy in copies:
        copy.wait()
    copies = [pltpu.make_async_copy(both.at[i], e, sems.at[i]) for i, e in enumerate((e0, e1))]
    for copy in copies:
        copy.start()
    for r in range(4):
        cut = slice(r * rows, (r + 1) * rows)
        pair[cut, :] = mm(both[0, cut, :], both[1]).astype(LOW)
    quarter[...] = pair[pl.ds(pl.multiple_of(group * rows, rows), rows), :]
    for copy in copies:
        copy.wait()


def spread_kernel(ids, e0, l_low, l_got, m_ref):
    part, rows = l_got.shape[0], l_low.shape[0]

    def product(slab):
        for r in range(4):
            m = mm_bt(e0[r * rows : (r + 1) * rows, :], slab).astype(LOW)
            m_ref[2 * r] = m
            m_ref[2 * r + 1] = m

    @pl.when(ids[0] == 0)
    def _():
        product(l_got[...])

    @pl.when(ids[0] == 1)
    def _():
        product(l_low[part:, :])


def spread_start_kernel(ids, e0, blocks, spread, l_got, unused, prod, slab, a_low, m):
    part = l_got.shape[0]
    gather_lanes(blocks, m, 0, part)
    prod[...] = mm_bt(m[...], e0[...])

    @pl.when(ids[0] == 0)
    def _():
        slab[...] = (prod[:part, :] + spread[0, :part, :]).T

    @pl.when(ids[0] == 1)
    def _():
        slab[...] = (prod[part:, :] + l_got[...].astype(WIDE)).T

    a_low[...] = slab[...].astype(LOW)


def spread_hop_kernel(ids, pair, e1, got, unused, m_ref, near):
    part = got.shape[1]
    rows = 2 * part
    m = mm(pair[...], got[...]).astype(LOW)
    m_ref[...] = m
    other = mm(e1[...], got[...]).astype(LOW)
    for r in range(4):
        near[2 * r] = m[r * rows : (r + 1) * rows, :]
        near[2 * r + 1] = other[r * rows : (r + 1) * rows, :]


def next_kernel(ids, pair, slab, blocks, quarters, quarters_c, following, out, m, sems):
    part = m.shape[0]
    rows = 2 * part
    group = 2 * ids[1] + ids[2]
    copies = []
    for i, (piece, at) in enumerate(((quarters, 0), (quarters, 2), (quarters_c, 1), (quarters_c, 3))):
        into = following.at[pl.ds(pl.multiple_of((group ^ at) * rows, rows), rows), :]
        cut = piece.at[(at >> 1) * rows : ((at >> 1) + 1) * rows, :]
        copies.append(pltpu.make_async_copy(cut, into, sems.at[i]))
        copies[-1].start()
    gather_lanes(blocks, m, 0, part)
    out[:, part:] = (mm_bt(pair[...], m[...]) + slab[...]).astype(LOW)
    for copy in copies:
        copy.wait()
    columns_here = pl.ds(pl.multiple_of((2 * group + ids[0]) * part, part), part)
    out[:, :part] = mm(pair[...], following[:, columns_here]).astype(LOW)


def far_kernel(ids, pair, e1, following, f_a, f_b, unused, out, far):
    size, rows = far.shape
    part = rows // 2
    far[...] = f_a[...] + f_b[...]

    @pl.when(ids[3] >= 2)
    def _():
        slab = (2 * ids[1] + ids[2]) * 2 + ids[0]
        column = lax.broadcasted_iota(jnp.int32, (size, part), 1) + slab * part
        row = lax.broadcasted_iota(jnp.int32, (size, part), 0)
        far[:, :part] = jnp.where(row == column, 1.0, 0.0).astype(LOW)

    @pl.when(ids[3] % 2 == 0)
    def _():
        far[...] = mm(following[...], far[...]).astype(LOW)

    one = mm(pair[...], far[...]).astype(LOW)
    two = mm(e1[...], far[...]).astype(LOW)
    for r in range(4):
        out[2 * r] = one[r * rows : (r + 1) * rows, :]
        out[2 * r + 1] = two[r * rows : (r + 1) * rows, :]


def end_kernel(ids, pair, e1, following, near, prod, spread, blocks, out_gain, out_spread, m, m_near):
    part = blocks.shape[2] // 2
    gather_lanes(near, m_near, 0, part)
    gather_lanes(blocks, m, part, part)
    for s in range(blocks.shape[0]):
        out_gain[:, s * part : (s + 1) * part] = blocks[s, :, :part].astype(WIDE)

    @pl.when(ids[3] % 2 == 0)
    def _():
        m[...] = mm_bt(m[...], following[...]).astype(LOW)

    @pl.when(ids[0] == 0)
    def _():
        total = mm_bt(m_near[...], pair[...]) + prod[...] + spread[0]
        out_spread[...] = mm_bt(m[...], pair[...]) + total

    @pl.when(ids[0] == 1)
    def _():
        total = mm_bt(m_near[...], e1[...]) + spread[0]
        out_spread[...] = mm_bt(m[...], e1[...]) + total


def columns(ref, side, chunk, width):
    start = side * (ref.shape[1] // 2) + chunk * width
    return ref.at[:, pl.ds(pl.multiple_of(start, width), width)]


def start_kernel(chunk, ids, e0, got, offset, p, own, keep, sem):
    copy = pltpu.make_async_copy(columns(offset, ids[0], chunk, keep.shape[1]), keep, sem)
    copy.start()

    @pl.when(ids[0] == 0)
    def _():
        p[...] = mm(e0[...], got[...])

    copy.wait()

    @pl.when(ids[0] == 0)
    def _():
        own[...] = (p[...] + keep[...]).astype(LOW)

    @pl.when(ids[0] == 1)
    def _():
        p[...] = mm(e0[...], keep[...].astype(LOW))
        own[...] = (p[...] + got[...].astype(WIDE)).astype(LOW)


def hop_kernel(ids, pair, got, own0, own1, now):
    product = mm(pair[...], got[...])

    @pl.when(ids[3] == 1)
    def _():
        now[...] = (product + own0[...].astype(WIDE)).astype(LOW)

    @pl.when(ids[3] != 1)
    def _():
        now[...] = (product + own1[...].astype(WIDE)).astype(LOW)


def end_hop_kernel(ids, pair, got, own, now):
    now[...] = (mm(pair[...], got[...]) + own[...].astype(WIDE)).astype(LOW)


def hop_start_kernel(chunk, ids, pair, got_hop, own_hop, e0, got, offset, wave, p, own, keep, sem):
    start_kernel(chunk, ids, e0, got, offset, p, own, keep, sem)

    @pl.when(ids[3] == 3)
    def _():
        wave[...] = own[...]

    @pl.when(ids[3] != 3)
    def _():
        end_hop_kernel(ids, pair, got_hop, own_hop, wave)


def last_kernel(chunk, ids, pair, later, p_far, got_a, got_b, got_c, offset, *refs):
    out, send, keep, far, e1, p, sems = refs[-7:]
    width = keep.shape[1]
    for z, got in ((2, got_a), (1, got_b), (0, got_c)):

        @pl.when(ids[3] == z)
        def _():
            pltpu.make_async_copy(got, far, sems.at[0]).start()

    load_e1 = pltpu.make_async_copy(later, e1, sems.at[1])
    load_e1.start()
    load_p = pltpu.make_async_copy(p_far, p, sems.at[2])
    load_p.start()
    load_keep = pltpu.make_async_copy(columns(offset, ids[0], chunk, width), keep, sems.at[3])
    load_keep.start()

    @pl.when(ids[3] == 3)
    def _():
        far[...] = jnp.zeros_like(far)

    @pl.when(ids[3] != 3)
    def _():
        pltpu.make_async_copy(got_a, far, sems.at[0]).wait()

    first = mm(pair[...], far[...])
    load_p.wait()
    p[...] = first + p[...]
    load_keep.wait()
    load_e1.wait()

    @pl.when(ids[0] == 0)
    def _():
        keep[...] = p[...] + keep[...]

    @pl.when(ids[0] == 1)
    def _():
        keep[...] = mm(e1[...], far[...]) + keep[...]

    store = pltpu.make_async_copy(keep, columns(out, ids[0], chunk, width), sems.at[4])
    store.start()

    @pl.when(ids[0] == 0)
    def _():
        send[...] = mm(e1[...], far[...]).astype(LOW)

    @pl.when(ids[0] == 1)
    def _():
        send[...] = p[...].astype(LOW)

    store.wait()


def add_kernel(chunk, ids, got, offset, into, out, keep, sems):
    width = keep.shape[1]
    copy = pltpu.make_async_copy(columns(offset, 1 - ids[0], chunk, width), keep, sems.at[0])
    copy.start()
    copy.wait()
    keep[...] = got[...].astype(WIDE) + keep[...]
    copy = pltpu.make_async_copy(keep, columns(out, 1 - ids[0], chunk, width), sems.at[1])
    copy.start()
    copy.wait()


def suffix(gains, spreads, offsets):
    x, y, c, z = (lax.axis_index(name) for name in ("x", "y", "c", "z"))
    gain = gains[0]
    rows, size_d = gain.shape
    part = rows // 2
    chunks = 2
    half = offsets.shape[2] // 2
    width = half // chunks
    ids = jnp.stack([x, y, c, z]).astype(jnp.int32)
    level = [(3, 2), (1, 0)]
    order = Order(ids)
    in_hbm = lambda a: pltpu.with_memory_space_constraint(a, pltpu.HBM)

    e_low = gain.astype(LOW)
    e_x, e_y = swap(e_low, "x"), swap(e_low, "y")

    l_low = spreads[0].astype(LOW)
    l_send = lax.dynamic_slice_in_dim(l_low, (1 - x) * part, part, 0)
    g_send = [
        lax.dynamic_slice_in_dim(offsets[0], (1 - x) * half + i * width, width, 1).astype(LOW) for i in range(chunks)
    ]
    tied = lax.optimization_barrier
    l_send, g_send[0], e_x = tied((l_send, g_send[0], e_x))
    e_xy = swap(e_x, "y")
    l_got = swap(l_send, "x")
    g_got = [swap(g_send[0], "x")]
    l_got, e_xy = tied((l_got, e_xy))
    g_send[1], g_got[0] = tied((g_send[1], g_got[0]))
    g_got.append(swap(g_send[1], "x"))
    three = jnp.concatenate([e_low, e_x, e_y], axis=0)
    pieces = [in_hbm(a) for a in (three, e_xy, swap(three, "c"), swap(e_xy, "c"))]
    offset, spread = in_hbm(offsets[0]), in_hbm(spreads)

    keep = pltpu.VMEM((size_d, width), WIDE)
    column = pltpu.VMEM((size_d, width), LOW)
    slab_rows = pltpu.VMEM((rows, size_d), LOW)

    def start(i):
        return order.call(
            functools.partial(start_kernel, i), [in_hbm(e0), g_got[i], offset], [hbm(size_d, width, dtype=WIDE), hbm(size_d, width)],
            12, far_in=(2,), scratch=[keep, pltpu.SemaphoreType.DMA(())],
        )

    def down(value, *sources):
        return lax.ppermute(value, "z", [(source, source - 1) for source in sources])

    def last(i, p, gots, into):
        extra = [] if into is None else [into]
        return order.call(
            functools.partial(last_kernel, i), [pair, in_hbm(e1), in_hbm(p), *gots, offset] + extra,
            [wide(*offset.shape), hbm(size_d, width)], 14,
            far_in=(1, 2, 3, 4, 5, 6, 7), far_out=(0,), aliases={7: 0} if extra else {},
            scratch=[keep, column, pltpu.VMEM((size_d, size_d), LOW), keep, pltpu.SemaphoreType.DMA((5,))],
        )

    def add(i, got, into):
        return order.call(
            functools.partial(add_kernel, i), [got, offset, into], [wide(*offset.shape)], 8,
            far_in=(1, 2), far_out=(0,), aliases={2: 0}, scratch=[keep, pltpu.SemaphoreType.DMA((2,))],
        )[0]

    e0, e1, pair, quarter = order.call(
        pair_kernel, pieces,
        [hbm(size_d, size_d), hbm(size_d, size_d), pltpu.VMEM((size_d, size_d), LOW), hbm(rows, size_d)], 14,
        far_in=range(4), far_out=(0, 1),
        scratch=[pltpu.VMEM((2, size_d, size_d), LOW), pltpu.SemaphoreType.DMA((8,))],
    )
    quarter = lax.ppermute(quarter, "z", level)
    p0, own0 = start(0)
    wave1 = down(own0, 3)
    quarter, own0 = tied((quarter, own0))
    quarter_y = swap(quarter, "y")
    (m,) = order.call(spread_kernel, [in_hbm(e0), l_low, l_got], [hbm(8, rows, part)], 8)
    m = exchange(m)
    prod, slab, a_low = order.call(
        spread_start_kernel, [in_hbm(e0), m, spread, l_got, g_got[1]],
        [hbm(rows, size_d, dtype=WIDE), hbm(size_d, part, dtype=WIDE), hbm(size_d, part)], 12,
        far_in=(4,), scratch=[slab_rows],
    )
    l_next = lax.ppermute(a_low, "z", level)
    wave2, p1, own1 = order.call(
        functools.partial(hop_start_kernel, 1), [pair, wave1, in_hbm(own0), in_hbm(e0), g_got[1], offset],
        [hbm(size_d, width), hbm(size_d, width, dtype=WIDE), hbm(size_d, width)], 16,
        far_in=(5,), scratch=[keep, pltpu.SemaphoreType.DMA(())],
    )
    wave2 = down(wave2, 3, 2)

    quarters = jnp.concatenate([quarter, quarter_y], axis=0)
    quarters = [quarters, swap(quarters, "c")]
    m, near = order.call(
        spread_hop_kernel, [pair, in_hbm(e1), l_next, quarters[1]], [hbm(size_d, part), hbm(8, rows, part)], 10, far_in=(3,)
    )
    m = exchange(m.reshape(8, part, part))
    (wave3,) = order.call(hop_kernel, [pair, wave2, in_hbm(own0), in_hbm(own1)], [hbm(size_d, width)], 10)
    wave3 = down(wave3, 2, 1)
    following, far_slab = order.call(
        next_kernel, [pair, in_hbm(slab), m, *quarters], [hbm(size_d, size_d), hbm(size_d, rows)], 12,
        far_in=(3, 4), scratch=[pltpu.VMEM((part, size_d), LOW), pltpu.SemaphoreType.DMA((4,))],
    )
    far = lax.ppermute(far_slab, "z", [(2, 1)]), lax.ppermute(far_slab, "z", [(2, 0)])
    near, far_slab = tied((near, far_slab))
    near = exchange(near)

    out_offset, other0 = last(0, p0, [wave1, wave2, wave3], None)
    other0 = swap(other0, "x")
    (wave4,) = order.call(end_hop_kernel, [pair, wave3, in_hbm(own1)], [hbm(size_d, width)], 8)
    wave4 = down(wave4, 1)
    (m,) = order.call(
        far_kernel, [pair, in_hbm(e1), in_hbm(following), *far, near], [hbm(8, rows, rows)], 14,
        far_in=(5,), scratch=[pltpu.VMEM((size_d, rows), LOW)],
    )
    m = exchange(m)
    out_offset = add(0, other0, out_offset)
    out_offset, other1 = last(1, p1, [wave2, wave3, wave4], out_offset)
    other1 = swap(other1, "x")
    out_gain, out_spread = order.call(
        end_kernel, [pair, in_hbm(e1), in_hbm(following), near, in_hbm(prod), spread, m],
        [wide(rows, size_d), wide(rows, size_d)], 18, scratch=[slab_rows, slab_rows],
    )
    out_offset = add(1, other1, out_offset)
    return (out_gain[None], out_spread[None], out_offset[None])


def solution(mesh):
    steps, rows = mesh.shape["tm"], mesh.shape["rows"]
    if steps == 2**LEVELS and rows == 4:
        devices = mesh.devices.reshape(steps // 2, 2, 2, 2)
        mesh = Mesh(devices, ("z", "x", "y", "c"))
        by_row, by_column = P(("z", "x"), ("y", "c"), None), P(("z", "x"), None, ("y", "c"))
        body = suffix
    else:
        by_row, by_column = P("tm", "rows", None), P("tm", None, "rows")
        body = doubling
    return jax.shard_map(
        body,
        mesh=mesh,
        in_specs=(by_row, by_row, by_column),
        out_specs=(by_row, by_row, by_column),
        check_vma=False,
    )
```

```python
import functools

import jax
import jax.numpy as jnp
from jax import lax
from jax.experimental import pallas as pl
from jax.experimental.pallas import tpu as pltpu
from jax.sharding import Mesh, PartitionSpec as P

LEVELS = 3
LOW = jnp.bfloat16
WIDE = jnp.float32
MIB = 2**20


def shifted(value, axis, steps):
    count = lax.axis_size(axis)
    first, last = (max(0, -steps), min(count, count - steps))
    return lax.ppermute(value, axis, [(source, source + steps) for source in range(first, last)])


def doubling(gains, spreads, offsets):
    gain = gains[0]
    spread = spreads[0]
    offset = offsets[0]
    size_d = gain.shape[1]
    identity = jnp.eye(size_d, dtype=LOW)
    for section_number in range(LEVELS):
        distance = 2**section_number
        beyond = lax.axis_index("tm") + distance >= lax.axis_size("tm")
        own_gain = gain.astype(LOW)
        own_spread = spread.astype(LOW)
        own_offset = offset.astype(LOW)
        own_full = lax.all_gather(own_gain, "rows", axis=0, tiled=True)
        spread_full = lax.all_gather(own_spread, "rows", axis=0, tiled=True)
        far_full, far_spread_full, far_offset = shifted((own_full, spread_full, own_offset), "tm", -distance)
        far_full = jnp.where(beyond, identity, far_full)
        row_start = lax.axis_index("rows") * gain.shape[0]
        own_rows = lax.dynamic_slice_in_dim(own_full, row_start, gain.shape[0], 0)
        middle = jnp.dot(own_rows, far_spread_full, preferred_element_type=WIDE).astype(LOW)
        new_gain = jnp.dot(own_rows, far_full, preferred_element_type=WIDE)
        new_spread = (
            lax.dot_general(middle, own_full, (((1,), (1,)), ((), ())), preferred_element_type=WIDE) + spread
        )
        new_offset = jnp.dot(own_full, far_offset, preferred_element_type=WIDE) + offset
        gain, spread, offset = (new_gain, new_spread, new_offset)
    return (gain[None], spread[None], offset[None])


def swap(value, axis):
    return lax.ppermute(value, axis, [(0, 1), (1, 0)])


def mm(a, b):
    return jnp.dot(a, b, preferred_element_type=WIDE)


def mm_bt(a, b):
    return lax.dot_general(a, b, (((1,), (1,)), ((), ())), preferred_element_type=WIDE)


GROUP = ("y", "c", "x")


def exchange(blocks):
    return lax.all_to_all(blocks, GROUP, 0, 0)


def hbm(*shape, dtype=LOW):
    return pltpu.HBM(shape, dtype)


def wide(*shape):
    return jax.ShapeDtypeStruct(shape, WIDE)


ANY = pl.BlockSpec(memory_space=pl.ANY)
VMEM = pl.BlockSpec(memory_space=pltpu.VMEM)
SMEM = pl.BlockSpec(memory_space=pltpu.SMEM)


class Order:
    def __init__(self, ids):
        self.ids = ids
        self.token = jnp.zeros((8, 128), jnp.int32)

    def call(self, kernel, operands, outs, mib, scratch=(), aliases={}, far_in=(), far_out=()):
        n, m = len(operands), len(outs)

        def body(ids, token, *refs):
            kernel(ids, *refs[: n + m], *refs[n + m + 1 :])

        results = pl.pallas_call(
            body,
            in_specs=[SMEM, ANY] + [ANY if i in far_in else VMEM for i in range(n)],
            out_specs=[ANY if i in far_out else VMEM for i in range(m)] + [ANY],
            out_shape=list(outs) + [jax.ShapeDtypeStruct(self.token.shape, jnp.int32)],
            scratch_shapes=list(scratch),
            input_output_aliases={1: m} | {2 + i: o for i, o in aliases.items()},
            cost_estimate=pl.CostEstimate(flops=1, bytes_accessed=1, transcendentals=0),
            compiler_params=pltpu.CompilerParams(vmem_limit_bytes=mib * MIB),
        )(self.ids, self.token, *operands)
        self.token = results[-1]
        return results[:-1]


def gather_lanes(blocks, into, start, width):
    for s in range(blocks.shape[0]):
        into[:, s * width : (s + 1) * width] = blocks[s, :, start : start + width]


def pair_kernel(ids, three, last, three_c, last_c, e0, e1, pair, part_rows, both, sems):
    group = 2 * ids[1] + ids[2]
    me = 4 * ids[0] + group
    rows = last.shape[0]
    pieces = []
    for flip, (some, other) in enumerate(((three, last), (three_c, last_c))):
        pieces += [(some.at[i * rows : (i + 1) * rows, :], at + flip) for i, at in enumerate((0, 4, 2))]
        pieces.append((other, 6 + flip))
    copies = []
    for i, (piece, at) in enumerate(pieces):
        place = me ^ at
        into = both.at[place >> 2, pl.ds(pl.multiple_of((place & 3) * rows, rows), rows), :]
        copies.append(pltpu.make_async_copy(piece, into, sems.at[i]))
        copies[-1].start()
    for copy in copies:
        copy.wait()
    copies = [pltpu.make_async_copy(both.at[i], e, sems.at[i]) for i, e in enumerate((e0, e1))]
    for copy in copies:
        copy.start()
    for r in range(4):
        cut = slice(r * rows, (r + 1) * rows)
        pair[cut, :] = mm(both[0, cut, :], both[1]).astype(LOW)
    for i in range(2):
        here = pl.ds(pl.multiple_of((2 * i + ids[2]) * rows, rows), rows)
        part_rows[i * rows : (i + 1) * rows, :] = pair[here, :]
    for copy in copies:
        copy.wait()


def spread_kernel(ids, e0, l_low, l_got, m_ref):
    part, rows = l_got.shape[0], l_low.shape[0]

    def product(slab):
        for r in range(4):
            m = mm_bt(e0[r * rows : (r + 1) * rows, :], slab).astype(LOW)
            m_ref[2 * r] = m
            m_ref[2 * r + 1] = m

    @pl.when(ids[0] == 0)
    def _():
        product(l_got[...])

    @pl.when(ids[0] == 1)
    def _():
        product(l_low[part:, :])


def spread_start_kernel(ids, e0, blocks, spread, l_got, unused, prod, slab, a_low, m):
    part = l_got.shape[0]
    gather_lanes(blocks, m, 0, part)
    prod[...] = mm_bt(m[...], e0[...])

    @pl.when(ids[0] == 0)
    def _():
        slab[...] = (prod[:part, :] + spread[0, :part, :]).T

    @pl.when(ids[0] == 1)
    def _():
        slab[...] = (prod[part:, :] + l_got[...].astype(WIDE)).T

    a_low[...] = slab[...].astype(LOW)


def spread_hop_kernel(ids, pair, e1, got, m_ref, near):
    part = got.shape[1]
    rows = 2 * part
    m = mm(pair[...], got[...]).astype(LOW)
    m_ref[...] = m
    other = mm(e1[...], got[...]).astype(LOW)
    for r in range(4):
        near[2 * r] = m[r * rows : (r + 1) * rows, :]
        near[2 * r + 1] = other[r * rows : (r + 1) * rows, :]


def next_kernel(ids, pair, slab, blocks, quarters, quarters_c, following, out, m, sems):
    part = m.shape[0]
    rows = 2 * part
    c = ids[2]
    group = 2 * ids[1] + c
    copies = []
    for i in range(4):
        piece, at = ((quarters, c), (quarters_c, 1 - c))[i % 2]
        into = following.at[pl.ds(pl.multiple_of((2 * (i // 2) + at) * rows, rows), rows), :]
        cut = piece.at[(i // 2) * rows : (i // 2 + 1) * rows, :]
        copies.append(pltpu.make_async_copy(cut, into, sems.at[i]))
        copies[-1].start()
    gather_lanes(blocks, m, 0, part)
    out[:, part:] = (mm_bt(pair[...], m[...]) + slab[...]).astype(LOW)
    for copy in copies:
        copy.wait()
    columns_here = pl.ds(pl.multiple_of((2 * group + ids[0]) * part, part), part)
    out[:, :part] = mm(pair[...], following[:, columns_here]).astype(LOW)


def far_kernel(ids, pair, e1, following, f_a, f_b, unused, out, far):
    size, rows = far.shape
    part = rows // 2
    far[...] = f_a[...] + f_b[...]

    @pl.when(ids[3] >= 2)
    def _():
        slab = (2 * ids[1] + ids[2]) * 2 + ids[0]
        column = lax.broadcasted_iota(jnp.int32, (size, part), 1) + slab * part
        row = lax.broadcasted_iota(jnp.int32, (size, part), 0)
        far[:, :part] = jnp.where(row == column, 1.0, 0.0).astype(LOW)

    @pl.when(ids[3] % 2 == 0)
    def _():
        far[...] = mm(following[...], far[...]).astype(LOW)

    one = mm(pair[...], far[...]).astype(LOW)
    two = mm(e1[...], far[...]).astype(LOW)
    for r in range(4):
        out[2 * r] = one[r * rows : (r + 1) * rows, :]
        out[2 * r + 1] = two[r * rows : (r + 1) * rows, :]


def end_kernel(ids, pair, e1, following, near, prod, spread, blocks, out_gain, out_spread, m, m_near):
    part = blocks.shape[2] // 2
    gather_lanes(near, m_near, 0, part)
    gather_lanes(blocks, m, part, part)
    for s in range(blocks.shape[0]):
        out_gain[:, s * part : (s + 1) * part] = blocks[s, :, :part].astype(WIDE)

    @pl.when(ids[3] % 2 == 0)
    def _():
        m[...] = mm_bt(m[...], following[...]).astype(LOW)

    @pl.when(ids[0] == 0)
    def _():
        total = mm_bt(m_near[...], pair[...]) + prod[...] + spread[0]
        out_spread[...] = mm_bt(m[...], pair[...]) + total

    @pl.when(ids[0] == 1)
    def _():
        total = mm_bt(m_near[...], e1[...]) + spread[0]
        out_spread[...] = mm_bt(m[...], e1[...]) + total


def columns(ref, side, chunk, width):
    start = side * (ref.shape[1] // 2) + chunk * width
    return ref.at[:, pl.ds(pl.multiple_of(start, width), width)]


def start_kernel(chunk, ids, e0, got, offset, p, own, keep, sem):
    copy = pltpu.make_async_copy(columns(offset, ids[0], chunk, keep.shape[1]), keep, sem)
    copy.start()

    @pl.when(ids[0] == 0)
    def _():
        p[...] = mm(e0[...], got[...])

    copy.wait()

    @pl.when(ids[0] == 0)
    def _():
        own[...] = (p[...] + keep[...]).astype(LOW)

    @pl.when(ids[0] == 1)
    def _():
        p[...] = mm(e0[...], keep[...].astype(LOW))
        own[...] = (p[...] + got[...].astype(WIDE)).astype(LOW)


def hop_kernel(ids, pair, got, own0, own1, now):
    product = mm(pair[...], got[...])

    @pl.when(ids[3] == 1)
    def _():
        now[...] = (product + own0[...].astype(WIDE)).astype(LOW)

    @pl.when(ids[3] != 1)
    def _():
        now[...] = (product + own1[...].astype(WIDE)).astype(LOW)


def end_hop_kernel(ids, pair, got, own, now):
    now[...] = (mm(pair[...], got[...]) + own[...].astype(WIDE)).astype(LOW)


def hop_start_kernel(chunk, ids, pair, got_hop, own_hop, e0, got, offset, unused, wave, p, own, keep, sem):
    start_kernel(chunk, ids, e0, got, offset, p, own, keep, sem)

    @pl.when(ids[3] == 3)
    def _():
        wave[...] = own[...]

    @pl.when(ids[3] != 3)
    def _():
        end_hop_kernel(ids, pair, got_hop, own_hop, wave)


def last_kernel(chunk, ids, pair, later, p_far, got_a, got_b, got_c, offset, *refs):
    out, send, keep, far, e1, p, sems = refs[-7:]
    width = keep.shape[1]
    for z, got in ((2, got_a), (1, got_b), (0, got_c)):

        @pl.when(ids[3] == z)
        def _():
            pltpu.make_async_copy(got, far, sems.at[0]).start()

    load_e1 = pltpu.make_async_copy(later, e1, sems.at[1])
    load_e1.start()
    load_p = pltpu.make_async_copy(p_far, p, sems.at[2])
    load_p.start()
    load_keep = pltpu.make_async_copy(columns(offset, ids[0], chunk, width), keep, sems.at[3])
    load_keep.start()

    @pl.when(ids[3] == 3)
    def _():
        far[...] = jnp.zeros_like(far)

    @pl.when(ids[3] != 3)
    def _():
        pltpu.make_async_copy(got_a, far, sems.at[0]).wait()

    first = mm(pair[...], far[...])
    load_p.wait()
    p[...] = first + p[...]
    load_keep.wait()
    load_e1.wait()

    @pl.when(ids[0] == 0)
    def _():
        keep[...] = p[...] + keep[...]

    @pl.when(ids[0] == 1)
    def _():
        keep[...] = mm(e1[...], far[...]) + keep[...]

    store = pltpu.make_async_copy(keep, columns(out, ids[0], chunk, width), sems.at[4])
    store.start()

    @pl.when(ids[0] == 0)
    def _():
        send[...] = mm(e1[...], far[...]).astype(LOW)

    @pl.when(ids[0] == 1)
    def _():
        send[...] = p[...].astype(LOW)

    store.wait()


def add_kernel(chunk, ids, got, offset, into, out, keep, sems):
    width = keep.shape[1]
    copy = pltpu.make_async_copy(columns(offset, 1 - ids[0], chunk, width), keep, sems.at[0])
    copy.start()
    copy.wait()
    keep[...] = got[...].astype(WIDE) + keep[...]
    copy = pltpu.make_async_copy(keep, columns(out, 1 - ids[0], chunk, width), sems.at[1])
    copy.start()
    copy.wait()


def suffix(gains, spreads, offsets):
    x, y, c, z = (lax.axis_index(name) for name in ("x", "y", "c", "z"))
    gain = gains[0]
    rows, size_d = gain.shape
    part = rows // 2
    chunks = 2
    half = offsets.shape[2] // 2
    width = half // chunks
    ids = jnp.stack([x, y, c, z]).astype(jnp.int32)
    level = [(3, 2), (1, 0)]
    order = Order(ids)
    in_hbm = lambda a: pltpu.with_memory_space_constraint(a, pltpu.HBM)

    e_low = gain.astype(LOW)
    e_x, e_y = swap(e_low, "x"), swap(e_low, "y")

    l_low = spreads[0].astype(LOW)
    l_send = lax.dynamic_slice_in_dim(l_low, (1 - x) * part, part, 0)
    g_send = [
        lax.dynamic_slice_in_dim(offsets[0], (1 - x) * half + i * width, width, 1).astype(LOW) for i in range(chunks)
    ]
    tied = lax.optimization_barrier
    l_send, g_send[0], e_x = tied((l_send, g_send[0], e_x))
    e_xy = swap(e_x, "y")
    l_got = swap(l_send, "x")
    g_got = [swap(g_send[0], "x")]
    l_got, e_xy = tied((l_got, e_xy))
    g_send[1], g_got[0] = tied((g_send[1], g_got[0]))
    g_got.append(swap(g_send[1], "x"))
    three = jnp.concatenate([e_low, e_x, e_y], axis=0)
    pieces = [in_hbm(a) for a in (three, e_xy, swap(three, "c"), swap(e_xy, "c"))]
    offset, spread = in_hbm(offsets[0]), in_hbm(spreads)

    keep = pltpu.VMEM((size_d, width), WIDE)
    column = pltpu.VMEM((size_d, width), LOW)
    slab_rows = pltpu.VMEM((rows, size_d), LOW)

    def start(i):
        return order.call(
            functools.partial(start_kernel, i), [in_hbm(e0), g_got[i], offset], [hbm(size_d, width, dtype=WIDE), hbm(size_d, width)],
            12, far_in=(2,), scratch=[keep, pltpu.SemaphoreType.DMA(())],
        )

    def down(value, *sources):
        return lax.ppermute(value, "z", [(source, source - 1) for source in sources])

    def last(i, p, gots, into):
        extra = [] if into is None else [into]
        return order.call(
            functools.partial(last_kernel, i), [pair, in_hbm(e1), in_hbm(p), *gots, offset] + extra,
            [wide(*offset.shape), hbm(size_d, width)], 14,
            far_in=(1, 2, 3, 4, 5, 6, 7), far_out=(0,), aliases={7: 0} if extra else {},
            scratch=[keep, column, pltpu.VMEM((size_d, size_d), LOW), keep, pltpu.SemaphoreType.DMA((5,))],
        )

    def add(i, got, into):
        return order.call(
            functools.partial(add_kernel, i), [got, offset, into], [wide(*offset.shape)], 8,
            far_in=(1, 2), far_out=(0,), aliases={2: 0}, scratch=[keep, pltpu.SemaphoreType.DMA((2,))],
        )[0]

    e0, e1, pair, quarters = order.call(
        pair_kernel, pieces,
        [hbm(size_d, size_d), hbm(size_d, size_d), pltpu.VMEM((size_d, size_d), LOW), hbm(2 * rows, size_d)], 14,
        far_in=range(4), far_out=(0, 1),
        scratch=[pltpu.VMEM((2, size_d, size_d), LOW), pltpu.SemaphoreType.DMA((8,))],
    )
    quarters = lax.ppermute(quarters, "z", level)
    p0, own0 = start(0)
    wave1 = down(own0, 3)
    (m,) = order.call(spread_kernel, [in_hbm(e0), l_low, l_got], [hbm(8, rows, part)], 8)
    m = exchange(m)
    prod, slab, a_low = order.call(
        spread_start_kernel, [in_hbm(e0), m, spread, l_got, g_got[1]],
        [hbm(rows, size_d, dtype=WIDE), hbm(size_d, part, dtype=WIDE), hbm(size_d, part)], 12,
        far_in=(4,), scratch=[slab_rows],
    )
    l_next = lax.ppermute(a_low, "z", level)
    wave2, p1, own1 = order.call(
        functools.partial(hop_start_kernel, 1), [pair, wave1, in_hbm(own0), in_hbm(e0), g_got[1], offset, quarters],
        [hbm(size_d, width), hbm(size_d, width, dtype=WIDE), hbm(size_d, width)], 16,
        far_in=(5, 6), scratch=[keep, pltpu.SemaphoreType.DMA(())],
    )
    wave2 = down(wave2, 3, 2)

    m, near = order.call(
        spread_hop_kernel, [pair, in_hbm(e1), l_next], [hbm(size_d, part), hbm(8, rows, part)], 10
    )
    m = exchange(m.reshape(8, part, part))
    quarters, near = tied((quarters, near))
    quarters = [quarters, swap(quarters, "c")]
    (wave3,) = order.call(hop_kernel, [pair, wave2, in_hbm(own0), in_hbm(own1)], [hbm(size_d, width)], 10)
    wave3 = down(wave3, 2, 1)
    following, far_slab = order.call(
        next_kernel, [pair, in_hbm(slab), m, *quarters], [hbm(size_d, size_d), hbm(size_d, rows)], 12,
        far_in=(3, 4), scratch=[pltpu.VMEM((part, size_d), LOW), pltpu.SemaphoreType.DMA((4,))],
    )
    far = lax.ppermute(far_slab, "z", [(2, 1)]), lax.ppermute(far_slab, "z", [(2, 0)])
    near, far_slab = tied((near, far_slab))
    near = exchange(near)

    out_offset, other0 = last(0, p0, [wave1, wave2, wave3], None)
    other0 = swap(other0, "x")
    (wave4,) = order.call(end_hop_kernel, [pair, wave3, in_hbm(own1)], [hbm(size_d, width)], 8)
    wave4 = down(wave4, 1)
    (m,) = order.call(
        far_kernel, [pair, in_hbm(e1), in_hbm(following), *far, near], [hbm(8, rows, rows)], 14,
        far_in=(5,), scratch=[pltpu.VMEM((size_d, rows), LOW)],
    )
    m = exchange(m)
    out_offset = add(0, other0, out_offset)
    out_offset, other1 = last(1, p1, [wave2, wave3, wave4], out_offset)
    other1 = swap(other1, "x")
    out_gain, out_spread = order.call(
        end_kernel, [pair, in_hbm(e1), in_hbm(following), near, in_hbm(prod), spread, m],
        [wide(rows, size_d), wide(rows, size_d)], 18, scratch=[slab_rows, slab_rows],
    )
    out_offset = add(1, other1, out_offset)
    return (out_gain[None], out_spread[None], out_offset[None])


def solution(mesh):
    steps, rows = mesh.shape["tm"], mesh.shape["rows"]
    if steps == 2**LEVELS and rows == 4:
        devices = mesh.devices.reshape(steps // 2, 2, 2, 2)
        mesh = Mesh(devices, ("z", "x", "y", "c"))
        by_row, by_column = P(("z", "x"), ("y", "c"), None), P(("z", "x"), None, ("y", "c"))
        body = suffix
    else:
        by_row, by_column = P("tm", "rows", None), P("tm", None, "rows")
        body = doubling
    return jax.shard_map(
        body,
        mesh=mesh,
        in_specs=(by_row, by_row, by_column),
        out_specs=(by_row, by_row, by_column),
        check_vma=False,
    )
```

```python
import functools

import jax
import jax.numpy as jnp
from jax import lax
from jax.experimental import pallas as pl
from jax.experimental.pallas import tpu as pltpu
from jax.sharding import Mesh, PartitionSpec as P

LEVELS = 3
LOW = jnp.bfloat16
WIDE = jnp.float32
MIB = 2**20


def shifted(value, axis, steps):
    count = lax.axis_size(axis)
    first, last = (max(0, -steps), min(count, count - steps))
    return lax.ppermute(value, axis, [(source, source + steps) for source in range(first, last)])


def doubling(gains, spreads, offsets):
    gain = gains[0]
    spread = spreads[0]
    offset = offsets[0]
    size_d = gain.shape[1]
    identity = jnp.eye(size_d, dtype=LOW)
    for section_number in range(LEVELS):
        distance = 2**section_number
        beyond = lax.axis_index("tm") + distance >= lax.axis_size("tm")
        own_gain = gain.astype(LOW)
        own_spread = spread.astype(LOW)
        own_offset = offset.astype(LOW)
        own_full = lax.all_gather(own_gain, "rows", axis=0, tiled=True)
        spread_full = lax.all_gather(own_spread, "rows", axis=0, tiled=True)
        far_full, far_spread_full, far_offset = shifted((own_full, spread_full, own_offset), "tm", -distance)
        far_full = jnp.where(beyond, identity, far_full)
        row_start = lax.axis_index("rows") * gain.shape[0]
        own_rows = lax.dynamic_slice_in_dim(own_full, row_start, gain.shape[0], 0)
        middle = jnp.dot(own_rows, far_spread_full, preferred_element_type=WIDE).astype(LOW)
        new_gain = jnp.dot(own_rows, far_full, preferred_element_type=WIDE)
        new_spread = (
            lax.dot_general(middle, own_full, (((1,), (1,)), ((), ())), preferred_element_type=WIDE) + spread
        )
        new_offset = jnp.dot(own_full, far_offset, preferred_element_type=WIDE) + offset
        gain, spread, offset = (new_gain, new_spread, new_offset)
    return (gain[None], spread[None], offset[None])


def swap(value, axis):
    return lax.ppermute(value, axis, [(0, 1), (1, 0)])


def mm(a, b):
    return jnp.dot(a, b, preferred_element_type=WIDE)


def mm_bt(a, b):
    return lax.dot_general(a, b, (((1,), (1,)), ((), ())), preferred_element_type=WIDE)


GROUP = ("y", "c", "x")


def exchange(blocks):
    return lax.all_to_all(blocks, GROUP, 0, 0)


def hbm(*shape, dtype=LOW):
    return pltpu.HBM(shape, dtype)


def wide(*shape):
    return jax.ShapeDtypeStruct(shape, WIDE)


ANY = pl.BlockSpec(memory_space=pl.ANY)
VMEM = pl.BlockSpec(memory_space=pltpu.VMEM)
SMEM = pl.BlockSpec(memory_space=pltpu.SMEM)


class Order:
    def __init__(self, ids):
        self.ids = ids
        self.token = jnp.zeros((8, 128), jnp.int32)

    def call(self, kernel, operands, outs, mib, scratch=(), aliases={}, far_in=(), far_out=()):
        n, m = len(operands), len(outs)

        def body(ids, token, *refs):
            kernel(ids, *refs[: n + m], *refs[n + m + 1 :])

        results = pl.pallas_call(
            body,
            in_specs=[SMEM, ANY] + [ANY if i in far_in else VMEM for i in range(n)],
            out_specs=[ANY if i in far_out else VMEM for i in range(m)] + [ANY],
            out_shape=list(outs) + [jax.ShapeDtypeStruct(self.token.shape, jnp.int32)],
            scratch_shapes=list(scratch),
            input_output_aliases={1: m} | {2 + i: o for i, o in aliases.items()},
            cost_estimate=pl.CostEstimate(flops=1, bytes_accessed=1, transcendentals=0),
            compiler_params=pltpu.CompilerParams(vmem_limit_bytes=mib * MIB),
        )(self.ids, self.token, *operands)
        self.token = results[-1]
        return results[:-1]


def gather_lanes(blocks, into, start, width):
    for s in range(blocks.shape[0]):
        into[:, s * width : (s + 1) * width] = blocks[s, :, start : start + width]


def pair_kernel(ids, three, last, three_c, last_c, e0, e1, pair, part_rows, both, sems):
    group = 2 * ids[1] + ids[2]
    me = 4 * ids[0] + group
    rows = last.shape[0]
    pieces = []
    for flip, (some, other) in enumerate(((three, last), (three_c, last_c))):
        pieces += [(some.at[i * rows : (i + 1) * rows, :], at + flip) for i, at in enumerate((0, 4, 2))]
        pieces.append((other, 6 + flip))
    copies = []
    for i, (piece, at) in enumerate(pieces):
        place = me ^ at
        into = both.at[place >> 2, pl.ds(pl.multiple_of((place & 3) * rows, rows), rows), :]
        copies.append(pltpu.make_async_copy(piece, into, sems.at[i]))
        copies[-1].start()
    for copy in copies:
        copy.wait()
    copies = [pltpu.make_async_copy(both.at[i], e, sems.at[i]) for i, e in enumerate((e0, e1))]
    for copy in copies:
        copy.start()
    for r in range(4):
        cut = slice(r * rows, (r + 1) * rows)
        pair[cut, :] = mm(both[0, cut, :], both[1]).astype(LOW)
    for i in range(2):
        here = pl.ds(pl.multiple_of((2 * i + ids[2]) * rows, rows), rows)
        part_rows[i * rows : (i + 1) * rows, :] = pair[here, :]
    for copy in copies:
        copy.wait()


def spread_kernel(ids, e0, l_low, l_got, m_ref):
    part, rows = l_got.shape[0], l_low.shape[0]

    def product(slab):
        for r in range(4):
            m = mm_bt(e0[r * rows : (r + 1) * rows, :], slab).astype(LOW)
            m_ref[2 * r] = m
            m_ref[2 * r + 1] = m

    @pl.when(ids[0] == 0)
    def _():
        product(l_got[...])

    @pl.when(ids[0] == 1)
    def _():
        product(l_low[part:, :])


def spread_start_kernel(ids, e0, blocks, spread, l_got, unused, prod, slab, a_low, m):
    part = l_got.shape[0]
    gather_lanes(blocks, m, 0, part)
    prod[...] = mm_bt(m[...], e0[...])

    @pl.when(ids[0] == 0)
    def _():
        slab[...] = (prod[:part, :] + spread[0, :part, :]).T

    @pl.when(ids[0] == 1)
    def _():
        slab[...] = (prod[part:, :] + l_got[...].astype(WIDE)).T

    a_low[...] = slab[...].astype(LOW)


def spread_hop_kernel(ids, pair, e1, got, m_ref, near):
    part = got.shape[1]
    rows = 2 * part
    m = mm(pair[...], got[...]).astype(LOW)
    m_ref[...] = m
    other = mm(e1[...], got[...]).astype(LOW)
    for r in range(4):
        near[2 * r] = m[r * rows : (r + 1) * rows, :]
        near[2 * r + 1] = other[r * rows : (r + 1) * rows, :]


def next_kernel(ids, pair, slab, blocks, quarters, quarters_c, following, out, m, sems):
    part = m.shape[0]
    rows = 2 * part
    c = ids[2]
    group = 2 * ids[1] + c
    copies = []
    for i in range(4):
        piece, at = ((quarters, c), (quarters_c, 1 - c))[i % 2]
        into = following.at[pl.ds(pl.multiple_of((2 * (i // 2) + at) * rows, rows), rows), :]
        cut = piece.at[(i // 2) * rows : (i // 2 + 1) * rows, :]
        copies.append(pltpu.make_async_copy(cut, into, sems.at[i]))
        copies[-1].start()
    gather_lanes(blocks, m, 0, part)
    out[:, part:] = (mm_bt(pair[...], m[...]) + slab[...]).astype(LOW)
    for copy in copies:
        copy.wait()
    columns_here = pl.ds(pl.multiple_of((2 * group + ids[0]) * part, part), part)
    out[:, :part] = mm(pair[...], following[:, columns_here]).astype(LOW)


def far_kernel(ids, pair, e1, following, f_a, f_b, unused, out, far):
    size, rows = far.shape
    part = rows // 2
    far[...] = f_a[...] + f_b[...]

    @pl.when(ids[3] >= 2)
    def _():
        slab = (2 * ids[1] + ids[2]) * 2 + ids[0]
        column = lax.broadcasted_iota(jnp.int32, (size, part), 1) + slab * part
        row = lax.broadcasted_iota(jnp.int32, (size, part), 0)
        far[:, :part] = jnp.where(row == column, 1.0, 0.0).astype(LOW)

    @pl.when(ids[3] % 2 == 0)
    def _():
        far[...] = mm(following[...], far[...]).astype(LOW)

    one = mm(pair[...], far[...]).astype(LOW)
    two = mm(e1[...], far[...]).astype(LOW)
    for r in range(4):
        out[2 * r] = one[r * rows : (r + 1) * rows, :]
        out[2 * r + 1] = two[r * rows : (r + 1) * rows, :]


def end_kernel(ids, pair, e1, following, near, prod, spread, blocks, out_gain, out_spread, m, m_near):
    part = blocks.shape[2] // 2
    gather_lanes(near, m_near, 0, part)
    gather_lanes(blocks, m, part, part)
    for s in range(blocks.shape[0]):
        out_gain[:, s * part : (s + 1) * part] = blocks[s, :, :part].astype(WIDE)

    @pl.when(ids[3] % 2 == 0)
    def _():
        m[...] = mm_bt(m[...], following[...]).astype(LOW)

    @pl.when(ids[0] == 0)
    def _():
        total = mm_bt(m_near[...], pair[...]) + prod[...] + spread[0]
        out_spread[...] = mm_bt(m[...], pair[...]) + total

    @pl.when(ids[0] == 1)
    def _():
        total = mm_bt(m_near[...], e1[...]) + spread[0]
        out_spread[...] = mm_bt(m[...], e1[...]) + total


def columns(ref, side, chunk, width):
    start = side * (ref.shape[1] // 2) + chunk * width
    return ref.at[:, pl.ds(pl.multiple_of(start, width), width)]


def start_kernel(chunk, ids, e0, got, offset, p, own, keep, sem):
    copy = pltpu.make_async_copy(columns(offset, ids[0], chunk, keep.shape[1]), keep, sem)
    copy.start()

    @pl.when(ids[0] == 0)
    def _():
        p[...] = mm(e0[...], got[...])

    copy.wait()

    @pl.when(ids[0] == 0)
    def _():
        own[...] = (p[...] + keep[...]).astype(LOW)

    @pl.when(ids[0] == 1)
    def _():
        p[...] = mm(e0[...], keep[...].astype(LOW))
        own[...] = (p[...] + got[...].astype(WIDE)).astype(LOW)


def hop_kernel(ids, pair, got, own0, own1, unused, now):
    product = mm(pair[...], got[...])

    @pl.when(ids[3] == 1)
    def _():
        now[...] = (product + own0[...].astype(WIDE)).astype(LOW)

    @pl.when(ids[3] != 1)
    def _():
        now[...] = (product + own1[...].astype(WIDE)).astype(LOW)


def end_hop_kernel(ids, pair, got, own, now):
    now[...] = (mm(pair[...], got[...]) + own[...].astype(WIDE)).astype(LOW)


def hop_start_kernel(chunk, ids, pair, got_hop, own_hop, e0, got, offset, wave, p, own, keep, sem):
    start_kernel(chunk, ids, e0, got, offset, p, own, keep, sem)

    @pl.when(ids[3] == 3)
    def _():
        wave[...] = own[...]

    @pl.when(ids[3] != 3)
    def _():
        end_hop_kernel(ids, pair, got_hop, own_hop, wave)


def last_kernel(chunk, ids, pair, later, p_far, got_a, got_b, got_c, offset, *refs):
    out, send, keep, far, e1, p, sems = refs[-7:]
    width = keep.shape[1]
    for z, got in ((2, got_a), (1, got_b), (0, got_c)):

        @pl.when(ids[3] == z)
        def _():
            pltpu.make_async_copy(got, far, sems.at[0]).start()

    load_e1 = pltpu.make_async_copy(later, e1, sems.at[1])
    load_e1.start()
    load_p = pltpu.make_async_copy(p_far, p, sems.at[2])
    load_p.start()
    load_keep = pltpu.make_async_copy(columns(offset, ids[0], chunk, width), keep, sems.at[3])
    load_keep.start()

    @pl.when(ids[3] == 3)
    def _():
        far[...] = jnp.zeros_like(far)

    @pl.when(ids[3] != 3)
    def _():
        pltpu.make_async_copy(got_a, far, sems.at[0]).wait()

    first = mm(pair[...], far[...])
    load_p.wait()
    p[...] = first + p[...]
    load_keep.wait()
    load_e1.wait()

    @pl.when(ids[0] == 0)
    def _():
        keep[...] = p[...] + keep[...]

    @pl.when(ids[0] == 1)
    def _():
        keep[...] = mm(e1[...], far[...]) + keep[...]

    store = pltpu.make_async_copy(keep, columns(out, ids[0], chunk, width), sems.at[4])
    store.start()

    @pl.when(ids[0] == 0)
    def _():
        send[...] = mm(e1[...], far[...]).astype(LOW)

    @pl.when(ids[0] == 1)
    def _():
        send[...] = p[...].astype(LOW)

    store.wait()


def add_kernel(chunk, ids, got, offset, into, out, keep, sems):
    width = keep.shape[1]
    copy = pltpu.make_async_copy(columns(offset, 1 - ids[0], chunk, width), keep, sems.at[0])
    copy.start()
    copy.wait()
    keep[...] = got[...].astype(WIDE) + keep[...]
    copy = pltpu.make_async_copy(keep, columns(out, 1 - ids[0], chunk, width), sems.at[1])
    copy.start()
    copy.wait()


def suffix(gains, spreads, offsets):
    x, y, c, z = (lax.axis_index(name) for name in ("x", "y", "c", "z"))
    gain = gains[0]
    rows, size_d = gain.shape
    part = rows // 2
    chunks = 2
    half = offsets.shape[2] // 2
    width = half // chunks
    ids = jnp.stack([x, y, c, z]).astype(jnp.int32)
    level = [(3, 2), (1, 0)]
    order = Order(ids)
    in_hbm = lambda a: pltpu.with_memory_space_constraint(a, pltpu.HBM)

    e_low = gain.astype(LOW)
    e_x, e_y = swap(e_low, "x"), swap(e_low, "y")

    l_low = spreads[0].astype(LOW)
    l_send = lax.dynamic_slice_in_dim(l_low, (1 - x) * part, part, 0)
    g_send = [
        lax.dynamic_slice_in_dim(offsets[0], (1 - x) * half + i * width, width, 1).astype(LOW) for i in range(chunks)
    ]
    tied = lax.optimization_barrier
    l_send, g_send[0], e_x = tied((l_send, g_send[0], e_x))
    e_xy = swap(e_x, "y")
    l_got = swap(l_send, "x")
    g_got = [swap(g_send[0], "x")]
    l_got, e_xy = tied((l_got, e_xy))
    g_send[1], g_got[0] = tied((g_send[1], g_got[0]))
    g_got.append(swap(g_send[1], "x"))
    three = jnp.concatenate([e_low, e_x, e_y], axis=0)
    three, e_xy = tied((three, e_xy))
    pieces = [in_hbm(a) for a in (three, e_xy, swap(three, "c"), swap(e_xy, "c"))]
    offset, spread = in_hbm(offsets[0]), in_hbm(spreads)

    keep = pltpu.VMEM((size_d, width), WIDE)
    column = pltpu.VMEM((size_d, width), LOW)
    slab_rows = pltpu.VMEM((rows, size_d), LOW)

    def start(i):
        return order.call(
            functools.partial(start_kernel, i), [in_hbm(e0), g_got[i], offset], [hbm(size_d, width, dtype=WIDE), hbm(size_d, width)],
            12, far_in=(2,), scratch=[keep, pltpu.SemaphoreType.DMA(())],
        )

    def down(value, *sources):
        return lax.ppermute(value, "z", [(source, source - 1) for source in sources])

    def last(i, p, gots, into):
        extra = [] if into is None else [into]
        return order.call(
            functools.partial(last_kernel, i), [pair, in_hbm(e1), in_hbm(p), *gots, offset] + extra,
            [wide(*offset.shape), hbm(size_d, width)], 14,
            far_in=(1, 2, 3, 4, 5, 6, 7), far_out=(0,), aliases={7: 0} if extra else {},
            scratch=[keep, column, pltpu.VMEM((size_d, size_d), LOW), keep, pltpu.SemaphoreType.DMA((5,))],
        )

    def add(i, got, into):
        return order.call(
            functools.partial(add_kernel, i), [got, offset, into], [wide(*offset.shape)], 8,
            far_in=(1, 2), far_out=(0,), aliases={2: 0}, scratch=[keep, pltpu.SemaphoreType.DMA((2,))],
        )[0]

    e0, e1, pair, quarters = order.call(
        pair_kernel, pieces,
        [hbm(size_d, size_d), hbm(size_d, size_d), pltpu.VMEM((size_d, size_d), LOW), hbm(2 * rows, size_d)], 14,
        far_in=range(4), far_out=(0, 1),
        scratch=[pltpu.VMEM((2, size_d, size_d), LOW), pltpu.SemaphoreType.DMA((8,))],
    )
    quarters = lax.ppermute(quarters, "z", level)
    p0, own0 = start(0)
    wave1 = down(own0, 3)
    (m,) = order.call(spread_kernel, [in_hbm(e0), l_low, l_got], [hbm(8, rows, part)], 8)
    m = exchange(m)
    wave2, p1, own1 = order.call(
        functools.partial(hop_start_kernel, 1), [pair, wave1, in_hbm(own0), in_hbm(e0), g_got[1], offset],
        [hbm(size_d, width), hbm(size_d, width, dtype=WIDE), hbm(size_d, width)], 16,
        far_in=(5,), scratch=[keep, pltpu.SemaphoreType.DMA(())],
    )
    wave2 = down(wave2, 3, 2)
    prod, slab, a_low = order.call(
        spread_start_kernel, [in_hbm(e0), m, spread, l_got, g_got[1]],
        [hbm(rows, size_d, dtype=WIDE), hbm(size_d, part, dtype=WIDE), hbm(size_d, part)], 12,
        far_in=(4,), scratch=[slab_rows],
    )
    l_next = lax.ppermute(a_low, "z", level)
    (wave3,) = order.call(
        hop_kernel, [pair, wave2, in_hbm(own0), in_hbm(own1), quarters], [hbm(size_d, width)], 10, far_in=(4,)
    )
    wave3 = down(wave3, 2, 1)
    m, near = order.call(
        spread_hop_kernel, [pair, in_hbm(e1), l_next], [hbm(size_d, part), hbm(8, rows, part)], 10
    )
    m = exchange(m.reshape(8, part, part))
    quarters, near = tied((quarters, near))
    quarters = [quarters, swap(quarters, "c")]
    following, far_slab = order.call(
        next_kernel, [pair, in_hbm(slab), m, *quarters], [hbm(size_d, size_d), hbm(size_d, rows)], 12,
        far_in=(3, 4), scratch=[pltpu.VMEM((part, size_d), LOW), pltpu.SemaphoreType.DMA((4,))],
    )
    far = lax.ppermute(far_slab, "z", [(2, 1)]), lax.ppermute(far_slab, "z", [(2, 0)])
    near, far_slab = tied((near, far_slab))
    near = exchange(near)

    (wave4,) = order.call(end_hop_kernel, [pair, wave3, in_hbm(own1)], [hbm(size_d, width)], 8)
    wave4 = down(wave4, 1)
    out_offset, other0 = last(0, p0, [wave1, wave2, wave3], None)
    other0 = swap(other0, "x")
    out_offset, other1 = last(1, p1, [wave2, wave3, wave4], out_offset)
    other1 = swap(other1, "x")
    (m,) = order.call(
        far_kernel, [pair, in_hbm(e1), in_hbm(following), *far, near], [hbm(8, rows, rows)], 14,
        far_in=(5,), scratch=[pltpu.VMEM((size_d, rows), LOW)],
    )
    m = exchange(m)
    out_offset = add(0, other0, out_offset)
    out_offset = add(1, other1, out_offset)
    out_gain, out_spread = order.call(
        end_kernel, [pair, in_hbm(e1), in_hbm(following), near, in_hbm(prod), spread, m],
        [wide(rows, size_d), wide(rows, size_d)], 18, scratch=[slab_rows, slab_rows],
    )
    return (out_gain[None], out_spread[None], out_offset[None])


def solution(mesh):
    steps, rows = mesh.shape["tm"], mesh.shape["rows"]
    if steps == 2**LEVELS and rows == 4:
        devices = mesh.devices.reshape(steps // 2, 2, 2, 2)
        mesh = Mesh(devices, ("z", "x", "y", "c"))
        by_row, by_column = P(("z", "x"), ("y", "c"), None), P(("z", "x"), None, ("y", "c"))
        body = suffix
    else:
        by_row, by_column = P("tm", "rows", None), P("tm", None, "rows")
        body = doubling
    return jax.shard_map(
        body,
        mesh=mesh,
        in_specs=(by_row, by_row, by_column),
        out_specs=(by_row, by_row, by_column),
        check_vma=False,
    )
```

```python
import functools

import jax
import jax.numpy as jnp
from jax import lax
from jax.experimental import pallas as pl
from jax.experimental.pallas import tpu as pltpu
from jax.sharding import Mesh, PartitionSpec as P

LEVELS = 3
LOW = jnp.bfloat16
WIDE = jnp.float32
MIB = 2**20


def shifted(value, axis, steps):
    count = lax.axis_size(axis)
    first, last = (max(0, -steps), min(count, count - steps))
    return lax.ppermute(value, axis, [(source, source + steps) for source in range(first, last)])


def doubling(gains, spreads, offsets):
    gain = gains[0]
    spread = spreads[0]
    offset = offsets[0]
    size_d = gain.shape[1]
    identity = jnp.eye(size_d, dtype=LOW)
    for section_number in range(LEVELS):
        distance = 2**section_number
        beyond = lax.axis_index("tm") + distance >= lax.axis_size("tm")
        own_gain = gain.astype(LOW)
        own_spread = spread.astype(LOW)
        own_offset = offset.astype(LOW)
        own_full = lax.all_gather(own_gain, "rows", axis=0, tiled=True)
        spread_full = lax.all_gather(own_spread, "rows", axis=0, tiled=True)
        far_full, far_spread_full, far_offset = shifted((own_full, spread_full, own_offset), "tm", -distance)
        far_full = jnp.where(beyond, identity, far_full)
        row_start = lax.axis_index("rows") * gain.shape[0]
        own_rows = lax.dynamic_slice_in_dim(own_full, row_start, gain.shape[0], 0)
        middle = jnp.dot(own_rows, far_spread_full, preferred_element_type=WIDE).astype(LOW)
        new_gain = jnp.dot(own_rows, far_full, preferred_element_type=WIDE)
        new_spread = (
            lax.dot_general(middle, own_full, (((1,), (1,)), ((), ())), preferred_element_type=WIDE) + spread
        )
        new_offset = jnp.dot(own_full, far_offset, preferred_element_type=WIDE) + offset
        gain, spread, offset = (new_gain, new_spread, new_offset)
    return (gain[None], spread[None], offset[None])


def swap(value, axis):
    return lax.ppermute(value, axis, [(0, 1), (1, 0)])


def mm(a, b):
    return jnp.dot(a, b, preferred_element_type=WIDE)


def mm_bt(a, b):
    return lax.dot_general(a, b, (((1,), (1,)), ((), ())), preferred_element_type=WIDE)


GROUP = ("y", "c", "x")


def exchange(blocks):
    return lax.all_to_all(blocks, GROUP, 0, 0)


def hbm(*shape, dtype=LOW):
    return pltpu.HBM(shape, dtype)


def wide(*shape):
    return jax.ShapeDtypeStruct(shape, WIDE)


ANY = pl.BlockSpec(memory_space=pl.ANY)
VMEM = pl.BlockSpec(memory_space=pltpu.VMEM)
SMEM = pl.BlockSpec(memory_space=pltpu.SMEM)


class Order:
    def __init__(self, ids):
        self.ids = ids
        self.token = jnp.zeros((8, 128), jnp.int32)

    def call(self, kernel, operands, outs, mib, scratch=(), aliases={}, far_in=(), far_out=()):
        n, m = len(operands), len(outs)

        def body(ids, token, *refs):
            kernel(ids, *refs[: n + m], *refs[n + m + 1 :])

        results = pl.pallas_call(
            body,
            in_specs=[SMEM, ANY] + [ANY if i in far_in else VMEM for i in range(n)],
            out_specs=[ANY if i in far_out else VMEM for i in range(m)] + [ANY],
            out_shape=list(outs) + [jax.ShapeDtypeStruct(self.token.shape, jnp.int32)],
            scratch_shapes=list(scratch),
            input_output_aliases={1: m} | {2 + i: o for i, o in aliases.items()},
            cost_estimate=pl.CostEstimate(flops=1, bytes_accessed=1, transcendentals=0),
            compiler_params=pltpu.CompilerParams(vmem_limit_bytes=mib * MIB),
        )(self.ids, self.token, *operands)
        self.token = results[-1]
        return results[:-1]


def gather_lanes(blocks, into, start, width):
    for s in range(blocks.shape[0]):
        into[:, s * width : (s + 1) * width] = blocks[s, :, start : start + width]


def pair_kernel(ids, three, last, three_c, last_c, e0, e1, pair, part_rows, both, sems):
    group = 2 * ids[1] + ids[2]
    me = 4 * ids[0] + group
    rows = last.shape[0]
    pieces = []
    for flip, (some, other) in enumerate(((three, last), (three_c, last_c))):
        pieces += [(some.at[i * rows : (i + 1) * rows, :], at + flip) for i, at in enumerate((0, 4, 2))]
        pieces.append((other, 6 + flip))
    copies = []
    for i, (piece, at) in enumerate(pieces):
        place = me ^ at
        into = both.at[place >> 2, pl.ds(pl.multiple_of((place & 3) * rows, rows), rows), :]
        copies.append(pltpu.make_async_copy(piece, into, sems.at[i]))
        copies[-1].start()
    for copy in copies:
        copy.wait()
    copies = [pltpu.make_async_copy(both.at[i], e, sems.at[i]) for i, e in enumerate((e0, e1))]
    for copy in copies:
        copy.start()
    for r in range(4):
        cut = slice(r * rows, (r + 1) * rows)
        pair[cut, :] = mm(both[0, cut, :], both[1]).astype(LOW)
    for i in range(2):
        here = pl.ds(pl.multiple_of((2 * i + ids[2]) * rows, rows), rows)
        part_rows[i * rows : (i + 1) * rows, :] = pair[here, :]
    for copy in copies:
        copy.wait()


def spread_kernel(ids, e0, l_low, l_got, m_ref):
    part, rows = l_got.shape[0], l_low.shape[0]

    def product(slab):
        for r in range(4):
            m = mm_bt(e0[r * rows : (r + 1) * rows, :], slab).astype(LOW)
            m_ref[2 * r] = m
            m_ref[2 * r + 1] = m

    @pl.when(ids[0] == 0)
    def _():
        product(l_got[...])

    @pl.when(ids[0] == 1)
    def _():
        product(l_low[part:, :])


def spread_start_kernel(ids, e0, blocks, spread, l_got, unused, prod, slab, a_low, m):
    part = l_got.shape[0]
    gather_lanes(blocks, m, 0, part)
    prod[...] = mm_bt(m[...], e0[...])

    @pl.when(ids[0] == 0)
    def _():
        slab[...] = (prod[:part, :] + spread[0, :part, :]).T

    @pl.when(ids[0] == 1)
    def _():
        slab[...] = (prod[part:, :] + l_got[...].astype(WIDE)).T

    a_low[...] = slab[...].astype(LOW)


def spread_hop_kernel(ids, pair, e1, got, unused, m_ref, near):
    part = got.shape[1]
    rows = 2 * part
    m = mm(pair[...], got[...]).astype(LOW)
    m_ref[...] = m
    other = mm(e1[...], got[...]).astype(LOW)
    for r in range(4):
        near[2 * r] = m[r * rows : (r + 1) * rows, :]
        near[2 * r + 1] = other[r * rows : (r + 1) * rows, :]


def next_kernel(ids, pair, slab, blocks, quarters, quarters_c, following, out, m, sems):
    part = m.shape[0]
    rows = 2 * part
    c = ids[2]
    group = 2 * ids[1] + c
    copies = []
    for i in range(4):
        piece, at = ((quarters, c), (quarters_c, 1 - c))[i % 2]
        into = following.at[pl.ds(pl.multiple_of((2 * (i // 2) + at) * rows, rows), rows), :]
        cut = piece.at[(i // 2) * rows : (i // 2 + 1) * rows, :]
        copies.append(pltpu.make_async_copy(cut, into, sems.at[i]))
        copies[-1].start()
    gather_lanes(blocks, m, 0, part)
    out[:, part:] = (mm_bt(pair[...], m[...]) + slab[...]).astype(LOW)
    for copy in copies:
        copy.wait()
    columns_here = pl.ds(pl.multiple_of((2 * group + ids[0]) * part, part), part)
    out[:, :part] = mm(pair[...], following[:, columns_here]).astype(LOW)


def far_kernel(ids, pair, e1, following, f_a, f_b, unused, out, far):
    size, rows = far.shape
    part = rows // 2
    far[...] = f_a[...] + f_b[...]

    @pl.when(ids[3] >= 2)
    def _():
        slab = (2 * ids[1] + ids[2]) * 2 + ids[0]
        column = lax.broadcasted_iota(jnp.int32, (size, part), 1) + slab * part
        row = lax.broadcasted_iota(jnp.int32, (size, part), 0)
        far[:, :part] = jnp.where(row == column, 1.0, 0.0).astype(LOW)

    @pl.when(ids[3] % 2 == 0)
    def _():
        far[...] = mm(following[...], far[...]).astype(LOW)

    one = mm(pair[...], far[...]).astype(LOW)
    two = mm(e1[...], far[...]).astype(LOW)
    for r in range(4):
        out[2 * r] = one[r * rows : (r + 1) * rows, :]
        out[2 * r + 1] = two[r * rows : (r + 1) * rows, :]


def end_kernel(ids, pair, e1, following, near, prod, spread, blocks, out_gain, out_spread, m, m_near):
    part = blocks.shape[2] // 2
    gather_lanes(near, m_near, 0, part)
    gather_lanes(blocks, m, part, part)
    for s in range(blocks.shape[0]):
        out_gain[:, s * part : (s + 1) * part] = blocks[s, :, :part].astype(WIDE)

    @pl.when(ids[3] % 2 == 0)
    def _():
        m[...] = mm_bt(m[...], following[...]).astype(LOW)

    @pl.when(ids[0] == 0)
    def _():
        total = mm_bt(m_near[...], pair[...]) + prod[...] + spread[0]
        out_spread[...] = mm_bt(m[...], pair[...]) + total

    @pl.when(ids[0] == 1)
    def _():
        total = mm_bt(m_near[...], e1[...]) + spread[0]
        out_spread[...] = mm_bt(m[...], e1[...]) + total


def columns(ref, side, chunk, width):
    start = side * (ref.shape[1] // 2) + chunk * width
    return ref.at[:, pl.ds(pl.multiple_of(start, width), width)]


def start_kernel(chunk, ids, e0, got, offset, p, own, keep, sem):
    copy = pltpu.make_async_copy(columns(offset, ids[0], chunk, keep.shape[1]), keep, sem)
    copy.start()

    @pl.when(ids[0] == 0)
    def _():
        p[...] = mm(e0[...], got[...])

    copy.wait()

    @pl.when(ids[0] == 0)
    def _():
        own[...] = (p[...] + keep[...]).astype(LOW)

    @pl.when(ids[0] == 1)
    def _():
        p[...] = mm(e0[...], keep[...].astype(LOW))
        own[...] = (p[...] + got[...].astype(WIDE)).astype(LOW)


def hop_kernel(ids, pair, got, own0, own1, now):
    product = mm(pair[...], got[...])

    @pl.when(ids[3] == 1)
    def _():
        now[...] = (product + own0[...].astype(WIDE)).astype(LOW)

    @pl.when(ids[3] != 1)
    def _():
        now[...] = (product + own1[...].astype(WIDE)).astype(LOW)


def end_hop_kernel(ids, pair, got, own, now):
    now[...] = (mm(pair[...], got[...]) + own[...].astype(WIDE)).astype(LOW)


def hop_start_kernel(chunk, ids, pair, got_hop, own_hop, e0, got, offset, wave, p, own, keep, sem):
    start_kernel(chunk, ids, e0, got, offset, p, own, keep, sem)

    @pl.when(ids[3] == 3)
    def _():
        wave[...] = own[...]

    @pl.when(ids[3] != 3)
    def _():
        end_hop_kernel(ids, pair, got_hop, own_hop, wave)


def last_kernel(chunk, ids, pair, later, p_far, got_a, got_b, got_c, offset, *refs):
    out, send, keep, far, e1, p, sems = refs[-7:]
    width = keep.shape[1]
    for z, got in ((2, got_a), (1, got_b), (0, got_c)):

        @pl.when(ids[3] == z)
        def _():
            pltpu.make_async_copy(got, far, sems.at[0]).start()

    load_e1 = pltpu.make_async_copy(later, e1, sems.at[1])
    load_e1.start()
    load_p = pltpu.make_async_copy(p_far, p, sems.at[2])
    load_p.start()
    load_keep = pltpu.make_async_copy(columns(offset, ids[0], chunk, width), keep, sems.at[3])
    load_keep.start()

    @pl.when(ids[3] == 3)
    def _():
        far[...] = jnp.zeros_like(far)

    @pl.when(ids[3] != 3)
    def _():
        pltpu.make_async_copy(got_a, far, sems.at[0]).wait()

    first = mm(pair[...], far[...])
    load_p.wait()
    p[...] = first + p[...]
    load_keep.wait()
    load_e1.wait()

    @pl.when(ids[0] == 0)
    def _():
        keep[...] = p[...] + keep[...]

    @pl.when(ids[0] == 1)
    def _():
        keep[...] = mm(e1[...], far[...]) + keep[...]

    store = pltpu.make_async_copy(keep, columns(out, ids[0], chunk, width), sems.at[4])
    store.start()

    @pl.when(ids[0] == 0)
    def _():
        send[...] = mm(e1[...], far[...]).astype(LOW)

    @pl.when(ids[0] == 1)
    def _():
        send[...] = p[...].astype(LOW)

    store.wait()


def add_kernel(chunk, ids, got, offset, into, out, keep, sems):
    width = keep.shape[1]
    copy = pltpu.make_async_copy(columns(offset, 1 - ids[0], chunk, width), keep, sems.at[0])
    copy.start()
    copy.wait()
    keep[...] = got[...].astype(WIDE) + keep[...]
    copy = pltpu.make_async_copy(keep, columns(out, 1 - ids[0], chunk, width), sems.at[1])
    copy.start()
    copy.wait()


def suffix(gains, spreads, offsets):
    x, y, c, z = (lax.axis_index(name) for name in ("x", "y", "c", "z"))
    gain = gains[0]
    rows, size_d = gain.shape
    part = rows // 2
    chunks = 2
    half = offsets.shape[2] // 2
    width = half // chunks
    ids = jnp.stack([x, y, c, z]).astype(jnp.int32)
    level = [(3, 2), (1, 0)]
    order = Order(ids)
    in_hbm = lambda a: pltpu.with_memory_space_constraint(a, pltpu.HBM)

    e_low = gain.astype(LOW)
    e_x, e_y = swap(e_low, "x"), swap(e_low, "y")

    l_low = spreads[0].astype(LOW)
    l_send = lax.dynamic_slice_in_dim(l_low, (1 - x) * part, part, 0)
    g_send = [
        lax.dynamic_slice_in_dim(offsets[0], (1 - x) * half + i * width, width, 1).astype(LOW) for i in range(chunks)
    ]
    tied = lax.optimization_barrier
    l_send, g_send[0], e_x = tied((l_send, g_send[0], e_x))
    e_xy = swap(e_x, "y")
    l_got = swap(l_send, "x")
    g_got = [swap(g_send[0], "x")]
    l_got, e_xy = tied((l_got, e_xy))
    g_send[1], g_got[0] = tied((g_send[1], g_got[0]))
    g_got.append(swap(g_send[1], "x"))
    three = jnp.concatenate([e_low, e_x, e_y], axis=0)
    pieces = [in_hbm(a) for a in (three, e_xy, swap(three, "c"), swap(e_xy, "c"))]
    offset, spread = in_hbm(offsets[0]), in_hbm(spreads)

    keep = pltpu.VMEM((size_d, width), WIDE)
    column = pltpu.VMEM((size_d, width), LOW)
    slab_rows = pltpu.VMEM((rows, size_d), LOW)

    def start(i):
        return order.call(
            functools.partial(start_kernel, i), [in_hbm(e0), g_got[i], offset], [hbm(size_d, width, dtype=WIDE), hbm(size_d, width)],
            12, far_in=(2,), scratch=[keep, pltpu.SemaphoreType.DMA(())],
        )

    def down(value, *sources):
        return lax.ppermute(value, "z", [(source, source - 1) for source in sources])

    def last(i, p, gots, into):
        extra = [] if into is None else [into]
        return order.call(
            functools.partial(last_kernel, i), [pair, in_hbm(e1), in_hbm(p), *gots, offset] + extra,
            [wide(*offset.shape), hbm(size_d, width)], 14,
            far_in=(1, 2, 3, 4, 5, 6, 7), far_out=(0,), aliases={7: 0} if extra else {},
            scratch=[keep, column, pltpu.VMEM((size_d, size_d), LOW), keep, pltpu.SemaphoreType.DMA((5,))],
        )

    def add(i, got, into):
        return order.call(
            functools.partial(add_kernel, i), [got, offset, into], [wide(*offset.shape)], 8,
            far_in=(1, 2), far_out=(0,), aliases={2: 0}, scratch=[keep, pltpu.SemaphoreType.DMA((2,))],
        )[0]

    e0, e1, pair, quarters = order.call(
        pair_kernel, pieces,
        [hbm(size_d, size_d), hbm(size_d, size_d), pltpu.VMEM((size_d, size_d), LOW), hbm(2 * rows, size_d)], 14,
        far_in=range(4), far_out=(0, 1),
        scratch=[pltpu.VMEM((2, size_d, size_d), LOW), pltpu.SemaphoreType.DMA((8,))],
    )
    quarters = lax.ppermute(quarters, "z", level)
    p0, own0 = start(0)
    wave1 = down(own0, 3)
    (m,) = order.call(spread_kernel, [in_hbm(e0), l_low, l_got], [hbm(8, rows, part)], 8)
    m = exchange(m)
    wave2, p1, own1 = order.call(
        functools.partial(hop_start_kernel, 1), [pair, wave1, in_hbm(own0), in_hbm(e0), g_got[1], offset],
        [hbm(size_d, width), hbm(size_d, width, dtype=WIDE), hbm(size_d, width)], 16,
        far_in=(5,), scratch=[keep, pltpu.SemaphoreType.DMA(())],
    )
    wave2 = down(wave2, 3, 2)
    prod, slab, a_low = order.call(
        spread_start_kernel, [in_hbm(e0), m, spread, l_got, g_got[1]],
        [hbm(rows, size_d, dtype=WIDE), hbm(size_d, part, dtype=WIDE), hbm(size_d, part)], 12,
        far_in=(4,), scratch=[slab_rows],
    )
    l_next = lax.ppermute(a_low, "z", level)
    m, near = order.call(
        spread_hop_kernel, [pair, in_hbm(e1), l_next, quarters], [hbm(size_d, part), hbm(8, rows, part)], 10, far_in=(3,)
    )
    m = exchange(m.reshape(8, part, part))
    quarters, near = tied((quarters, near))
    quarters = [quarters, swap(quarters, "c")]
    (wave3,) = order.call(hop_kernel, [pair, wave2, in_hbm(own0), in_hbm(own1)], [hbm(size_d, width)], 10)
    wave3 = down(wave3, 2, 1)
    following, far_slab = order.call(
        next_kernel, [pair, in_hbm(slab), m, *quarters], [hbm(size_d, size_d), hbm(size_d, rows)], 12,
        far_in=(3, 4), scratch=[pltpu.VMEM((part, size_d), LOW), pltpu.SemaphoreType.DMA((4,))],
    )
    far = lax.ppermute(far_slab, "z", [(2, 1)]), lax.ppermute(far_slab, "z", [(2, 0)])
    near, far_slab = tied((near, far_slab))
    near = exchange(near)

    out_offset, other0 = last(0, p0, [wave1, wave2, wave3], None)
    other0 = swap(other0, "x")
    (wave4,) = order.call(end_hop_kernel, [pair, wave3, in_hbm(own1)], [hbm(size_d, width)], 8)
    wave4 = down(wave4, 1)
    (m,) = order.call(
        far_kernel, [pair, in_hbm(e1), in_hbm(following), *far, near], [hbm(8, rows, rows)], 14,
        far_in=(5,), scratch=[pltpu.VMEM((size_d, rows), LOW)],
    )
    m = exchange(m)
    out_offset = add(0, other0, out_offset)
    out_offset, other1 = last(1, p1, [wave2, wave3, wave4], out_offset)
    other1 = swap(other1, "x")
    out_gain, out_spread = order.call(
        end_kernel, [pair, in_hbm(e1), in_hbm(following), near, in_hbm(prod), spread, m],
        [wide(rows, size_d), wide(rows, size_d)], 18, scratch=[slab_rows, slab_rows],
    )
    out_offset = add(1, other1, out_offset)
    return (out_gain[None], out_spread[None], out_offset[None])


def solution(mesh):
    steps, rows = mesh.shape["tm"], mesh.shape["rows"]
    if steps == 2**LEVELS and rows == 4:
        devices = mesh.devices.reshape(steps // 2, 2, 2, 2)
        mesh = Mesh(devices, ("z", "x", "y", "c"))
        by_row, by_column = P(("z", "x"), ("y", "c"), None), P(("z", "x"), None, ("y", "c"))
        body = suffix
    else:
        by_row, by_column = P("tm", "rows", None), P("tm", None, "rows")
        body = doubling
    return jax.shard_map(
        body,
        mesh=mesh,
        in_specs=(by_row, by_row, by_column),
        out_specs=(by_row, by_row, by_column),
        check_vma=False,
    )
```

```python
import functools

import jax
import jax.numpy as jnp
from jax import lax
from jax.experimental import pallas as pl
from jax.experimental.pallas import tpu as pltpu
from jax.sharding import Mesh, PartitionSpec as P

LEVELS = 3
LOW = jnp.bfloat16
WIDE = jnp.float32
MIB = 2**20


def shifted(value, axis, steps):
    count = lax.axis_size(axis)
    first, last = (max(0, -steps), min(count, count - steps))
    return lax.ppermute(value, axis, [(source, source + steps) for source in range(first, last)])


def doubling(gains, spreads, offsets):
    gain = gains[0]
    spread = spreads[0]
    offset = offsets[0]
    size_d = gain.shape[1]
    identity = jnp.eye(size_d, dtype=LOW)
    for section_number in range(LEVELS):
        distance = 2**section_number
        beyond = lax.axis_index("tm") + distance >= lax.axis_size("tm")
        own_gain = gain.astype(LOW)
        own_spread = spread.astype(LOW)
        own_offset = offset.astype(LOW)
        own_full = lax.all_gather(own_gain, "rows", axis=0, tiled=True)
        spread_full = lax.all_gather(own_spread, "rows", axis=0, tiled=True)
        far_full, far_spread_full, far_offset = shifted((own_full, spread_full, own_offset), "tm", -distance)
        far_full = jnp.where(beyond, identity, far_full)
        row_start = lax.axis_index("rows") * gain.shape[0]
        own_rows = lax.dynamic_slice_in_dim(own_full, row_start, gain.shape[0], 0)
        middle = jnp.dot(own_rows, far_spread_full, preferred_element_type=WIDE).astype(LOW)
        new_gain = jnp.dot(own_rows, far_full, preferred_element_type=WIDE)
        new_spread = (
            lax.dot_general(middle, own_full, (((1,), (1,)), ((), ())), preferred_element_type=WIDE) + spread
        )
        new_offset = jnp.dot(own_full, far_offset, preferred_element_type=WIDE) + offset
        gain, spread, offset = (new_gain, new_spread, new_offset)
    return (gain[None], spread[None], offset[None])


def swap(value, axis):
    return lax.ppermute(value, axis, [(0, 1), (1, 0)])


def mm(a, b):
    return jnp.dot(a, b, preferred_element_type=WIDE)


def mm_bt(a, b):
    return lax.dot_general(a, b, (((1,), (1,)), ((), ())), preferred_element_type=WIDE)


GROUP = ("y", "c", "x")


def exchange(blocks):
    return lax.all_to_all(blocks, GROUP, 0, 0)


def hbm(*shape, dtype=LOW):
    return pltpu.HBM(shape, dtype)


def wide(*shape):
    return jax.ShapeDtypeStruct(shape, WIDE)


ANY = pl.BlockSpec(memory_space=pl.ANY)
VMEM = pl.BlockSpec(memory_space=pltpu.VMEM)
SMEM = pl.BlockSpec(memory_space=pltpu.SMEM)


class Order:
    def __init__(self, ids):
        self.ids = ids
        self.token = jnp.zeros((8, 128), jnp.int32)

    def call(self, kernel, operands, outs, mib, scratch=(), aliases={}, far_in=(), far_out=()):
        n, m = len(operands), len(outs)

        def body(ids, token, *refs):
            kernel(ids, *refs[: n + m], *refs[n + m + 1 :])

        results = pl.pallas_call(
            body,
            in_specs=[SMEM, ANY] + [ANY if i in far_in else VMEM for i in range(n)],
            out_specs=[ANY if i in far_out else VMEM for i in range(m)] + [ANY],
            out_shape=list(outs) + [jax.ShapeDtypeStruct(self.token.shape, jnp.int32)],
            scratch_shapes=list(scratch),
            input_output_aliases={1: m} | {2 + i: o for i, o in aliases.items()},
            cost_estimate=pl.CostEstimate(flops=1, bytes_accessed=1, transcendentals=0),
            compiler_params=pltpu.CompilerParams(vmem_limit_bytes=mib * MIB),
        )(self.ids, self.token, *operands)
        self.token = results[-1]
        return results[:-1]


def gather_lanes(blocks, into, start, width):
    for s in range(blocks.shape[0]):
        into[:, s * width : (s + 1) * width] = blocks[s, :, start : start + width]


def pair_kernel(ids, three, last, three_c, last_c, e0, e1, pair, part_rows, both, sems):
    group = 2 * ids[1] + ids[2]
    me = 4 * ids[0] + group
    rows = last.shape[0]
    pieces = []
    for flip, (some, other) in enumerate(((three, last), (three_c, last_c))):
        pieces += [(some.at[i * rows : (i + 1) * rows, :], at + flip) for i, at in enumerate((0, 4, 2))]
        pieces.append((other, 6 + flip))
    copies = []
    for i, (piece, at) in enumerate(pieces):
        place = me ^ at
        into = both.at[place >> 2, pl.ds(pl.multiple_of((place & 3) * rows, rows), rows), :]
        copies.append(pltpu.make_async_copy(piece, into, sems.at[i]))
        copies[-1].start()
    for copy in copies:
        copy.wait()
    copies = [pltpu.make_async_copy(both.at[i], e, sems.at[i]) for i, e in enumerate((e0, e1))]
    for copy in copies:
        copy.start()
    for r in range(4):
        cut = slice(r * rows, (r + 1) * rows)
        pair[cut, :] = mm(both[0, cut, :], both[1]).astype(LOW)
    for i in range(2):
        here = pl.ds(pl.multiple_of((2 * i + ids[2]) * rows, rows), rows)
        part_rows[i * rows : (i + 1) * rows, :] = pair[here, :]
    for copy in copies:
        copy.wait()


def spread_kernel(ids, e0, l_low, l_got, m_ref):
    part, rows = l_got.shape[0], l_low.shape[0]

    def product(slab):
        for r in range(4):
            m = mm_bt(e0[r * rows : (r + 1) * rows, :], slab).astype(LOW)
            m_ref[2 * r] = m
            m_ref[2 * r + 1] = m

    @pl.when(ids[0] == 0)
    def _():
        product(l_got[...])

    @pl.when(ids[0] == 1)
    def _():
        product(l_low[part:, :])


def spread_start_kernel(ids, e0, blocks, spread, l_got, unused, prod, slab, a_low, m):
    part = l_got.shape[0]
    gather_lanes(blocks, m, 0, part)
    prod[...] = mm_bt(m[...], e0[...])

    @pl.when(ids[0] == 0)
    def _():
        slab[...] = (prod[:part, :] + spread[0, :part, :]).T

    @pl.when(ids[0] == 1)
    def _():
        slab[...] = (prod[part:, :] + l_got[...].astype(WIDE)).T

    a_low[...] = slab[...].astype(LOW)


def spread_hop_kernel(ids, pair, e1, got, unused, unused_wave, m_ref, near):
    part = got.shape[1]
    rows = 2 * part
    m = mm(pair[...], got[...]).astype(LOW)
    m_ref[...] = m
    other = mm(e1[...], got[...]).astype(LOW)
    for r in range(4):
        near[2 * r] = m[r * rows : (r + 1) * rows, :]
        near[2 * r + 1] = other[r * rows : (r + 1) * rows, :]


def next_kernel(ids, pair, slab, blocks, quarters, quarters_c, following, out, m, sems):
    part = m.shape[0]
    rows = 2 * part
    c = ids[2]
    group = 2 * ids[1] + c
    copies = []
    for i in range(4):
        piece, at = ((quarters, c), (quarters_c, 1 - c))[i % 2]
        into = following.at[pl.ds(pl.multiple_of((2 * (i // 2) + at) * rows, rows), rows), :]
        cut = piece.at[(i // 2) * rows : (i // 2 + 1) * rows, :]
        copies.append(pltpu.make_async_copy(cut, into, sems.at[i]))
        copies[-1].start()
    gather_lanes(blocks, m, 0, part)
    out[:, part:] = (mm_bt(pair[...], m[...]) + slab[...]).astype(LOW)
    for copy in copies:
        copy.wait()
    columns_here = pl.ds(pl.multiple_of((2 * group + ids[0]) * part, part), part)
    out[:, :part] = mm(pair[...], following[:, columns_here]).astype(LOW)


def far_kernel(ids, pair, e1, following, f_a, f_b, unused, out, far):
    size, rows = far.shape
    part = rows // 2
    far[...] = f_a[...] + f_b[...]

    @pl.when(ids[3] >= 2)
    def _():
        slab = (2 * ids[1] + ids[2]) * 2 + ids[0]
        column = lax.broadcasted_iota(jnp.int32, (size, part), 1) + slab * part
        row = lax.broadcasted_iota(jnp.int32, (size, part), 0)
        far[:, :part] = jnp.where(row == column, 1.0, 0.0).astype(LOW)

    @pl.when(ids[3] % 2 == 0)
    def _():
        far[...] = mm(following[...], far[...]).astype(LOW)

    one = mm(pair[...], far[...]).astype(LOW)
    two = mm(e1[...], far[...]).astype(LOW)
    for r in range(4):
        out[2 * r] = one[r * rows : (r + 1) * rows, :]
        out[2 * r + 1] = two[r * rows : (r + 1) * rows, :]


def end_kernel(ids, pair, e1, following, near, prod, spread, blocks, out_gain, out_spread, m, m_near):
    part = blocks.shape[2] // 2
    gather_lanes(near, m_near, 0, part)
    gather_lanes(blocks, m, part, part)
    for s in range(blocks.shape[0]):
        out_gain[:, s * part : (s + 1) * part] = blocks[s, :, :part].astype(WIDE)

    @pl.when(ids[3] % 2 == 0)
    def _():
        m[...] = mm_bt(m[...], following[...]).astype(LOW)

    @pl.when(ids[0] == 0)
    def _():
        total = mm_bt(m_near[...], pair[...]) + prod[...] + spread[0]
        out_spread[...] = mm_bt(m[...], pair[...]) + total

    @pl.when(ids[0] == 1)
    def _():
        total = mm_bt(m_near[...], e1[...]) + spread[0]
        out_spread[...] = mm_bt(m[...], e1[...]) + total


def columns(ref, side, chunk, width):
    start = side * (ref.shape[1] // 2) + chunk * width
    return ref.at[:, pl.ds(pl.multiple_of(start, width), width)]


def start_kernel(chunk, ids, e0, got, offset, p, own, keep, sem):
    copy = pltpu.make_async_copy(columns(offset, ids[0], chunk, keep.shape[1]), keep, sem)
    copy.start()

    @pl.when(ids[0] == 0)
    def _():
        p[...] = mm(e0[...], got[...])

    copy.wait()

    @pl.when(ids[0] == 0)
    def _():
        own[...] = (p[...] + keep[...]).astype(LOW)

    @pl.when(ids[0] == 1)
    def _():
        p[...] = mm(e0[...], keep[...].astype(LOW))
        own[...] = (p[...] + got[...].astype(WIDE)).astype(LOW)


def hop_kernel(ids, pair, got, own0, own1, now):
    product = mm(pair[...], got[...])

    @pl.when(ids[3] == 1)
    def _():
        now[...] = (product + own0[...].astype(WIDE)).astype(LOW)

    @pl.when(ids[3] != 1)
    def _():
        now[...] = (product + own1[...].astype(WIDE)).astype(LOW)


def end_hop_kernel(ids, pair, got, own, now):
    now[...] = (mm(pair[...], got[...]) + own[...].astype(WIDE)).astype(LOW)


def hop_start_kernel(chunk, ids, pair, got_hop, own_hop, e0, got, offset, wave, p, own, keep, sem):
    start_kernel(chunk, ids, e0, got, offset, p, own, keep, sem)

    @pl.when(ids[3] == 3)
    def _():
        wave[...] = own[...]

    @pl.when(ids[3] != 3)
    def _():
        end_hop_kernel(ids, pair, got_hop, own_hop, wave)


def last_kernel(chunk, ids, pair, later, p_far, got_a, got_b, got_c, offset, *refs):
    out, send, keep, far, e1, p, sems = refs[-7:]
    width = keep.shape[1]
    for z, got in ((2, got_a), (1, got_b), (0, got_c)):

        @pl.when(ids[3] == z)
        def _():
            pltpu.make_async_copy(got, far, sems.at[0]).start()

    load_e1 = pltpu.make_async_copy(later, e1, sems.at[1])
    load_e1.start()
    load_p = pltpu.make_async_copy(p_far, p, sems.at[2])
    load_p.start()
    load_keep = pltpu.make_async_copy(columns(offset, ids[0], chunk, width), keep, sems.at[3])
    load_keep.start()

    @pl.when(ids[3] == 3)
    def _():
        far[...] = jnp.zeros_like(far)

    @pl.when(ids[3] != 3)
    def _():
        pltpu.make_async_copy(got_a, far, sems.at[0]).wait()

    first = mm(pair[...], far[...])
    load_p.wait()
    p[...] = first + p[...]
    load_keep.wait()
    load_e1.wait()

    @pl.when(ids[0] == 0)
    def _():
        keep[...] = p[...] + keep[...]

    @pl.when(ids[0] == 1)
    def _():
        keep[...] = mm(e1[...], far[...]) + keep[...]

    store = pltpu.make_async_copy(keep, columns(out, ids[0], chunk, width), sems.at[4])
    store.start()

    @pl.when(ids[0] == 0)
    def _():
        send[...] = mm(e1[...], far[...]).astype(LOW)

    @pl.when(ids[0] == 1)
    def _():
        send[...] = p[...].astype(LOW)

    store.wait()


def add_kernel(chunk, ids, got, offset, into, out, keep, sems):
    width = keep.shape[1]
    copy = pltpu.make_async_copy(columns(offset, 1 - ids[0], chunk, width), keep, sems.at[0])
    copy.start()
    copy.wait()
    keep[...] = got[...].astype(WIDE) + keep[...]
    copy = pltpu.make_async_copy(keep, columns(out, 1 - ids[0], chunk, width), sems.at[1])
    copy.start()
    copy.wait()


def suffix(gains, spreads, offsets):
    x, y, c, z = (lax.axis_index(name) for name in ("x", "y", "c", "z"))
    gain = gains[0]
    rows, size_d = gain.shape
    part = rows // 2
    chunks = 2
    half = offsets.shape[2] // 2
    width = half // chunks
    ids = jnp.stack([x, y, c, z]).astype(jnp.int32)
    level = [(3, 2), (1, 0)]
    order = Order(ids)
    in_hbm = lambda a: pltpu.with_memory_space_constraint(a, pltpu.HBM)

    e_low = gain.astype(LOW)
    e_x, e_y = swap(e_low, "x"), swap(e_low, "y")

    l_low = spreads[0].astype(LOW)
    l_send = lax.dynamic_slice_in_dim(l_low, (1 - x) * part, part, 0)
    g_send = [
        lax.dynamic_slice_in_dim(offsets[0], (1 - x) * half + i * width, width, 1).astype(LOW) for i in range(chunks)
    ]
    tied = lax.optimization_barrier
    l_send, g_send[0], e_x = tied((l_send, g_send[0], e_x))
    e_xy = swap(e_x, "y")
    l_got = swap(l_send, "x")
    g_got = [swap(g_send[0], "x")]
    l_got, e_xy = tied((l_got, e_xy))
    g_send[1], g_got[0] = tied((g_send[1], g_got[0]))
    g_got.append(swap(g_send[1], "x"))
    three = jnp.concatenate([e_low, e_x, e_y], axis=0)
    pieces = [in_hbm(a) for a in (three, e_xy, swap(three, "c"), swap(e_xy, "c"))]
    offset, spread = in_hbm(offsets[0]), in_hbm(spreads)

    keep = pltpu.VMEM((size_d, width), WIDE)
    column = pltpu.VMEM((size_d, width), LOW)
    slab_rows = pltpu.VMEM((rows, size_d), LOW)

    def start(i):
        return order.call(
            functools.partial(start_kernel, i), [in_hbm(e0), g_got[i], offset], [hbm(size_d, width, dtype=WIDE), hbm(size_d, width)],
            12, far_in=(2,), scratch=[keep, pltpu.SemaphoreType.DMA(())],
        )

    def down(value, *sources):
        return lax.ppermute(value, "z", [(source, source - 1) for source in sources])

    def last(i, p, gots, into):
        extra = [] if into is None else [into]
        return order.call(
            functools.partial(last_kernel, i), [pair, in_hbm(e1), in_hbm(p), *gots, offset] + extra,
            [wide(*offset.shape), hbm(size_d, width)], 14,
            far_in=(1, 2, 3, 4, 5, 6, 7), far_out=(0,), aliases={7: 0} if extra else {},
            scratch=[keep, column, pltpu.VMEM((size_d, size_d), LOW), keep, pltpu.SemaphoreType.DMA((5,))],
        )

    def add(i, got, into):
        return order.call(
            functools.partial(add_kernel, i), [got, offset, into], [wide(*offset.shape)], 8,
            far_in=(1, 2), far_out=(0,), aliases={2: 0}, scratch=[keep, pltpu.SemaphoreType.DMA((2,))],
        )[0]

    e0, e1, pair, quarters = order.call(
        pair_kernel, pieces,
        [hbm(size_d, size_d), hbm(size_d, size_d), pltpu.VMEM((size_d, size_d), LOW), hbm(2 * rows, size_d)], 14,
        far_in=range(4), far_out=(0, 1),
        scratch=[pltpu.VMEM((2, size_d, size_d), LOW), pltpu.SemaphoreType.DMA((8,))],
    )
    quarters = lax.ppermute(quarters, "z", level)
    p0, own0 = start(0)
    wave1 = down(own0, 3)
    (m,) = order.call(spread_kernel, [in_hbm(e0), l_low, l_got], [hbm(8, rows, part)], 8)
    m = exchange(m)
    wave2, p1, own1 = order.call(
        functools.partial(hop_start_kernel, 1), [pair, wave1, in_hbm(own0), in_hbm(e0), g_got[1], offset],
        [hbm(size_d, width), hbm(size_d, width, dtype=WIDE), hbm(size_d, width)], 16,
        far_in=(5,), scratch=[keep, pltpu.SemaphoreType.DMA(())],
    )
    wave2 = down(wave2, 3, 2)
    prod, slab, a_low = order.call(
        spread_start_kernel, [in_hbm(e0), m, spread, l_got, g_got[1]],
        [hbm(rows, size_d, dtype=WIDE), hbm(size_d, part, dtype=WIDE), hbm(size_d, part)], 12,
        far_in=(4,), scratch=[slab_rows],
    )
    l_next = lax.ppermute(a_low, "z", level)
    m, near = order.call(
        spread_hop_kernel, [pair, in_hbm(e1), l_next, quarters, wave2], [hbm(size_d, part), hbm(8, rows, part)], 10, far_in=(3, 4)
    )
    m = exchange(m.reshape(8, part, part))
    quarters, near = tied((quarters, near))
    quarters = [quarters, swap(quarters, "c")]
    (wave3,) = order.call(hop_kernel, [pair, wave2, in_hbm(own0), in_hbm(own1)], [hbm(size_d, width)], 10)
    wave3 = down(wave3, 2, 1)
    following, far_slab = order.call(
        next_kernel, [pair, in_hbm(slab), m, *quarters], [hbm(size_d, size_d), hbm(size_d, rows)], 12,
        far_in=(3, 4), scratch=[pltpu.VMEM((part, size_d), LOW), pltpu.SemaphoreType.DMA((4,))],
    )
    far = lax.ppermute(far_slab, "z", [(2, 1)]), lax.ppermute(far_slab, "z", [(2, 0)])
    near, far_slab = tied((near, far_slab))
    near = exchange(near)

    out_offset, other0 = last(0, p0, [wave1, wave2, wave3], None)
    other0 = swap(other0, "x")
    (wave4,) = order.call(end_hop_kernel, [pair, wave3, in_hbm(own1)], [hbm(size_d, width)], 8)
    wave4 = down(wave4, 1)
    (m,) = order.call(
        far_kernel, [pair, in_hbm(e1), in_hbm(following), *far, near], [hbm(8, rows, rows)], 14,
        far_in=(5,), scratch=[pltpu.VMEM((size_d, rows), LOW)],
    )
    m = exchange(m)
    out_offset = add(0, other0, out_offset)
    out_offset, other1 = last(1, p1, [wave2, wave3, wave4], out_offset)
    other1 = swap(other1, "x")
    out_gain, out_spread = order.call(
        end_kernel, [pair, in_hbm(e1), in_hbm(following), near, in_hbm(prod), spread, m],
        [wide(rows, size_d), wide(rows, size_d)], 18, scratch=[slab_rows, slab_rows],
    )
    out_offset = add(1, other1, out_offset)
    return (out_gain[None], out_spread[None], out_offset[None])


def solution(mesh):
    steps, rows = mesh.shape["tm"], mesh.shape["rows"]
    if steps == 2**LEVELS and rows == 4:
        devices = mesh.devices.reshape(steps // 2, 2, 2, 2)
        mesh = Mesh(devices, ("z", "x", "y", "c"))
        by_row, by_column = P(("z", "x"), ("y", "c"), None), P(("z", "x"), None, ("y", "c"))
        body = suffix
    else:
        by_row, by_column = P("tm", "rows", None), P("tm", None, "rows")
        body = doubling
    return jax.shard_map(
        body,
        mesh=mesh,
        in_specs=(by_row, by_row, by_column),
        out_specs=(by_row, by_row, by_column),
        check_vma=False,
    )
```

```python
import functools

import jax
import jax.numpy as jnp
from jax import lax
from jax.experimental import pallas as pl
from jax.experimental.pallas import tpu as pltpu
from jax.sharding import Mesh, PartitionSpec as P

LEVELS = 3
LOW = jnp.bfloat16
WIDE = jnp.float32
MIB = 2**20


def shifted(value, axis, steps):
    count = lax.axis_size(axis)
    first, last = (max(0, -steps), min(count, count - steps))
    return lax.ppermute(value, axis, [(source, source + steps) for source in range(first, last)])


def doubling(gains, spreads, offsets):
    gain = gains[0]
    spread = spreads[0]
    offset = offsets[0]
    size_d = gain.shape[1]
    identity = jnp.eye(size_d, dtype=LOW)
    for section_number in range(LEVELS):
        distance = 2**section_number
        beyond = lax.axis_index("tm") + distance >= lax.axis_size("tm")
        own_gain = gain.astype(LOW)
        own_spread = spread.astype(LOW)
        own_offset = offset.astype(LOW)
        own_full = lax.all_gather(own_gain, "rows", axis=0, tiled=True)
        spread_full = lax.all_gather(own_spread, "rows", axis=0, tiled=True)
        far_full, far_spread_full, far_offset = shifted((own_full, spread_full, own_offset), "tm", -distance)
        far_full = jnp.where(beyond, identity, far_full)
        row_start = lax.axis_index("rows") * gain.shape[0]
        own_rows = lax.dynamic_slice_in_dim(own_full, row_start, gain.shape[0], 0)
        middle = jnp.dot(own_rows, far_spread_full, preferred_element_type=WIDE).astype(LOW)
        new_gain = jnp.dot(own_rows, far_full, preferred_element_type=WIDE)
        new_spread = (
            lax.dot_general(middle, own_full, (((1,), (1,)), ((), ())), preferred_element_type=WIDE) + spread
        )
        new_offset = jnp.dot(own_full, far_offset, preferred_element_type=WIDE) + offset
        gain, spread, offset = (new_gain, new_spread, new_offset)
    return (gain[None], spread[None], offset[None])


def swap(value, axis):
    return lax.ppermute(value, axis, [(0, 1), (1, 0)])


def mm(a, b):
    return jnp.dot(a, b, preferred_element_type=WIDE)


def mm_bt(a, b):
    return lax.dot_general(a, b, (((1,), (1,)), ((), ())), preferred_element_type=WIDE)


GROUP = ("y", "c", "x")


def exchange(blocks):
    return lax.all_to_all(blocks, GROUP, 0, 0)


def hbm(*shape, dtype=LOW):
    return pltpu.HBM(shape, dtype)


def wide(*shape):
    return jax.ShapeDtypeStruct(shape, WIDE)


ANY = pl.BlockSpec(memory_space=pl.ANY)
VMEM = pl.BlockSpec(memory_space=pltpu.VMEM)
SMEM = pl.BlockSpec(memory_space=pltpu.SMEM)


class Order:
    def __init__(self, ids):
        self.ids = ids
        self.token = jnp.zeros((8, 128), jnp.int32)

    def call(self, kernel, operands, outs, mib, scratch=(), aliases={}, far_in=(), far_out=()):
        n, m = len(operands), len(outs)

        def body(ids, token, *refs):
            kernel(ids, *refs[: n + m], *refs[n + m + 1 :])

        results = pl.pallas_call(
            body,
            in_specs=[SMEM, ANY] + [ANY if i in far_in else VMEM for i in range(n)],
            out_specs=[ANY if i in far_out else VMEM for i in range(m)] + [ANY],
            out_shape=list(outs) + [jax.ShapeDtypeStruct(self.token.shape, jnp.int32)],
            scratch_shapes=list(scratch),
            input_output_aliases={1: m} | {2 + i: o for i, o in aliases.items()},
            cost_estimate=pl.CostEstimate(flops=1, bytes_accessed=1, transcendentals=0),
            compiler_params=pltpu.CompilerParams(vmem_limit_bytes=mib * MIB),
        )(self.ids, self.token, *operands)
        self.token = results[-1]
        return results[:-1]


def gather_lanes(blocks, into, start, width):
    for s in range(blocks.shape[0]):
        into[:, s * width : (s + 1) * width] = blocks[s, :, start : start + width]


def pair_kernel(ids, three, last, three_c, last_c, e0, e1, pair, part_rows, both, sems):
    group = 2 * ids[1] + ids[2]
    me = 4 * ids[0] + group
    rows = last.shape[0]
    pieces = []
    for flip, (some, other) in enumerate(((three, last), (three_c, last_c))):
        pieces += [(some.at[i * rows : (i + 1) * rows, :], at + flip) for i, at in enumerate((0, 4, 2))]
        pieces.append((other, 6 + flip))
    copies = []
    for i, (piece, at) in enumerate(pieces):
        place = me ^ at
        into = both.at[place >> 2, pl.ds(pl.multiple_of((place & 3) * rows, rows), rows), :]
        copies.append(pltpu.make_async_copy(piece, into, sems.at[i]))
        copies[-1].start()
    for copy in copies:
        copy.wait()
    copies = [pltpu.make_async_copy(both.at[i], e, sems.at[i]) for i, e in enumerate((e0, e1))]
    for copy in copies:
        copy.start()
    for r in range(4):
        cut = slice(r * rows, (r + 1) * rows)
        pair[cut, :] = mm(both[0, cut, :], both[1]).astype(LOW)
    for i in range(2):
        here = pl.ds(pl.multiple_of((2 * i + ids[2]) * rows, rows), rows)
        part_rows[i * rows : (i + 1) * rows, :] = pair[here, :]
    for copy in copies:
        copy.wait()


def spread_kernel(ids, e0, l_low, l_got, m_ref):
    part, rows = l_got.shape[0], l_low.shape[0]

    def product(slab):
        for r in range(4):
            m = mm_bt(e0[r * rows : (r + 1) * rows, :], slab).astype(LOW)
            m_ref[2 * r] = m
            m_ref[2 * r + 1] = m

    @pl.when(ids[0] == 0)
    def _():
        product(l_got[...])

    @pl.when(ids[0] == 1)
    def _():
        product(l_low[part:, :])


def spread_start_kernel(ids, e0, blocks, spread, l_got, unused, prod, slab, a_low, m):
    part = l_got.shape[0]
    gather_lanes(blocks, m, 0, part)
    prod[...] = mm_bt(m[...], e0[...])

    @pl.when(ids[0] == 0)
    def _():
        slab[...] = (prod[:part, :] + spread[0, :part, :]).T

    @pl.when(ids[0] == 1)
    def _():
        slab[...] = (prod[part:, :] + l_got[...].astype(WIDE)).T

    a_low[...] = slab[...].astype(LOW)


def spread_hop_kernel(ids, pair, e1, got, m_ref, near):
    part = got.shape[1]
    rows = 2 * part
    m = mm(pair[...], got[...]).astype(LOW)
    m_ref[...] = m
    other = mm(e1[...], got[...]).astype(LOW)
    for r in range(4):
        near[2 * r] = m[r * rows : (r + 1) * rows, :]
        near[2 * r + 1] = other[r * rows : (r + 1) * rows, :]


def next_kernel(ids, pair, slab, blocks, quarters, quarters_c, following, out, m, sems):
    part = m.shape[0]
    rows = 2 * part
    c = ids[2]
    group = 2 * ids[1] + c
    copies = []
    for i in range(4):
        piece, at = ((quarters, c), (quarters_c, 1 - c))[i % 2]
        into = following.at[pl.ds(pl.multiple_of((2 * (i // 2) + at) * rows, rows), rows), :]
        cut = piece.at[(i // 2) * rows : (i // 2 + 1) * rows, :]
        copies.append(pltpu.make_async_copy(cut, into, sems.at[i]))
        copies[-1].start()
    gather_lanes(blocks, m, 0, part)
    out[:, part:] = (mm_bt(pair[...], m[...]) + slab[...]).astype(LOW)
    for copy in copies:
        copy.wait()
    columns_here = pl.ds(pl.multiple_of((2 * group + ids[0]) * part, part), part)
    out[:, :part] = mm(pair[...], following[:, columns_here]).astype(LOW)


def far_kernel(ids, pair, e1, following, f_a, f_b, unused, out, far):
    size, rows = far.shape
    part = rows // 2
    far[...] = f_a[...] + f_b[...]

    @pl.when(ids[3] >= 2)
    def _():
        slab = (2 * ids[1] + ids[2]) * 2 + ids[0]
        column = lax.broadcasted_iota(jnp.int32, (size, part), 1) + slab * part
        row = lax.broadcasted_iota(jnp.int32, (size, part), 0)
        far[:, :part] = jnp.where(row == column, 1.0, 0.0).astype(LOW)

    @pl.when(ids[3] % 2 == 0)
    def _():
        far[...] = mm(following[...], far[...]).astype(LOW)

    one = mm(pair[...], far[...]).astype(LOW)
    two = mm(e1[...], far[...]).astype(LOW)
    for r in range(4):
        out[2 * r] = one[r * rows : (r + 1) * rows, :]
        out[2 * r + 1] = two[r * rows : (r + 1) * rows, :]


def end_kernel(ids, pair, e1, following, near, prod, spread, blocks, out_gain, out_spread, m, m_near):
    part = blocks.shape[2] // 2
    gather_lanes(near, m_near, 0, part)
    gather_lanes(blocks, m, part, part)
    for s in range(blocks.shape[0]):
        out_gain[:, s * part : (s + 1) * part] = blocks[s, :, :part].astype(WIDE)

    @pl.when(ids[3] % 2 == 0)
    def _():
        m[...] = mm_bt(m[...], following[...]).astype(LOW)

    @pl.when(ids[0] == 0)
    def _():
        total = mm_bt(m_near[...], pair[...]) + prod[...] + spread[0]
        out_spread[...] = mm_bt(m[...], pair[...]) + total

    @pl.when(ids[0] == 1)
    def _():
        total = mm_bt(m_near[...], e1[...]) + spread[0]
        out_spread[...] = mm_bt(m[...], e1[...]) + total


def columns(ref, side, chunk, width):
    start = side * (ref.shape[1] // 2) + chunk * width
    return ref.at[:, pl.ds(pl.multiple_of(start, width), width)]


def start_kernel(chunk, ids, e0, got, offset, p, own, keep, sem):
    copy = pltpu.make_async_copy(columns(offset, ids[0], chunk, keep.shape[1]), keep, sem)
    copy.start()

    @pl.when(ids[0] == 0)
    def _():
        p[...] = mm(e0[...], got[...])

    copy.wait()

    @pl.when(ids[0] == 0)
    def _():
        own[...] = (p[...] + keep[...]).astype(LOW)

    @pl.when(ids[0] == 1)
    def _():
        p[...] = mm(e0[...], keep[...].astype(LOW))
        own[...] = (p[...] + got[...].astype(WIDE)).astype(LOW)


def hop_kernel(ids, pair, got, own0, own1, now):
    product = mm(pair[...], got[...])

    @pl.when(ids[3] == 1)
    def _():
        now[...] = (product + own0[...].astype(WIDE)).astype(LOW)

    @pl.when(ids[3] != 1)
    def _():
        now[...] = (product + own1[...].astype(WIDE)).astype(LOW)


def end_hop_kernel(ids, pair, got, own, now):
    now[...] = (mm(pair[...], got[...]) + own[...].astype(WIDE)).astype(LOW)


def hop_start_kernel(chunk, ids, pair, got_hop, own_hop, e0, got, offset, unused, wave, p, own, keep, sem):
    start_kernel(chunk, ids, e0, got, offset, p, own, keep, sem)

    @pl.when(ids[3] == 3)
    def _():
        wave[...] = own[...]

    @pl.when(ids[3] != 3)
    def _():
        end_hop_kernel(ids, pair, got_hop, own_hop, wave)


def last_kernel(chunk, ids, pair, later, p_far, got_a, got_b, got_c, offset, *refs):
    out, send, keep, far, e1, p, sems = refs[-7:]
    width = keep.shape[1]
    for z, got in ((2, got_a), (1, got_b), (0, got_c)):

        @pl.when(ids[3] == z)
        def _():
            pltpu.make_async_copy(got, far, sems.at[0]).start()

    load_e1 = pltpu.make_async_copy(later, e1, sems.at[1])
    load_e1.start()
    load_p = pltpu.make_async_copy(p_far, p, sems.at[2])
    load_p.start()
    load_keep = pltpu.make_async_copy(columns(offset, ids[0], chunk, width), keep, sems.at[3])
    load_keep.start()

    @pl.when(ids[3] == 3)
    def _():
        far[...] = jnp.zeros_like(far)

    @pl.when(ids[3] != 3)
    def _():
        pltpu.make_async_copy(got_a, far, sems.at[0]).wait()

    first = mm(pair[...], far[...])
    load_p.wait()
    p[...] = first + p[...]
    load_keep.wait()
    load_e1.wait()

    @pl.when(ids[0] == 0)
    def _():
        keep[...] = p[...] + keep[...]

    @pl.when(ids[0] == 1)
    def _():
        keep[...] = mm(e1[...], far[...]) + keep[...]

    store = pltpu.make_async_copy(keep, columns(out, ids[0], chunk, width), sems.at[4])
    store.start()

    @pl.when(ids[0] == 0)
    def _():
        send[...] = mm(e1[...], far[...]).astype(LOW)

    @pl.when(ids[0] == 1)
    def _():
        send[...] = p[...].astype(LOW)

    store.wait()


def add_kernel(chunk, ids, got, offset, into, out, keep, sems):
    width = keep.shape[1]
    copy = pltpu.make_async_copy(columns(offset, 1 - ids[0], chunk, width), keep, sems.at[0])
    copy.start()
    copy.wait()
    keep[...] = got[...].astype(WIDE) + keep[...]
    copy = pltpu.make_async_copy(keep, columns(out, 1 - ids[0], chunk, width), sems.at[1])
    copy.start()
    copy.wait()


def suffix(gains, spreads, offsets):
    x, y, c, z = (lax.axis_index(name) for name in ("x", "y", "c", "z"))
    gain = gains[0]
    rows, size_d = gain.shape
    part = rows // 2
    chunks = 2
    half = offsets.shape[2] // 2
    width = half // chunks
    ids = jnp.stack([x, y, c, z]).astype(jnp.int32)
    level = [(3, 2), (1, 0)]
    order = Order(ids)
    in_hbm = lambda a: pltpu.with_memory_space_constraint(a, pltpu.HBM)

    e_low = gain.astype(LOW)
    e_x, e_y = swap(e_low, "x"), swap(e_low, "y")

    l_low = spreads[0].astype(LOW)
    l_send = lax.dynamic_slice_in_dim(l_low, (1 - x) * part, part, 0)
    g_send = [
        lax.dynamic_slice_in_dim(offsets[0], (1 - x) * half + i * width, width, 1).astype(LOW) for i in range(chunks)
    ]
    tied = lax.optimization_barrier
    l_send, g_send[0], e_x = tied((l_send, g_send[0], e_x))
    e_xy = swap(e_x, "y")
    l_got = swap(l_send, "x")
    g_got = [swap(g_send[0], "x")]
    l_got, e_xy = tied((l_got, e_xy))
    g_send[1], g_got[0] = tied((g_send[1], g_got[0]))
    g_got.append(swap(g_send[1], "x"))
    three = jnp.concatenate([e_low, e_x, e_y], axis=0)
    pieces = [in_hbm(a) for a in (three, e_xy, swap(three, "c"), swap(e_xy, "c"))]
    offset, spread = in_hbm(offsets[0]), in_hbm(spreads)

    keep = pltpu.VMEM((size_d, width), WIDE)
    column = pltpu.VMEM((size_d, width), LOW)
    slab_rows = pltpu.VMEM((rows, size_d), LOW)

    def start(i):
        return order.call(
            functools.partial(start_kernel, i), [in_hbm(e0), g_got[i], offset], [hbm(size_d, width, dtype=WIDE), hbm(size_d, width)],
            12, far_in=(2,), scratch=[keep, pltpu.SemaphoreType.DMA(())],
        )

    def down(value, *sources):
        return lax.ppermute(value, "z", [(source, source - 1) for source in sources])

    def last(i, p, gots, into):
        extra = [] if into is None else [into]
        return order.call(
            functools.partial(last_kernel, i), [pair, in_hbm(e1), in_hbm(p), *gots, offset] + extra,
            [wide(*offset.shape), hbm(size_d, width)], 14,
            far_in=(1, 2, 3, 4, 5, 6, 7), far_out=(0,), aliases={7: 0} if extra else {},
            scratch=[keep, column, pltpu.VMEM((size_d, size_d), LOW), keep, pltpu.SemaphoreType.DMA((5,))],
        )

    def add(i, got, into):
        return order.call(
            functools.partial(add_kernel, i), [got, offset, into], [wide(*offset.shape)], 8,
            far_in=(1, 2), far_out=(0,), aliases={2: 0}, scratch=[keep, pltpu.SemaphoreType.DMA((2,))],
        )[0]

    e0, e1, pair, quarters = order.call(
        pair_kernel, pieces,
        [hbm(size_d, size_d), hbm(size_d, size_d), pltpu.VMEM((size_d, size_d), LOW), hbm(2 * rows, size_d)], 14,
        far_in=range(4), far_out=(0, 1),
        scratch=[pltpu.VMEM((2, size_d, size_d), LOW), pltpu.SemaphoreType.DMA((8,))],
    )
    quarters = lax.ppermute(quarters, "z", level)
    p0, own0 = start(0)
    wave1 = down(own0, 3)
    (m,) = order.call(spread_kernel, [in_hbm(e0), l_low, l_got], [hbm(8, rows, part)], 8)
    m = exchange(m)
    prod, slab, a_low = order.call(
        spread_start_kernel, [in_hbm(e0), m, spread, l_got, g_got[1]],
        [hbm(rows, size_d, dtype=WIDE), hbm(size_d, part, dtype=WIDE), hbm(size_d, part)], 12,
        far_in=(4,), scratch=[slab_rows],
    )
    l_next = lax.ppermute(a_low, "z", level)
    wave2, p1, own1 = order.call(
        functools.partial(hop_start_kernel, 1), [pair, wave1, in_hbm(own0), in_hbm(e0), g_got[1], offset, quarters],
        [hbm(size_d, width), hbm(size_d, width, dtype=WIDE), hbm(size_d, width)], 16,
        far_in=(5, 6), scratch=[keep, pltpu.SemaphoreType.DMA(())],
    )
    wave2 = down(wave2, 3, 2)

    m, near = order.call(
        spread_hop_kernel, [pair, in_hbm(e1), l_next], [hbm(size_d, part), hbm(8, rows, part)], 10
    )
    m = exchange(m.reshape(8, part, part))
    quarters, near = tied((quarters, near))
    quarters = [quarters, swap(quarters, "c")]
    (wave3,) = order.call(hop_kernel, [pair, wave2, in_hbm(own0), in_hbm(own1)], [hbm(size_d, width)], 10)
    wave3 = down(wave3, 2, 1)
    following, far_slab = order.call(
        next_kernel, [pair, in_hbm(slab), m, *quarters], [hbm(size_d, size_d), hbm(size_d, rows)], 12,
        far_in=(3, 4), scratch=[pltpu.VMEM((part, size_d), LOW), pltpu.SemaphoreType.DMA((4,))],
    )
    far = lax.ppermute(far_slab, "z", [(2, 1)]), lax.ppermute(far_slab, "z", [(2, 0)])
    near, far_slab = tied((near, far_slab))
    near = exchange(near)

    out_offset, other0 = last(0, p0, [wave1, wave2, wave3], None)
    other0 = swap(other0, "x")
    (wave4,) = order.call(end_hop_kernel, [pair, wave3, in_hbm(own1)], [hbm(size_d, width)], 8)
    wave4 = down(wave4, 1)
    (m,) = order.call(
        far_kernel, [pair, in_hbm(e1), in_hbm(following), *far, near], [hbm(8, rows, rows)], 14,
        far_in=(5,), scratch=[pltpu.VMEM((size_d, rows), LOW)],
    )
    m = exchange(m)
    out_offset, other1 = last(1, p1, [wave2, wave3, wave4], out_offset)
    other1 = swap(other1, "x")
    out_offset = add(0, other0, out_offset)
    out_gain, out_spread = order.call(
        end_kernel, [pair, in_hbm(e1), in_hbm(following), near, in_hbm(prod), spread, m],
        [wide(rows, size_d), wide(rows, size_d)], 18, scratch=[slab_rows, slab_rows],
    )
    out_offset = add(1, other1, out_offset)
    return (out_gain[None], out_spread[None], out_offset[None])


def solution(mesh):
    steps, rows = mesh.shape["tm"], mesh.shape["rows"]
    if steps == 2**LEVELS and rows == 4:
        devices = mesh.devices.reshape(steps // 2, 2, 2, 2)
        mesh = Mesh(devices, ("z", "x", "y", "c"))
        by_row, by_column = P(("z", "x"), ("y", "c"), None), P(("z", "x"), None, ("y", "c"))
        body = suffix
    else:
        by_row, by_column = P("tm", "rows", None), P("tm", None, "rows")
        body = doubling
    return jax.shard_map(
        body,
        mesh=mesh,
        in_specs=(by_row, by_row, by_column),
        out_specs=(by_row, by_row, by_column),
        check_vma=False,
    )
```
